32 devices in a mesh: frame: 4 (over y, core), row: 4 (over z), head: 2 (over x).
Axes of the slice: x: 2, y: 2, z: 4, core: 2. Of those that a mesh axis runs over, the one named last changes fastest.
Arguments:
- queries: bfloat16 [8, 32, 16, 12, 128], P('frame', 'row', 'head'), may hold values from -6 to 6
- keys: bfloat16 [8, 32, 16, 12, 128], P('frame', 'row', 'head'), may hold values from -6 to 6
- values: bfloat16 [8, 32, 16, 12, 128], P('frame', 'row', 'head'), may hold values from -6 to 6
- out_grad: bfloat16 [8, 32, 16, 12, 128], P('frame', 'row', 'head'), may hold values from -6 to 6
- active: int32 [8, 4, 2, 27], replicated, may hold values from 0 to 1, as said below
Outputs:
- attended: bfloat16 [8, 32, 16, 12, 128], P('frame', 'row', 'head')
- query_grad: bfloat16 [8, 32, 16, 12, 128], P('frame', 'row', 'head')
- key_grad: bfloat16 [8, 32, 16, 12, 128], P('frame', 'row', 'head')
- value_grad: bfloat16 [8, 32, 16, 12, 128], P('frame', 'row', 'head')
The draws below stay inside these ranges and needn't reach their ends.
Inputs may be any that keep to these rules, and one draw needn't show every extreme that they name: `active`: entry 13 (the tile with itself) is 1 for every tile; all other entries are 0 or 1.
All inputs are finite; a program needn't handle non-finite values.
Results may differ from the reference program's by a relative error of at most 0.011.
Values may be sent and summed in bfloat16 or wider, within the bound.
No kernel may reach another device: no remote copies, remote signals or barrier semaphores. Data moves between devices by JAX's collectives and lax.ppermute only.
A program may use at most 64 MiB of HBM per device.

```python
import jax
import jax.numpy as jnp
from jax import lax

HEADS = 12
HD = 128
TF = 1
TR = 8
TC = 8
SLOTS = 27
COLS = 16
NF = 8
NR = 32
NTF = 8
NTR = 4
NTC = 2


def draw_queries(key, part):
    shape = (NF, NR, COLS, HEADS, HD)
    base_key = jax.random.fold_in(key, 11)
    result = jnp.clip(jax.random.normal(base_key, shape, jnp.float32), -6.0, 6.0)
    return result.astype(jnp.bfloat16)


def draw_keys(key, part):
    shape = (NF, NR, COLS, HEADS, HD)
    base_key = jax.random.fold_in(key, 17)
    result = jnp.clip(jax.random.normal(base_key, shape, jnp.float32), -6.0, 6.0)
    return result.astype(jnp.bfloat16)


def draw_active(key, part):
    level = jax.random.randint(jax.random.fold_in(key, 3), (NTF, NTR, NTC, 1), 1, 5)
    rolled = jax.random.randint(jax.random.fold_in(key, 5), (NTF, NTR, NTC, SLOTS), 0, 4)
    picked = (rolled < level).astype(jnp.int32)
    center = lax.broadcasted_iota(jnp.int32, (NTF, NTR, NTC, SLOTS), 3) == 13
    return jnp.where(center, 1, picked).astype(jnp.int32)


def shard_levels(stream_key, extent, shards, smallest, high):
    gain = 1.0
    for axis_at, blocks in shards:
        steps = jax.random.uniform(jax.random.fold_in(jax.random.fold_in(stream_key, 6), axis_at), (blocks,), jnp.float32, smallest / len(shards), high / len(shards))
        gain = gain * jnp.repeat(jnp.exp(steps), extent[axis_at] // blocks).reshape((-1,) + (1,) * (len(extent) - 1 - axis_at))
    return gain


def gaussian(stream_key, extent, deviation, bound, cuts=(), held_as=jnp.bfloat16):
    loudness = shard_levels(stream_key, extent, cuts, -0.22, 0.18) if cuts else 1.0
    entries = jax.random.normal(stream_key, extent, jnp.float32) * deviation * loudness
    return jnp.minimum(jnp.maximum(entries, -bound), bound).astype(held_as)


def setup_inputs(seed: int = 0) -> dict:
    key_of = jax.random.split(jax.random.key(seed), 6)
    return {
        "queries": draw_queries(jax.random.fold_in(key_of[5], 71), 0),
        "keys": draw_keys(jax.random.fold_in(key_of[5], 71), 0),
        "values": gaussian(key_of[2], (NF, NR, COLS, HEADS, HD), 1.0, 6.0, ((0, 4), (1, 4), (2, 2))),
        "out_grad": gaussian(key_of[3], (NF, NR, COLS, HEADS, HD), 1.0, 6.0, ((0, 4), (1, 4), (2, 2))),
        "active": draw_active(jax.random.fold_in(key_of[5], 71), 0),
    }


def product(form, left, right):
    return jnp.einsum(form, left.astype(jnp.float32), right.astype(jnp.float32))


def slot_masks(act_ext, one_ext, frame_tiles, row_tiles, sign):
    col_tiles = act_ext.shape[2]
    own = jnp.arange(col_tiles, dtype=jnp.int32)[:, None]
    other = jnp.arange(col_tiles, dtype=jnp.int32)[None, :]
    offsets = jnp.arange(3, dtype=jnp.int32) - 1
    matches = (((other - own) * sign)[:, :, None] == offsets[None, None, :]).astype(jnp.float32)
    layers = []
    for offset in range(9):
        frame_step = offset // 3 - 1
        row_step = offset % 3 - 1
        if sign > 0:
            chosen = act_ext[1:1 + frame_tiles, 1:1 + row_tiles, :, 3 * offset:3 * offset + 3]
            inside = one_ext[1 + frame_step:1 + frame_step + frame_tiles, 1 + row_step:1 + row_step + row_tiles]
        else:
            chosen = act_ext[1 - frame_step:1 - frame_step + frame_tiles, 1 - row_step:1 - row_step + row_tiles, :, 3 * offset:3 * offset + 3]
            inside = jnp.ones((frame_tiles, row_tiles), jnp.float32)
        layers.append(jnp.einsum("abio,ijo->abij", chosen.astype(jnp.float32), matches) * inside[:, :, None, None])
    tiles = jnp.transpose(jnp.stack(layers, axis=2), (0, 1, 3, 2, 4))
    spread = jnp.broadcast_to(tiles[:, :, None, :, None, :, None, :, None], (frame_tiles, row_tiles, TF * TR, col_tiles, TC, 9, TF * TR, col_tiles, TC))
    slab = TF * TR * col_tiles * TC
    return spread.reshape(frame_tiles, row_tiles, slab, 9 * slab) > 0.5


def gather_bands(wide, frame_tiles, row_tiles, sign):
    parts = []
    for offset in range(9):
        frame_step = sign * (offset // 3 - 1)
        row_step = sign * (offset % 3 - 1)
        parts.append(wide[1 + frame_step:1 + frame_step + frame_tiles, 1 + row_step:1 + row_step + row_tiles])
    stacked = jnp.stack(parts, axis=2)
    return stacked.reshape((frame_tiles, row_tiles, 9 * wide.shape[2]) + wide.shape[3:])


def query_side(query_slab, key_wide, value_wide, grad_slab, allowed, scaling):
    frame_tiles, row_tiles = query_slab.shape[0], query_slab.shape[1]
    key_band = gather_bands(key_wide, frame_tiles, row_tiles, 1)
    value_band = gather_bands(value_wide, frame_tiles, row_tiles, 1)
    scores = product("abqd,abkd->abqk", query_slab, key_band) * scaling
    scores = jnp.where(allowed, scores, -jnp.inf)
    highest = jnp.max(scores, axis=-1, keepdims=True)
    log_total = highest + jnp.log(jnp.sum(jnp.exp(scores - highest), axis=-1, keepdims=True))
    weights = jnp.where(allowed, jnp.exp(scores - log_total), 0.0).astype(jnp.bfloat16)
    weights = lax.optimization_barrier(weights)
    attended = product("abqk,abkd->abqd", weights, value_band).astype(jnp.bfloat16)
    attended = lax.optimization_barrier(attended)
    grad_dot = jnp.sum(grad_slab.astype(jnp.float32) * attended.astype(jnp.float32), axis=-1)
    grad_probs = product("abqd,abkd->abqk", grad_slab, value_band)
    grad_scores = (weights.astype(jnp.float32) * (grad_probs - grad_dot[..., None]) * scaling).astype(jnp.bfloat16)
    query_grad = product("abqk,abkd->abqd", grad_scores, key_band).astype(jnp.bfloat16)
    return attended, query_grad, log_total[..., 0], grad_dot


def key_side(key_slab, value_slab, query_wide, grad_wide, total_wide, dot_wide, allowed, scaling):
    frame_tiles, row_tiles = key_slab.shape[0], key_slab.shape[1]
    query_band = gather_bands(query_wide, frame_tiles, row_tiles, -1)
    grad_band = gather_bands(grad_wide, frame_tiles, row_tiles, -1)
    total_band = gather_bands(total_wide, frame_tiles, row_tiles, -1)
    dot_band = gather_bands(dot_wide, frame_tiles, row_tiles, -1)
    scores = product("abkd,abqd->abkq", key_slab, query_band) * scaling
    weights = jnp.where(allowed, jnp.exp(scores - total_band[:, :, None, :]), 0.0).astype(jnp.bfloat16)
    weights = lax.optimization_barrier(weights)
    grad_probs = product("abkd,abqd->abkq", value_slab, grad_band)
    grad_scores = (weights.astype(jnp.float32) * (grad_probs - dot_band[:, :, None, :]) * scaling).astype(jnp.bfloat16)
    key_grad = product("abkq,abqd->abkd", grad_scores, query_band).astype(jnp.bfloat16)
    value_grad = product("abkq,abqd->abkd", weights, grad_band).astype(jnp.bfloat16)
    return key_grad, value_grad


def to_slabs(tensor):
    shaped = tensor.reshape(NTF, TF, NTR, TR, COLS, HEADS, HD)
    return jnp.transpose(shaped, (5, 0, 2, 1, 3, 4, 6)).reshape(HEADS, NTF, NTR, TF * TR * COLS, HD)


def from_slabs(result):
    shaped = result.reshape(HEADS, NTF, NTR, TF, TR, COLS, HD)
    return jnp.transpose(shaped, (1, 3, 2, 4, 5, 0, 6)).reshape(NF, NR, COLS, HEADS, HD)


def pad_tiles(tensor):
    widths = ((1, 1), (1, 1)) + ((0, 0),) * (tensor.ndim - 2)
    return jnp.pad(tensor, widths)


def reference(queries, keys, values, out_grad, active):
    scaling = HD ** -0.5
    padded_active = jnp.pad(active, ((1, 1), (1, 1), (0, 0), (0, 0)))
    padded_ones = jnp.pad(jnp.ones((NTF, NTR), jnp.float32), 1)
    frame_list = jnp.arange(NTF, dtype=jnp.int32)

    def head_pass(pieces):
        query_pad, key_pad, value_pad, grad_pad = [pad_tiles(piece) for piece in pieces]

        def front(frame_tile):
            act_ext = lax.dynamic_slice_in_dim(padded_active, frame_tile, 3, 0)
            one_ext = lax.dynamic_slice_in_dim(padded_ones, frame_tile, 3, 0)
            allowed = slot_masks(act_ext, one_ext, 1, NTR, 1)
            key_wide = lax.dynamic_slice_in_dim(key_pad, frame_tile, 3, 0)
            value_wide = lax.dynamic_slice_in_dim(value_pad, frame_tile, 3, 0)
            query_here = lax.dynamic_slice_in_dim(query_pad, frame_tile + 1, 1, 0)[:, 1:-1]
            grad_here = lax.dynamic_slice_in_dim(grad_pad, frame_tile + 1, 1, 0)[:, 1:-1]
            return query_side(query_here, key_wide, value_wide, grad_here, allowed, scaling)

        attended, query_grad, log_total, grad_dot = lax.map(front, frame_list)
        total_pad = pad_tiles(log_total[:, 0])
        dot_pad = pad_tiles(grad_dot[:, 0])

        def back(frame_tile):
            act_ext = lax.dynamic_slice_in_dim(padded_active, frame_tile, 3, 0)
            one_ext = lax.dynamic_slice_in_dim(padded_ones, frame_tile, 3, 0)
            allowed = slot_masks(act_ext, one_ext, 1, NTR, -1)
            query_wide = lax.dynamic_slice_in_dim(query_pad, frame_tile, 3, 0)
            grad_wide = lax.dynamic_slice_in_dim(grad_pad, frame_tile, 3, 0)
            total_wide = lax.dynamic_slice_in_dim(total_pad, frame_tile, 3, 0)
            dot_wide = lax.dynamic_slice_in_dim(dot_pad, frame_tile, 3, 0)
            key_here = lax.dynamic_slice_in_dim(key_pad, frame_tile + 1, 1, 0)[:, 1:-1]
            value_here = lax.dynamic_slice_in_dim(value_pad, frame_tile + 1, 1, 0)[:, 1:-1]
            return key_side(key_here, value_here, query_wide, grad_wide, total_wide, dot_wide, allowed, scaling)

        key_grad, value_grad = lax.map(back, frame_list)
        return attended[:, 0], query_grad[:, 0], key_grad[:, 0], value_grad[:, 0]

    results = lax.map(head_pass, (to_slabs(queries), to_slabs(keys), to_slabs(values), to_slabs(out_grad)))
    return (from_slabs(results[0]), from_slabs(results[1]), from_slabs(results[2]), from_slabs(results[3]))
```

```python
import functools

import jax
import jax.numpy as jnp
from jax import lax
from jax.experimental import pallas as pl
from jax.experimental.pallas import tpu as pltpu
from jax.sharding import PartitionSpec as P

TF = 1
TR = 8
TC = 8
MASKED = -1e30
NT = (((1,), (1,)), ((), ()))
NN = (((1,), (0,)), ((), ()))


def dot(left, right, dims):
    return lax.dot_general(left, right, dims, preferred_element_type=jnp.float32)


def spread(bias, tokens):
    blocks, width = bias.shape
    return jnp.broadcast_to(bias[:, None, :], (blocks, tokens // blocks, width)).reshape(tokens, width)


def fill_band(own, before, after, low, high, first, second):
    frames, tokens = own.shape[1], own.shape[3]
    for at in range(frames + 2):
        for row, beside in enumerate((before, own, after)):
            place = pl.ds((3 * at + row) * tokens, tokens)
            for which, band in enumerate((first, second)):
                if at == 0:
                    band[place, :] = low[row, which, 0]
                elif at == frames + 1:
                    band[place, :] = high[row, which, 0]
                else:
                    band[place, :] = beside[which, at - 1, 0]


def front_kernel(
    scaling, pair, own, before, after, low, high, bias, attended, query_grad, stats, key_all, value_all
):
    frames, tokens = own.shape[1], own.shape[3]
    fill_band(own, before, after, low, high, key_all, value_all)
    for at in range(frames):
        window = pl.ds(3 * at * tokens, 9 * tokens)
        key_band = key_all[window, :]
        value_band = value_all[window, :]
        scores = dot(pair[0, at, 0], key_band, NT) * scaling + spread(bias[at], tokens)
        highest = jnp.max(scores, axis=1, keepdims=True)
        raised = jnp.exp(scores - highest)
        total = jnp.sum(raised, axis=1, keepdims=True)
        weights = (raised * (1.0 / total)).astype(jnp.bfloat16)
        out = dot(weights, value_band, NN).astype(jnp.bfloat16)
        grad = pair[1, at, 0]
        grad_dot = jnp.sum(grad.astype(jnp.float32) * out.astype(jnp.float32), axis=1, keepdims=True)
        grad_probs = dot(grad, value_band, NT)
        grad_scores = (weights.astype(jnp.float32) * (grad_probs - grad_dot)).astype(jnp.bfloat16)
        attended[at, 0] = out
        query_grad[at, 0] = (dot(grad_scores, key_band, NN) * scaling).astype(jnp.bfloat16)
        lane = lax.broadcasted_iota(jnp.int32, (tokens, 128), 1)
        both = jnp.where(lane == 0, highest + jnp.log(total), grad_dot)
        stats[at, 0] = jnp.transpose(both)[:2]


def back_kernel(
    scaling, pair, own, before, after, low, high, own_st, before_st, after_st, low_st, high_st, bias,
    key_grad, value_grad, query_all, grad_all
):
    frames, tokens = own.shape[1], own.shape[3]
    fill_band(own, before, after, low, high, query_all, grad_all)

    def stat_row(at, row, which):
        if at == 0:
            return low_st[row, 0, which : which + 1]
        if at == frames + 1:
            return high_st[row, 0, which : which + 1]
        return (before_st, own_st, after_st)[row][at - 1, 0, which : which + 1]

    def stat_band(at, which):
        rows = [stat_row(at + step, row, which) for step in range(3) for row in range(3)]
        return jnp.concatenate(rows, axis=1)

    for at in range(frames):
        window = pl.ds(3 * at * tokens, 9 * tokens)
        query_band = query_all[window, :]
        grad_band = grad_all[window, :]
        shift = bias[at] - stat_band(at, 0)
        weights = jnp.exp(dot(pair[0, at, 0], query_band, NT) * scaling + spread(shift, tokens))
        weights = weights.astype(jnp.bfloat16)
        grad_probs = dot(pair[1, at, 0], grad_band, NT)
        grad_scores = weights.astype(jnp.float32) * (grad_probs - stat_band(at, 1))
        key_grad[at, 0] = (dot(grad_scores.astype(jnp.bfloat16), query_band, NN) * scaling).astype(jnp.bfloat16)
        value_grad[at, 0] = dot(weights, grad_band, NN).astype(jnp.bfloat16)


def pair_spec(frames, tokens, dim):
    return pl.BlockSpec((2, frames, 1, tokens, dim), lambda head: (0, 0, head, 0, 0))


def edge_spec(tokens, dim):
    return pl.BlockSpec((3, 2, 1, tokens, dim), lambda head: (0, 0, head, 0, 0))


def whole_spec(shape):
    return pl.BlockSpec(shape, lambda head: (0,) * len(shape))


def head_spec(count, rows, dim):
    return pl.BlockSpec((count, 1, rows, dim), lambda head: (0, head, 0, 0))


def cost(frames, groups, tokens, dim):
    return pl.CostEstimate(
        flops=frames * groups * 8 * tokens * 9 * tokens * dim,
        bytes_accessed=groups * (frames + 2) * 3 * 2 * tokens * dim * 2,
        transcendentals=frames * groups * tokens * 9 * tokens,
    )


def front(pair, halo, bias, scaling):
    _, frames, groups, tokens, dim = pair.shape
    grad = jax.ShapeDtypeStruct((frames, groups, tokens, dim), jnp.bfloat16)
    near = pair_spec(frames, tokens, dim)
    edge = edge_spec(tokens, dim)
    return pl.pallas_call(
        functools.partial(front_kernel, scaling),
        grid=(groups,),
        out_shape=(grad, grad, jax.ShapeDtypeStruct((frames, groups, 2, tokens), jnp.float32)),
        in_specs=[near, near, near, near, edge, edge, whole_spec(bias.shape)],
        out_specs=(
            head_spec(frames, tokens, dim),
            head_spec(frames, tokens, dim),
            head_spec(frames, 2, tokens),
        ),
        scratch_shapes=[pltpu.VMEM((3 * (frames + 2) * tokens, dim), jnp.bfloat16)] * 2,
        compiler_params=pltpu.CompilerParams(vmem_limit_bytes=32 * 2**20),
        cost_estimate=cost(frames, groups, tokens, dim),
    )(pair, *halo, bias)


def back(pair, halo, stats, bias, scaling):
    _, frames, groups, tokens, dim = pair.shape
    grad = jax.ShapeDtypeStruct((frames, groups, tokens, dim), jnp.bfloat16)
    near = pair_spec(frames, tokens, dim)
    edge = edge_spec(tokens, dim)
    near_st = head_spec(frames, 2, tokens)
    edge_st = head_spec(3, 2, tokens)
    return pl.pallas_call(
        functools.partial(back_kernel, scaling),
        grid=(groups,),
        out_shape=(grad, grad),
        in_specs=[near, near, near, near, edge, edge]
        + [near_st, near_st, near_st, edge_st, edge_st, whole_spec(bias.shape)],
        out_specs=(head_spec(frames, tokens, dim), head_spec(frames, tokens, dim)),
        scratch_shapes=[pltpu.VMEM((3 * (frames + 2) * tokens, dim), jnp.bfloat16)] * 2,
        compiler_params=pltpu.CompilerParams(vmem_limit_bytes=32 * 2**20),
        cost_estimate=cost(frames, groups, tokens, dim),
    )(pair, *halo, *stats, bias)


def step_along(tensor, axis, sign):
    size = lax.axis_size(axis)
    return lax.ppermute(tensor, axis, [(i, i + sign) for i in range(size) if 0 <= i + sign < size])


def turn(tensor, shift):
    size = lax.axis_size("head")
    return lax.ppermute(tensor, "head", [(i, (i + shift) % size) for i in range(size)])


def surroundings(own, frame_dim):
    before = step_along(own, "row", 1)
    after = step_along(own, "row", -1)

    def edge(at):
        parts = [lax.index_in_dim(part, at, frame_dim, keepdims=False) for part in (before, own, after)]
        return jnp.stack(parts)

    low = step_along(edge(own.shape[frame_dim] - 1), "frame", 1)
    high = step_along(edge(0), "frame", -1)
    return own, before, after, low, high


def tile_biases(active, frames, columns_here, tokens):
    size = lax.axis_size("head")
    me = lax.axis_index("head")
    frame_at = lax.axis_index("frame") * frames
    row_at = lax.axis_index("row")
    all_frames, all_rows, count, slots = active.shape
    padded = jnp.pad(active.astype(jnp.float32), ((1, 1), (1, 1), (0, 0), (0, 0)))
    near = lax.dynamic_slice(padded, (frame_at, row_at, 0, 0), (frames + 2, 3, count, slots))
    near = near.reshape(frames + 2, 3, count, 9, 3)
    frame_ids = frame_at - 1 + jnp.arange(frames + 2)
    row_ids = row_at - 1 + jnp.arange(3)
    inside = ((frame_ids >= 0) & (frame_ids < all_frames))[:, None] & ((row_ids >= 0) & (row_ids < all_rows))
    inside = inside.astype(jnp.float32)
    tile_of = ((me + jnp.arange(size)) % size * columns_here) // TC

    def layers(own_tile, other_tile):
        shift = other_tile - own_tile
        if abs(shift) > 1:
            nothing = jnp.zeros((frames, 9), jnp.float32)
            return nothing, nothing
        ahead, behind = [], []
        for offset in range(9):
            frame_step, row_step = offset // 3, offset % 3
            chosen = near[1 : 1 + frames, 1, own_tile, offset, shift + 1]
            ahead.append(chosen * inside[frame_step : frame_step + frames, row_step])
            behind.append(near[frame_step : frame_step + frames, row_step, own_tile, 8 - offset, 1 - shift])
        return jnp.stack(ahead, 1), jnp.stack(behind, 1)

    table = [[layers(i, j) for j in range(count)] for i in range(count)]
    biases = []
    for which in range(2):
        tiles = jnp.stack([jnp.stack([table[i][j][which] for j in range(count)]) for i in range(count)])
        chosen = jnp.zeros((size, size, frames, 9), jnp.float32)
        for i in range(count):
            for j in range(count):
                here = ((tile_of == i)[:, None] & (tile_of == j)[None, :])[:, :, None, None]
                chosen = jnp.where(here, tiles[i, j], chosen)
        bias = jnp.where(chosen > 0.5, 0.0, MASKED).transpose(2, 0, 3, 1)
        bias = jnp.broadcast_to(bias[..., None], (frames, size, 9, size, tokens // size))
        biases.append(bias.reshape(frames, size, 9 * tokens))
    return biases


def on_device(queries, keys, values, out_grad, active):
    frames, rows, columns_here, heads, dim = queries.shape
    size = lax.axis_size("head")
    me = lax.axis_index("head")
    groups = heads // size
    cells = rows * columns_here
    tokens = cells * size
    scaling = dim ** (-0.5)

    def to_heads(tensors):
        moved = [t.reshape(frames, cells, heads, dim).transpose(0, 2, 1, 3) for t in tensors]
        stacked = jnp.stack(moved)

        def group(shift):
            return lax.dynamic_slice_in_dim(stacked, (me + shift) % size * groups, groups, 2)

        parts = [group(0)] + [turn(group(size - b), size - b) for b in range(1, size)]
        return jnp.concatenate(parts, axis=3)

    def from_heads(tensors):
        stacked = jnp.stack(tensors)

        def block(b):
            return lax.slice_in_dim(stacked, b * cells, (b + 1) * cells, axis=3)

        whole = jnp.zeros((len(tensors), frames, heads, cells, dim), jnp.bfloat16)
        for b in range(size):
            piece = block(0) if b == 0 else turn(block(b), b)
            whole = lax.dynamic_update_slice_in_dim(whole, piece, (me + size - b) % size * groups, 2)
        whole = whole.reshape(len(tensors), frames, heads, rows, columns_here, dim).transpose(0, 1, 3, 4, 2, 5)
        return [whole[i] for i in range(len(tensors))]

    front_bias, back_bias = tile_biases(active, frames, columns_here, tokens)
    key_value = to_heads((keys, values))
    query_grad_out = to_heads((queries, out_grad))
    key_halo = surroundings(key_value, 1)
    query_halo = surroundings(query_grad_out, 1)
    attended, query_grad, stats = front(query_grad_out, key_halo, front_bias, scaling)
    stat_halo = surroundings(stats, 0)
    key_grad, value_grad = back(key_value, query_halo, stat_halo, back_bias, scaling)
    attended, query_grad = from_heads((attended, query_grad))
    key_grad, value_grad = from_heads((key_grad, value_grad))
    return attended, query_grad, key_grad, value_grad


def solution(mesh):
    spec = P("frame", "row", "head", None, None)
    return jax.shard_map(
        on_device, mesh=mesh, in_specs=(spec,) * 4 + (P(),), out_specs=(spec,) * 4, check_vma=False
    )
```

```python
import functools

import jax
import jax.numpy as jnp
import numpy as np
from jax import lax
from jax.experimental import pallas as pl
from jax.experimental.pallas import tpu as pltpu
from jax.sharding import PartitionSpec as P

TF = 1
TR = 8
TC = 8
MASKED = -1e30
LOG2E = 1.4426950408889634
NT = (((1,), (1,)), ((), ()))
NN = (((1,), (0,)), ((), ()))


def dot(left, right, dims):
    return lax.dot_general(left, right, dims, preferred_element_type=jnp.float32)


def flat(tiles):
    return tiles.reshape(tiles.shape[-4] * tiles.shape[-2], tiles.shape[-1])


def spread(bias, tokens):
    columns, width = bias.shape
    return jnp.broadcast_to(bias[None], (tokens // columns, columns, width)).reshape(tokens, width)


def fill_band(own, before, after, low, high, bands):
    frames = own.shape[0]
    tokens = own.shape[2] * own.shape[4]
    for at in range(frames + 2):
        for row, beside in enumerate((before, own, after)):
            place = pl.ds((3 * at + row) * tokens, tokens)
            for which, band in enumerate(bands):
                if at == 0:
                    band[place, :] = flat(low[row, which])
                elif at == frames + 1:
                    band[place, :] = flat(high[row, which])
                else:
                    band[place, :] = flat(beside[at - 1, which])


def front_kernel(scaling, pair, own, before, after, low, high, bias, grads, stats, key_all, value_all):
    frames, _, rows, _, columns, dim = pair.shape
    tokens = rows * columns
    fill_band(own, before, after, low, high, (key_all, value_all))
    windows = [pl.ds(3 * at * tokens, 9 * tokens) for at in range(frames)]
    scores = [
        dot(flat(pair[at, 0]), key_all[windows[at], :], NT) * (scaling * LOG2E) + spread(bias[at], tokens)
        for at in range(frames)
    ]
    grad_probs = [dot(flat(pair[at, 1]), value_all[windows[at], :], NT) for at in range(frames)]
    highest = [jnp.max(part, axis=1, keepdims=True) for part in scores]
    raised = [jnp.exp2(part - top) for part, top in zip(scores, highest)]
    total = [jnp.sum(part, axis=1, keepdims=True) for part in raised]
    weights = [part.astype(jnp.bfloat16) for part in raised]
    for at in range(frames):
        share = 1.0 / total[at]
        out = (dot(weights[at], value_all[windows[at], :], NN) * share).astype(jnp.bfloat16)
        grad = flat(pair[at, 1]).astype(jnp.float32)
        grad_dot = jnp.sum(grad * out.astype(jnp.float32), axis=1, keepdims=True)
        grad_scores = (weights[at].astype(jnp.float32) * (grad_probs[at] - grad_dot)).astype(jnp.bfloat16)
        query_grad = dot(grad_scores, key_all[windows[at], :], NN) * (share * scaling)
        grads[0, at, :, 0] = out.reshape(rows, columns, dim)
        grads[1, at, :, 0] = query_grad.astype(jnp.bfloat16).reshape(rows, columns, dim)
        lane = lax.broadcasted_iota(jnp.int32, (tokens, 128), 1)
        both = jnp.where(lane == 0, highest[at] + jnp.log2(total[at]), grad_dot)
        stats[at, 0] = jnp.transpose(both)[:2]


def back_kernel(
    scaling, pair, own, before, after, low, high, own_st, before_st, after_st, low_st, high_st, bias,
    grads, query_all, grad_all
):
    frames, _, rows, _, columns, dim = pair.shape
    tokens = rows * columns
    fill_band(own, before, after, low, high, (query_all, grad_all))

    def stat_row(at, row, which):
        if at == 0:
            return low_st[row, 0, which : which + 1]
        if at == frames + 1:
            return high_st[row, 0, which : which + 1]
        return (before_st, own_st, after_st)[row][at - 1, 0, which : which + 1]

    def stat_band(at, which):
        parts = [stat_row(at + step, row, which) for step in range(3) for row in range(3)]
        return jnp.concatenate(parts, axis=1)

    windows = [pl.ds(3 * at * tokens, 9 * tokens) for at in range(frames)]
    scores = [dot(flat(pair[at, 0]), query_all[windows[at], :], NT) for at in range(frames)]
    grad_probs = [dot(flat(pair[at, 1]), grad_all[windows[at], :], NT) for at in range(frames)]
    for at in range(frames):
        shift = spread(bias[at] - stat_band(at, 0), tokens)
        weights = jnp.exp2(scores[at] * (scaling * LOG2E) + shift).astype(jnp.bfloat16)
        grad_scores = weights.astype(jnp.float32) * (grad_probs[at] - stat_band(at, 1))
        key_grad = dot(grad_scores.astype(jnp.bfloat16), query_all[windows[at], :], NN) * scaling
        value_grad = dot(weights, grad_all[windows[at], :], NN)
        grads[0, at, :, 0] = key_grad.astype(jnp.bfloat16).reshape(rows, columns, dim)
        grads[1, at, :, 0] = value_grad.astype(jnp.bfloat16).reshape(rows, columns, dim)


def slab_spec(shape, first):
    lead, pairs, rows, _, columns, dim = shape
    return pl.BlockSpec((lead, pairs, rows, 1, columns, dim), lambda head: (0, 0, 0, head + first, 0, 0))


def stat_spec(shape, first):
    lead, _, pairs, tokens = shape
    return pl.BlockSpec((lead, 1, pairs, tokens), lambda head: (0, head + first, 0, 0))


def whole_spec(shape):
    return pl.BlockSpec(shape, lambda head: (0,) * len(shape))


def run(kernel, scaling, pair, halo, stats, bias, first, count):
    frames, _, rows, _, columns, dim = pair.shape
    tokens = rows * columns
    grads = jax.ShapeDtypeStruct((2, frames, rows, count, columns, dim), jnp.bfloat16)
    outs = [grads]
    out_specs = [slab_spec(grads.shape, 0)]
    if stats is None:
        outs.append(jax.ShapeDtypeStruct((frames, count, 2, tokens), jnp.float32))
        out_specs.append(stat_spec(outs[-1].shape, 0))
    stats = () if stats is None else stats
    return pl.pallas_call(
        functools.partial(kernel, scaling),
        grid=(count,),
        out_shape=tuple(outs),
        in_specs=[slab_spec(part.shape, first) for part in (pair,) + halo]
        + [stat_spec(part.shape, first) for part in stats]
        + [whole_spec(bias.shape)],
        out_specs=tuple(out_specs),
        scratch_shapes=[pltpu.VMEM((3 * (frames + 2) * tokens, dim), jnp.bfloat16)] * 2,
        compiler_params=pltpu.CompilerParams(vmem_limit_bytes=32 * 2**20),
        cost_estimate=pl.CostEstimate(
            flops=frames * count * 8 * tokens * 9 * tokens * dim,
            bytes_accessed=count * (frames + 2) * 3 * 2 * tokens * dim * 2,
            transcendentals=frames * count * tokens * 9 * tokens,
        ),
    )(pair, *halo, *stats, bias)


def step_along(tensor, axis, sign):
    size = lax.axis_size(axis)
    return lax.ppermute(tensor, axis, [(i, i + sign) for i in range(size) if 0 <= i + sign < size])


def turn(tensor, shift):
    size = lax.axis_size("head")
    return lax.ppermute(tensor, "head", [(i, (i + shift) % size) for i in range(size)])


def frame_edges(before, own, after):
    last = own.shape[0] - 1
    low = step_along(jnp.stack([before[last], own[last], after[last]]), "frame", 1)
    high = step_along(jnp.stack([before[0], own[0], after[0]]), "frame", -1)
    return low, high


def row_sides(own):
    return step_along(own, "row", 1), step_along(own, "row", -1)


def tile_biases(active, frames, rows, columns_here):
    size = lax.axis_size("head")
    me = lax.axis_index("head")
    frame_at = lax.axis_index("frame") * frames
    row_at = lax.axis_index("row")
    all_frames, all_rows, count, slots = active.shape
    padded = jnp.pad(active.astype(jnp.float32), ((1, 1), (1, 1), (0, 0), (0, 0)))
    near = lax.dynamic_slice(padded, (frame_at, row_at, 0, 0), (frames + 2, 3, count, slots))
    near = near.reshape(frames + 2, 3, count, 9, 3)
    steps = jnp.arange(3, dtype=jnp.int32) - 1
    frame_ids = frame_at + jnp.arange(frames, dtype=jnp.int32)[:, None] + steps
    frame_in = (frame_ids >= 0) & (frame_ids < all_frames)
    row_in = (row_at + steps >= 0) & (row_at + steps < all_rows)
    inside = (frame_in[:, :, None] & row_in).reshape(frames, 9).astype(jnp.float32)
    ahead = near[1 : 1 + frames, 1] * inside[:, None, :, None]
    pick = np.zeros((frames + 2, 3, 9, frames, 9), np.float32)
    for at in range(frames):
        for offset in range(9):
            pick[at + offset // 3, offset % 3, 8 - offset, at, offset] = 1.0
    behind = jnp.einsum("xyioc,xyofq->fiqc", near, pick)
    place = jnp.arange(size * columns_here, dtype=jnp.int32)
    tile = ((me + place // columns_here) % size * columns_here + place % columns_here) // TC
    biases = []
    for table, sign in ((ahead, 1), (behind, -1)):
        owner = tile[None] == jnp.arange(count, dtype=jnp.int32)[:, None]
        shift = (sign * (tile[None, :] - tile[:, None]))[None] == steps[:, None, None]
        chosen = (owner[:, None, :, None] & shift[None]).astype(jnp.float32)
        allowed = jnp.einsum("fioc,icpk->fpok", table, chosen)
        bias = jnp.where(allowed > 0.5, 0.0, MASKED)[:, :, :, None, :]
        bias = jnp.broadcast_to(bias, bias.shape[:3] + (rows,) + bias.shape[4:])
        biases.append(bias.reshape(frames, place.shape[0], -1))
    return biases


def on_device(queries, keys, values, out_grad, active):
    frames, rows, columns_here, heads, dim = queries.shape
    size = lax.axis_size("head")
    me = lax.axis_index("head")
    groups = heads // size
    scaling = dim ** (-0.5)

    def group_of(tensors, shift):
        start = (me + shift) % size * groups
        parts = [
            lax.dynamic_slice_in_dim(jnp.transpose(t, (0, 1, 3, 2, 4)), start, groups, 2) for t in tensors
        ]
        return jnp.stack(parts, 1)

    def send_columns(tensors):
        return [group_of(tensors, size - b) for b in range(1, size)]

    def from_heads(grads):
        whole = jnp.zeros((2, frames, rows, heads, columns_here, dim), jnp.bfloat16)
        for b in range(size):
            piece = lax.slice_in_dim(grads, b * columns_here, (b + 1) * columns_here, axis=4)
            piece = piece if b == 0 else turn(piece, b)
            whole = lax.dynamic_update_slice_in_dim(whole, piece, (me + size - b) % size * groups, 3)
        whole = jnp.transpose(whole, (0, 1, 2, 4, 3, 5))
        return whole[0], whole[1]

    front_bias, back_bias = tile_biases(active, frames, rows, columns_here)
    own_kv = group_of((keys, values), 0)
    moved_kv = [turn(part, size - 1 - at) for at, part in enumerate(send_columns((keys, values)))]
    sent_qg = send_columns((queries, out_grad))
    sent_qg, moved_kv = lax.optimization_barrier((sent_qg, moved_kv))
    kv = jnp.concatenate([own_kv] + moved_kv, axis=4)
    kv_before, kv_after = row_sides(kv)
    moved_qg = [turn(part, size - 1 - at) for at, part in enumerate(sent_qg)]
    qg = jnp.concatenate([group_of((queries, out_grad), 0)] + moved_qg, axis=4)
    qg, kv_before, kv_after = lax.optimization_barrier((qg, kv_before, kv_after))
    kv_low, kv_high = frame_edges(kv_before, kv, kv_after)
    qg_before, qg_after = row_sides(qg)
    key_halo = (kv, kv_before, kv_after, kv_low, kv_high)
    front_grads, stats = run(front_kernel, scaling, qg, key_halo, None, front_bias, 0, groups)
    st_before, st_after = row_sides(stats)
    qg_low, qg_high = frame_edges(qg_before, qg, qg_after)
    st_low, st_high = frame_edges(st_before, stats, st_after)
    query_halo = (qg, qg_before, qg_after, qg_low, qg_high)
    stat_halo = (stats, st_before, st_after, st_low, st_high)
    (back_grads,) = run(back_kernel, scaling, kv, query_halo, stat_halo, back_bias, 0, groups)
    return from_heads(front_grads) + from_heads(back_grads)


def solution(mesh):
    spec = P("frame", "row", "head", None, None)
    return jax.shard_map(
        on_device, mesh=mesh, in_specs=(spec,) * 4 + (P(),), out_specs=(spec,) * 4, check_vma=False
    )
```

```python
import functools

import jax
import jax.numpy as jnp
import numpy as np
from jax import lax
from jax.experimental import pallas as pl
from jax.experimental.pallas import tpu as pltpu
from jax.sharding import PartitionSpec as P

TF = 1
TR = 8
TC = 8
MASKED = -1e30
LOG2E = 1.4426950408889634
NT = (((1,), (1,)), ((), ()))
NN = (((1,), (0,)), ((), ()))


def dot(left, right, dims):
    return lax.dot_general(left, right, dims, preferred_element_type=jnp.float32)


def flat(tiles):
    return tiles.reshape(tiles.shape[-4] * tiles.shape[-2], tiles.shape[-1])


def spread(bias, tokens):
    columns, width = bias.shape
    return jnp.broadcast_to(bias[None], (tokens // columns, columns, width)).reshape(tokens, width)


def fill_band(band, own, before, after, low, high, at_of):
    frames = own.shape[0]
    tokens = own.shape[-4] * own.shape[-2]
    for at in range(frames + 2):
        for row, beside in enumerate((before, own, after)):
            if at == 0:
                tiles = low[at_of(row)]
            elif at == frames + 1:
                tiles = high[at_of(row)]
            else:
                tiles = beside[at_of(at - 1)]
            band[pl.ds((3 * at + row) * tokens, tokens), :] = flat(tiles)


def single(at):
    return at


def attend_kernel(scaling, pair, *refs):
    keys, values = refs[:5], refs[5:10]
    bias, attended, stats, key_all, value_all = refs[10:]
    frames, _, rows, _, columns, dim = pair.shape
    tokens = rows * columns
    fill_band(key_all, *keys, single)
    fill_band(value_all, *values, single)
    windows = [pl.ds(3 * at * tokens, 9 * tokens) for at in range(frames)]
    scores = [
        dot(flat(pair[at, 0]), key_all[windows[at], :], NT) * (scaling * LOG2E) + spread(bias[at], tokens)
        for at in range(frames)
    ]
    highest = [jnp.max(part, axis=1, keepdims=True) for part in scores]
    raised = [jnp.exp2(part - top) for part, top in zip(scores, highest)]
    total = [jnp.sum(part, axis=1, keepdims=True) for part in raised]
    sums = [dot(raised[at].astype(jnp.bfloat16), value_all[windows[at], :], NN) for at in range(frames)]
    for at in range(frames):
        out = (sums[at] * (1.0 / total[at])).astype(jnp.bfloat16)
        grad = flat(pair[at, 1]).astype(jnp.float32)
        grad_dot = jnp.sum(grad * out.astype(jnp.float32), axis=1, keepdims=True)
        attended[at, :, 0] = out.reshape(rows, columns, dim)
        lane = lax.broadcasted_iota(jnp.int32, (tokens, 128), 1)
        both = jnp.where(lane == 0, highest[at] + jnp.log2(total[at]), grad_dot)
        stats[at, 0] = jnp.transpose(both)[:2]


def query_kernel(scaling, pair, *refs):
    keys, values = refs[:5], refs[5:10]
    attended, stats, bias, grads, key_all, value_all = refs[10:]
    frames, _, rows, _, columns, dim = pair.shape
    tokens = rows * columns
    fill_band(key_all, *keys, single)
    fill_band(value_all, *values, single)
    windows = [pl.ds(3 * at * tokens, 9 * tokens) for at in range(frames)]

    def column(at, which):
        wide = jnp.broadcast_to(stats[at, 0, which : which + 1], (128, tokens))
        return jnp.transpose(wide)[:, :1]

    scores = [dot(flat(pair[at, 0]), key_all[windows[at], :], NT) for at in range(frames)]
    grad_probs = [dot(flat(pair[at, 1]), value_all[windows[at], :], NT) for at in range(frames)]
    for at in range(frames):
        shift = spread(bias[at], tokens) - column(at, 0)
        weights = jnp.exp2(scores[at] * (scaling * LOG2E) + shift)
        grad_scores = (weights * (grad_probs[at] - column(at, 1))).astype(jnp.bfloat16)
        query_grad = dot(grad_scores, key_all[windows[at], :], NN) * scaling
        grads[0, at, :, 0] = attended[at, :, 0]
        grads[1, at, :, 0] = query_grad.astype(jnp.bfloat16).reshape(rows, columns, dim)


def back_kernel(
    scaling, keys, values, own, before, after, low, high, own_st, before_st, after_st, low_st, high_st, bias,
    grads, query_all, grad_all
):
    frames, rows, _, columns, dim = keys.shape
    tokens = rows * columns
    halo = (own, before, after, low, high)
    fill_band(query_all, *halo, lambda at: (at, 0))
    fill_band(grad_all, *halo, lambda at: (at, 1))

    def stat_row(at, row, which):
        if at == 0:
            return low_st[row, 0, which : which + 1]
        if at == frames + 1:
            return high_st[row, 0, which : which + 1]
        return (before_st, own_st, after_st)[row][at - 1, 0, which : which + 1]

    def stat_band(at, which):
        parts = [stat_row(at + step, row, which) for step in range(3) for row in range(3)]
        return jnp.concatenate(parts, axis=1)

    windows = [pl.ds(3 * at * tokens, 9 * tokens) for at in range(frames)]
    scores = [dot(flat(keys[at]), query_all[windows[at], :], NT) for at in range(frames)]
    grad_probs = [dot(flat(values[at]), grad_all[windows[at], :], NT) for at in range(frames)]
    for at in range(frames):
        shift = spread(bias[at] - stat_band(at, 0), tokens)
        weights = jnp.exp2(scores[at] * (scaling * LOG2E) + shift).astype(jnp.bfloat16)
        grad_scores = weights.astype(jnp.float32) * (grad_probs[at] - stat_band(at, 1))
        key_grad = dot(grad_scores.astype(jnp.bfloat16), query_all[windows[at], :], NN) * scaling
        value_grad = dot(weights, grad_all[windows[at], :], NN)
        grads[0, at, :, 0] = key_grad.astype(jnp.bfloat16).reshape(rows, columns, dim)
        grads[1, at, :, 0] = value_grad.astype(jnp.bfloat16).reshape(rows, columns, dim)


def head_spec(shape, dim, first):
    block = shape[:dim] + (1,) + shape[dim + 1 :]
    return pl.BlockSpec(block, lambda head: (0,) * dim + (head + first,) + (0,) * (len(shape) - dim - 1))


def whole_spec(shape):
    return pl.BlockSpec(shape, lambda head: (0,) * len(shape))


def run(kernel, scaling, tiles, stats, bias, outs, first, count, products):
    rows, _, columns, dim = tiles[0].shape[-4:]
    frames = tiles[0].shape[0]
    tokens = rows * columns
    return pl.pallas_call(
        functools.partial(kernel, scaling),
        grid=(count,),
        out_shape=tuple(outs),
        in_specs=[head_spec(part.shape, part.ndim - 3, first) for part in tuple(tiles) + tuple(stats)]
        + [whole_spec(bias.shape)],
        out_specs=tuple(head_spec(out.shape, len(out.shape) - 3, 0) for out in outs),
        scratch_shapes=[pltpu.VMEM((3 * (frames + 2) * tokens, dim), jnp.bfloat16)] * 2,
        compiler_params=pltpu.CompilerParams(vmem_limit_bytes=32 * 2**20),
        cost_estimate=pl.CostEstimate(
            flops=frames * count * 2 * products * tokens * 9 * tokens * dim,
            bytes_accessed=count * (frames + 2) * 3 * 2 * tokens * dim * 2,
            transcendentals=frames * count * tokens * 9 * tokens,
        ),
    )(*tiles, *stats, bias)


def step_along(tensor, axis, sign):
    size = lax.axis_size(axis)
    return lax.ppermute(tensor, axis, [(i, i + sign) for i in range(size) if 0 <= i + sign < size])


def turn(tensor, shift):
    size = lax.axis_size("head")
    return lax.ppermute(tensor, "head", [(i, (i + shift) % size) for i in range(size)])


def frame_edges(before, own, after):
    last = own.shape[0] - 1
    low = step_along(jnp.stack([before[last], own[last], after[last]]), "frame", 1)
    high = step_along(jnp.stack([before[0], own[0], after[0]]), "frame", -1)
    return low, high


def row_sides(own):
    return step_along(own, "row", 1), step_along(own, "row", -1)


def tile_biases(active, frames, rows, columns_here):
    size = lax.axis_size("head")
    me = lax.axis_index("head")
    frame_at = lax.axis_index("frame") * frames
    row_at = lax.axis_index("row")
    all_frames, all_rows, count, slots = active.shape
    padded = jnp.pad(active.astype(jnp.float32), ((1, 1), (1, 1), (0, 0), (0, 0)))
    near = lax.dynamic_slice(padded, (frame_at, row_at, 0, 0), (frames + 2, 3, count, slots))
    near = near.reshape(frames + 2, 3, count, 9, 3)
    steps = jnp.arange(3, dtype=jnp.int32) - 1
    frame_ids = frame_at + jnp.arange(frames, dtype=jnp.int32)[:, None] + steps
    frame_in = (frame_ids >= 0) & (frame_ids < all_frames)
    row_in = (row_at + steps >= 0) & (row_at + steps < all_rows)
    inside = (frame_in[:, :, None] & row_in).reshape(frames, 9).astype(jnp.float32)
    ahead = near[1 : 1 + frames, 1] * inside[:, None, :, None]
    pick = np.zeros((frames + 2, 3, 9, frames, 9), np.float32)
    for at in range(frames):
        for offset in range(9):
            pick[at + offset // 3, offset % 3, 8 - offset, at, offset] = 1.0
    behind = jnp.einsum("xyioc,xyofq->fiqc", near, pick)
    place = jnp.arange(size * columns_here, dtype=jnp.int32)
    tile = ((me + place // columns_here) % size * columns_here + place % columns_here) // TC
    repeat = np.kron(np.eye(9), np.kron(np.ones((1, rows)), np.eye(place.shape[0])))
    spread_out = jnp.asarray(repeat, jnp.bfloat16)
    smalls = []
    for table, sign in ((ahead, 1), (behind, -1)):
        owner = tile[None] == jnp.arange(count, dtype=jnp.int32)[:, None]
        shift = (sign * (tile[None, :] - tile[:, None]))[None] == steps[:, None, None]
        chosen = (owner[:, None, :, None] & shift[None]).astype(jnp.float32)
        smalls.append(jnp.einsum("fioc,icpk->fpok", table, chosen))
    small = jnp.stack(smalls).reshape(2 * frames * place.shape[0], -1).astype(jnp.bfloat16)
    allowed = jnp.dot(small, spread_out, preferred_element_type=jnp.float32)
    bias = jnp.where(allowed > 0.5, 0.0, MASKED).reshape(2, frames, place.shape[0], -1)
    return bias[0], bias[1]


def on_device(queries, keys, values, out_grad, active):
    frames, rows, columns_here, heads, dim = queries.shape
    size = lax.axis_size("head")
    me = lax.axis_index("head")
    groups = heads // size
    scaling = dim ** (-0.5)

    def group_of(tensor, shift):
        start = (me + shift) % size * groups
        return lax.dynamic_slice_in_dim(jnp.transpose(tensor, (0, 1, 3, 2, 4)), start, groups, 2)

    def pair_of(first, second, shift):
        return jnp.stack([group_of(first, shift), group_of(second, shift)], 1)

    def gather_columns(pick):
        moved = [turn(pick(size - b), size - b) for b in range(1, size)]
        return jnp.concatenate([pick(0)] + moved, axis=-2)

    def from_heads(parts):
        whole = jnp.zeros((2, frames, rows, heads, columns_here, dim), jnp.bfloat16)
        for first, grads in parts:
            for b in range(size):
                piece = lax.slice_in_dim(grads, b * columns_here, (b + 1) * columns_here, axis=4)
                piece = piece if b == 0 else turn(piece, b)
                start = (me + size - b) % size * groups + first
                whole = lax.dynamic_update_slice_in_dim(whole, piece, start, 3)
        whole = jnp.transpose(whole, (0, 1, 2, 4, 3, 5))
        return whole[0], whole[1]

    front_bias, back_bias = tile_biases(active, frames, rows, columns_here)
    held = [pair_of(queries, out_grad, shift) for shift in range(size)]
    key = gather_columns(lambda shift: group_of(keys, shift))
    value = gather_columns(lambda shift: group_of(values, shift))
    held, key = lax.optimization_barrier((held, key))
    pair = gather_columns(lambda shift: held[shift])
    columns = columns_here * size
    tokens = rows * columns

    def surround(own):
        sides = row_sides(own)
        return (own,) + sides + frame_edges(sides[0], own, sides[1])

    def out_shape(lead, count):
        return jax.ShapeDtypeStruct(lead + (frames, rows, count, columns, dim), jnp.bfloat16)

    stat_shape = jax.ShapeDtypeStruct((frames, groups, 2, tokens), jnp.float32)
    key_sides = row_sides(key)
    pair, key_sides = lax.optimization_barrier((pair, key_sides))
    around = (key,) + key_sides + frame_edges(key_sides[0], key, key_sides[1]) + surround(value)
    attended, stats = run(
        attend_kernel, scaling, (pair,) + around, (), front_bias, [out_shape((), groups), stat_shape], 0, groups, 2
    )
    (front_grads,) = run(
        query_kernel, scaling, (pair,) + around + (attended,), (stats,), front_bias, [out_shape((2,), groups)],
        0, groups, 3
    )
    pair_around = surround(pair)
    stats_around = surround(stats)
    halves = [(0, groups - groups // 2), (groups - groups // 2, groups // 2)]
    parts = []
    for first, count in halves:
        (back_grads,) = run(
            back_kernel, scaling, (key, value) + pair_around, stats_around, back_bias, [out_shape((2,), count)],
            first, count, 4
        )
        parts.append((first, back_grads))
    return from_heads([(0, front_grads)]) + from_heads(parts)


def solution(mesh):
    spec = P("frame", "row", "head", None, None)
    return jax.shard_map(
        on_device, mesh=mesh, in_specs=(spec,) * 4 + (P(),), out_specs=(spec,) * 4, check_vma=False
    )
```

```python
import functools

import jax
import jax.numpy as jnp
import numpy as np
from jax import lax
from jax.experimental import pallas as pl
from jax.experimental.pallas import tpu as pltpu
from jax.sharding import PartitionSpec as P

TF = 1
TR = 8
TC = 8
MASKED = -1e30
LOG2E = 1.4426950408889634
NT = (((1,), (1,)), ((), ()))
NN = (((1,), (0,)), ((), ()))


def dot(left, right, dims):
    return lax.dot_general(left, right, dims, preferred_element_type=jnp.float32)


def flat(tiles):
    return tiles.reshape(tiles.shape[-4] * tiles.shape[-2], tiles.shape[-1])


def spread(bias, tokens):
    columns, width = bias.shape
    return jnp.broadcast_to(bias[None], (tokens // columns, columns, width)).reshape(tokens, width)


def fill_band(band, own, before, after, low, high, side, edge):
    frames = own.shape[0]
    tokens = own.shape[-4] * own.shape[-2]
    for at in range(frames + 2):
        for row, beside in enumerate((before, own, after)):
            if at == 0:
                tiles = low[edge(row)]
            elif at == frames + 1:
                tiles = high[edge(row)]
            else:
                tiles = beside[side(at - 1)]
            band[pl.ds((3 * at + row) * tokens, tokens), :] = flat(tiles)


def fill_halo(halo, key_all, value_all):
    fill_band(key_all, *halo[:3], *halo[6:], lambda at: at, lambda row: (row, 0))
    fill_band(value_all, *halo[3:6], *halo[6:], lambda at: at, lambda row: (row, 1))


def attend_kernel(scaling, pair, *refs):
    bias, attended, stats, key_all, value_all = refs[8:]
    frames, _, rows, _, columns, dim = pair.shape
    tokens = rows * columns
    fill_halo(refs[:8], key_all, value_all)
    windows = [pl.ds(3 * at * tokens, 9 * tokens) for at in range(frames)]
    scores = [
        dot(flat(pair[at, 0]), key_all[windows[at], :], NT) * (scaling * LOG2E) + spread(bias[at], tokens)
        for at in range(frames)
    ]
    highest = [jnp.max(part, axis=1, keepdims=True) for part in scores]
    raised = [jnp.exp2(part - top) for part, top in zip(scores, highest)]
    total = [jnp.sum(part, axis=1, keepdims=True) for part in raised]
    sums = [dot(raised[at].astype(jnp.bfloat16), value_all[windows[at], :], NN) for at in range(frames)]
    for at in range(frames):
        out = (sums[at] * (1.0 / total[at])).astype(jnp.bfloat16)
        grad = flat(pair[at, 1]).astype(jnp.float32)
        grad_dot = jnp.sum(grad * out.astype(jnp.float32), axis=1, keepdims=True)
        attended[at, :, 0] = out.reshape(rows, columns, dim)
        lane = lax.broadcasted_iota(jnp.int32, (tokens, 128), 1)
        both = jnp.where(lane == 0, highest[at] + jnp.log2(total[at]), grad_dot)
        stats[at, 0] = jnp.transpose(both)[:2]


def query_kernel(scaling, pair, *refs):
    attended, stats, bias, grads, key_all, value_all = refs[8:]
    frames, _, rows, _, columns, dim = pair.shape
    tokens = rows * columns
    fill_halo(refs[:8], key_all, value_all)
    windows = [pl.ds(3 * at * tokens, 9 * tokens) for at in range(frames)]

    def column(at, which):
        wide = jnp.broadcast_to(stats[at, 0, which : which + 1], (128, tokens))
        return jnp.transpose(wide)[:, :1]

    scores = [dot(flat(pair[at, 0]), key_all[windows[at], :], NT) for at in range(frames)]
    grad_probs = [dot(flat(pair[at, 1]), value_all[windows[at], :], NT) for at in range(frames)]
    for at in range(frames):
        shift = spread(bias[at], tokens) - column(at, 0)
        weights = jnp.exp2(scores[at] * (scaling * LOG2E) + shift)
        grad_scores = (weights * (grad_probs[at] - column(at, 1))).astype(jnp.bfloat16)
        query_grad = dot(grad_scores, key_all[windows[at], :], NN) * scaling
        grads[0, at, :, 0] = attended[at, :, 0]
        grads[1, at, :, 0] = query_grad.astype(jnp.bfloat16).reshape(rows, columns, dim)


def back_kernel(scaling, spots, keys, values, own, before, after, low, high, *refs):
    stats, (bias, grads, query_all, grad_all) = refs[:9], refs[9:]
    frames, rows, _, columns, dim = keys.shape
    tokens = rows * columns
    halo = (own, before, after, low, high)
    fill_band(query_all, *halo, lambda at: (at, 0), lambda row: (row, 0))
    fill_band(grad_all, *halo, lambda at: (at, 1), lambda row: (row, 1))

    def stat_row(at, row, which):
        device = 0 if at == 0 else 2 if at == frames + 1 else 1
        return stats[3 * device + row][0, 0, (at - 1) % frames, 0, which : which + 1]

    def stat_band(at, which):
        parts = [stat_row(at + step, row, which) for step in range(3) for row in range(3)]
        return jnp.concatenate(parts, axis=1)

    windows = [pl.ds(3 * at * tokens, 9 * tokens) for at in range(frames)]
    scores = [dot(flat(keys[at]), query_all[windows[at], :], NT) for at in range(frames)]
    grad_probs = [dot(flat(values[at]), grad_all[windows[at], :], NT) for at in range(frames)]
    for at in range(frames):
        shift = spread(bias[at] - stat_band(at, 0), tokens)
        weights = jnp.exp2(scores[at] * (scaling * LOG2E) + shift).astype(jnp.bfloat16)
        grad_scores = weights.astype(jnp.float32) * (grad_probs[at] - stat_band(at, 1))
        key_grad = dot(grad_scores.astype(jnp.bfloat16), query_all[windows[at], :], NN) * scaling
        value_grad = dot(weights, grad_all[windows[at], :], NN)
        grads[0, at, :, 0] = key_grad.astype(jnp.bfloat16).reshape(rows, columns, dim)
        grads[1, at, :, 0] = value_grad.astype(jnp.bfloat16).reshape(rows, columns, dim)


def head_spec(shape, dim, first):
    block = shape[:dim] + (1,) + shape[dim + 1 :]
    return pl.BlockSpec(block, lambda head, *_: (0,) * dim + (head + first,) + (0,) * (len(shape) - dim - 1))


def near_spec(shape, first, at):
    block = (1, 1, shape[2], 1) + shape[4:]
    frame, row = at // 3, at % 3
    return pl.BlockSpec(block, lambda head, spots: (spots[0, frame], spots[1, row], 0, head + first, 0, 0))


def run(kernel, scaling, tiles, stats, bias, outs, first, count, products, spots=None):
    rows, _, columns, dim = tiles[0].shape[-4:]
    frames = tiles[0].shape[0]
    tokens = rows * columns
    bias_spec = pl.BlockSpec(bias.shape, lambda head, *_: (0,) * bias.ndim)
    in_specs = [head_spec(part.shape, part.ndim - 3, first) for part in tiles]
    prefetched = () if spots is None else (spots,)
    if spots is None:
        in_specs += [head_spec(part.shape, part.ndim - 3, first) for part in stats]
    else:
        in_specs += [near_spec(part.shape, first, at) for at, part in enumerate(stats)]
    return pl.pallas_call(
        functools.partial(kernel, scaling),
        grid_spec=pltpu.PrefetchScalarGridSpec(
            num_scalar_prefetch=len(prefetched),
            grid=(count,),
            in_specs=in_specs + [bias_spec],
            out_specs=tuple(head_spec(out.shape, len(out.shape) - 3, 0) for out in outs),
            scratch_shapes=[pltpu.VMEM((3 * (frames + 2) * tokens, dim), jnp.bfloat16)] * 2,
        ),
        out_shape=tuple(outs),
        compiler_params=pltpu.CompilerParams(vmem_limit_bytes=32 * 2**20),
        cost_estimate=pl.CostEstimate(
            flops=frames * count * 2 * products * tokens * 9 * tokens * dim,
            bytes_accessed=count * (frames + 2) * 3 * 2 * tokens * dim * 2,
            transcendentals=frames * count * tokens * 9 * tokens,
        ),
    )(*prefetched, *tiles, *stats, bias)


def step_along(tensor, axis, sign):
    size = lax.axis_size(axis)
    return lax.ppermute(tensor, axis, [(i, i + sign) for i in range(size) if 0 <= i + sign < size])


def turn(tensor, shift):
    size = lax.axis_size("head")
    return lax.ppermute(tensor, "head", [(i, (i + shift) % size) for i in range(size)])


def frame_edges(before, own, after):
    return step_along(jnp.stack([before[-1], own[-1], after[-1]]), "frame", 1), step_along(
        jnp.stack([before[0], own[0], after[0]]), "frame", -1
    )


def near_places(axis):
    at = lax.axis_index(axis) + jnp.arange(3, dtype=jnp.int32) - 1
    return jnp.clip(at, 0, lax.axis_size(axis) - 1)


def row_sides(own):
    return step_along(own, "row", 1), step_along(own, "row", -1)


def tile_biases(active, frames, rows, columns_here):
    size = lax.axis_size("head")
    me = lax.axis_index("head")
    frame_at = lax.axis_index("frame") * frames
    row_at = lax.axis_index("row")
    all_frames, all_rows, count, slots = active.shape
    padded = jnp.pad(active.astype(jnp.float32), ((1, 1), (1, 1), (0, 0), (0, 0)))
    near = lax.dynamic_slice(padded, (frame_at, row_at, 0, 0), (frames + 2, 3, count, slots))
    near = near.reshape(frames + 2, 3, count, 9, 3)
    steps = jnp.arange(3, dtype=jnp.int32) - 1
    frame_ids = frame_at + jnp.arange(frames, dtype=jnp.int32)[:, None] + steps
    frame_in = (frame_ids >= 0) & (frame_ids < all_frames)
    row_in = (row_at + steps >= 0) & (row_at + steps < all_rows)
    inside = (frame_in[:, :, None] & row_in).reshape(frames, 9).astype(jnp.float32)
    ahead = near[1 : 1 + frames, 1] * inside[:, None, :, None]
    pick = np.zeros((frames + 2, 3, 9, frames, 9), np.float32)
    for at in range(frames):
        for offset in range(9):
            pick[at + offset // 3, offset % 3, 8 - offset, at, offset] = 1.0
    behind = jnp.einsum("xyioc,xyofq->fiqc", near, pick)
    place = jnp.arange(size * columns_here, dtype=jnp.int32)
    tile = ((me + place // columns_here) % size * columns_here + place % columns_here) // TC
    repeat = np.kron(np.eye(9), np.kron(np.ones((1, rows)), np.eye(place.shape[0])))
    spread_out = jnp.asarray(repeat, jnp.bfloat16)
    smalls = []
    for table, sign in ((ahead, 1), (behind, -1)):
        owner = tile[None] == jnp.arange(count, dtype=jnp.int32)[:, None]
        shift = (sign * (tile[None, :] - tile[:, None]))[None] == steps[:, None, None]
        chosen = (owner[:, None, :, None] & shift[None]).astype(jnp.float32)
        smalls.append(jnp.einsum("fioc,icpk->fpok", table, chosen))
    small = jnp.stack(smalls).reshape(2 * frames * place.shape[0], -1).astype(jnp.bfloat16)
    allowed = jnp.dot(small, spread_out, preferred_element_type=jnp.float32)
    bias = jnp.where(allowed > 0.5, 0.0, MASKED).reshape(2, frames, place.shape[0], -1)
    return bias[0], bias[1]


def on_device(queries, keys, values, out_grad, active):
    frames, rows, columns_here, heads, dim = queries.shape
    size = lax.axis_size("head")
    me = lax.axis_index("head")
    groups = heads // size
    scaling = dim ** (-0.5)

    def group_of(tensor, shift):
        start = (me + shift) % size * groups
        return lax.dynamic_slice_in_dim(jnp.transpose(tensor, (0, 1, 3, 2, 4)), start, groups, 2)

    def pair_of(first, second, shift):
        return jnp.stack([group_of(first, shift), group_of(second, shift)], 1)

    def gather_columns(pick):
        moved = [turn(pick(size - b), size - b) for b in range(1, size)]
        return jnp.concatenate([pick(0)] + moved, axis=-2)

    def from_heads(parts):
        whole = jnp.zeros((2, frames, rows, heads, columns_here, dim), jnp.bfloat16)
        for first, grads in parts:
            for b in range(size):
                piece = lax.slice_in_dim(grads, b * columns_here, (b + 1) * columns_here, axis=4)
                piece = piece if b == 0 else turn(piece, b)
                start = (me + size - b) % size * groups + first
                whole = lax.dynamic_update_slice_in_dim(whole, piece, start, 3)
        whole = jnp.transpose(whole, (0, 1, 2, 4, 3, 5))
        return whole[0], whole[1]

    front_bias, back_bias = tile_biases(active, frames, rows, columns_here)
    held = [pair_of(queries, out_grad, shift) for shift in range(size)]
    key = gather_columns(lambda shift: group_of(keys, shift))
    value = gather_columns(lambda shift: group_of(values, shift))
    held, key = lax.optimization_barrier((held, key))
    pair = gather_columns(lambda shift: held[shift])
    columns = columns_here * size
    tokens = rows * columns

    def out_shape(lead, count):
        return jax.ShapeDtypeStruct(lead + (frames, rows, count, columns, dim), jnp.bfloat16)

    stat_shape = jax.ShapeDtypeStruct((frames, groups, 2, tokens), jnp.float32)
    key_sides = row_sides(key)
    pair, key_sides = lax.optimization_barrier((pair, key_sides))
    value_sides = row_sides(value)
    key_rows = (key_sides[0], key, key_sides[1])
    value_rows = (value_sides[0], value, value_sides[1])
    low, high = frame_edges(*[jnp.stack(two, 1) for two in zip(key_rows, value_rows)])
    around = (key,) + key_sides + (value,) + value_sides + (low, high)
    pair_sides = row_sides(pair)
    pair_around = (pair,) + pair_sides + frame_edges(pair_sides[0], pair, pair_sides[1])
    attended, stats = run(
        attend_kernel, scaling, (pair,) + around, (), front_bias, [out_shape((), groups), stat_shape], 0, groups, 2
    )
    (front_grads,) = run(
        query_kernel, scaling, (pair,) + around + (attended,), (stats,), front_bias, [out_shape((2,), groups)],
        0, groups, 3
    )
    gathered = lax.all_gather(stats, ("frame", "row")).reshape((lax.axis_size("frame"), lax.axis_size("row")) + stats.shape)
    spots = jnp.stack([near_places("frame"), near_places("row")])
    halves = [(0, groups - groups // 2), (groups - groups // 2, groups // 2)]
    parts = []
    for first, count in halves:
        (back_grads,) = run(
            back_kernel, scaling, (key, value) + pair_around, (gathered,) * 9, back_bias,
            [out_shape((2,), count)], first, count, 4, spots
        )
        parts.append((first, back_grads))
    return from_heads([(0, front_grads)]) + from_heads(parts)


def solution(mesh):
    spec = P("frame", "row", "head", None, None)
    return jax.shard_map(
        on_device, mesh=mesh, in_specs=(spec,) * 4 + (P(),), out_specs=(spec,) * 4, check_vma=False
    )
```

```python
import functools

import jax
import jax.numpy as jnp
import numpy as np
from jax import lax
from jax.experimental import pallas as pl
from jax.experimental.pallas import tpu as pltpu
from jax.sharding import PartitionSpec as P

TF = 1
TR = 8
TC = 8
MASKED = -1e30
LOG2E = 1.4426950408889634
NT = (((1,), (1,)), ((), ()))
NN = (((1,), (0,)), ((), ()))


def dot(left, right, dims):
    return lax.dot_general(left, right, dims, preferred_element_type=jnp.float32)


def spread(bias, tokens):
    parts, width = bias.shape
    return jnp.broadcast_to(bias[:, None], (parts, tokens // parts, width)).reshape(tokens, width)


def fill_bands(halo, bands):
    parts = len(halo) // 3
    own, before, after = halo[:parts], halo[parts : 2 * parts], halo[2 * parts : 3 * parts]
    low, high = halo[3 * parts :]
    frames, _, _, cells, _ = own[0].shape
    for at in range(frames + 2):
        for row, beside in enumerate((before, own, after)):
            for part in range(parts):
                place = pl.ds(((3 * at + row) * parts + part) * cells, cells)
                for which, band in enumerate(bands):
                    if at == 0:
                        band[place, :] = low[row * parts + part, which, 0]
                    elif at == frames + 1:
                        band[place, :] = high[row * parts + part, which, 0]
                    else:
                        band[place, :] = beside[part][at - 1, which, 0]


def slab(parts, at, which):
    return jnp.concatenate([part[at, which, 0] for part in parts], axis=0)


def attend_kernel(scaling, parts, *refs):
    pair, halo = refs[:parts], refs[parts : 4 * parts + 2]
    bias, attended, stats, key_all, value_all = refs[4 * parts + 2 :]
    frames, _, tokens, _ = attended.shape
    fill_bands(halo, (key_all, value_all))
    windows = [pl.ds(3 * at * tokens, 9 * tokens) for at in range(frames)]
    scores = [
        dot(slab(pair, at, 0), key_all[windows[at], :], NT) * (scaling * LOG2E) + spread(bias[at], tokens)
        for at in range(frames)
    ]
    highest = [jnp.max(part, axis=1, keepdims=True) for part in scores]
    raised = [jnp.exp2(part - top) for part, top in zip(scores, highest)]
    total = [jnp.sum(part, axis=1, keepdims=True) for part in raised]
    sums = [dot(raised[at].astype(jnp.bfloat16), value_all[windows[at], :], NN) for at in range(frames)]
    for at in range(frames):
        out = (sums[at] * (1.0 / total[at])).astype(jnp.bfloat16)
        grad = slab(pair, at, 1).astype(jnp.float32)
        grad_dot = jnp.sum(grad * out.astype(jnp.float32), axis=1, keepdims=True)
        attended[at, 0] = out
        lane = lax.broadcasted_iota(jnp.int32, (tokens, 128), 1)
        both = jnp.where(lane == 0, highest[at] + jnp.log2(total[at]), grad_dot)
        stats[at, 0] = jnp.transpose(both)[:2]


def store(grads, at, first, second):
    cells = grads[0].shape[-2]
    for part, out in enumerate(grads):
        own = slice(part * cells, (part + 1) * cells)
        out[0, at, 0] = first[own]
        out[1, at, 0] = second[own]


def query_kernel(scaling, parts, *refs):
    pair, halo = refs[:parts], refs[parts : 4 * parts + 2]
    attended, stats, bias = refs[4 * parts + 2 : 4 * parts + 5]
    grads, (key_all, value_all) = refs[4 * parts + 5 : -2], refs[-2:]
    frames, _, tokens, _ = attended.shape
    fill_bands(halo, (key_all, value_all))
    windows = [pl.ds(3 * at * tokens, 9 * tokens) for at in range(frames)]

    def column(at, which):
        wide = jnp.broadcast_to(stats[at, 0, which : which + 1], (128, tokens))
        return jnp.transpose(wide)[:, :1]

    scores = [dot(slab(pair, at, 0), key_all[windows[at], :], NT) for at in range(frames)]
    grad_probs = [dot(slab(pair, at, 1), value_all[windows[at], :], NT) for at in range(frames)]
    for at in range(frames):
        shift = spread(bias[at], tokens) - column(at, 0)
        weights = jnp.exp2(scores[at] * (scaling * LOG2E) + shift)
        grad_scores = (weights * (grad_probs[at] - column(at, 1))).astype(jnp.bfloat16)
        query_grad = dot(grad_scores, key_all[windows[at], :], NN) * scaling
        store(grads, at, attended[at, 0], query_grad.astype(jnp.bfloat16))


def back_kernel(scaling, parts, *refs):
    pair, halo = refs[:parts], refs[parts : 4 * parts + 2]
    own_st, before_st, after_st, low_st, high_st, bias = refs[4 * parts + 2 : 4 * parts + 8]
    grads, (query_all, grad_all) = refs[4 * parts + 8 : -2], refs[-2:]
    frames, _, _, tokens = own_st.shape
    fill_bands(halo, (query_all, grad_all))

    def stat_row(at, row, which):
        if at == 0:
            return low_st[row, 0, which : which + 1]
        if at == frames + 1:
            return high_st[row, 0, which : which + 1]
        return (before_st, own_st, after_st)[row][at - 1, 0, which : which + 1]

    def stat_band(at, which):
        rows = [stat_row(at + step, row, which) for step in range(3) for row in range(3)]
        return jnp.concatenate(rows, axis=1)

    windows = [pl.ds(3 * at * tokens, 9 * tokens) for at in range(frames)]
    scores = [dot(slab(pair, at, 0), query_all[windows[at], :], NT) for at in range(frames)]
    grad_probs = [dot(slab(pair, at, 1), grad_all[windows[at], :], NT) for at in range(frames)]
    for at in range(frames):
        shift = spread(bias[at] - stat_band(at, 0), tokens)
        weights = jnp.exp2(scores[at] * (scaling * LOG2E) + shift).astype(jnp.bfloat16)
        grad_scores = weights.astype(jnp.float32) * (grad_probs[at] - stat_band(at, 1))
        key_grad = dot(grad_scores.astype(jnp.bfloat16), query_all[windows[at], :], NN) * scaling
        value_grad = dot(weights, grad_all[windows[at], :], NN)
        store(grads, at, key_grad.astype(jnp.bfloat16), value_grad.astype(jnp.bfloat16))


def head_spec(shape, first):
    dim = len(shape) - 3
    block = shape[:dim] + (1,) + shape[dim + 1 :]
    return pl.BlockSpec(block, lambda head: (0,) * dim + (head + first,) + (0, 0))


def run(kernel, scaling, pair, halo, extra, bias, outs, first, count, products):
    parts = len(pair)
    frames, _, _, cells, dim = pair[0].shape
    tokens = parts * cells
    operands = tuple(pair) + tuple(halo) + tuple(extra)
    return pl.pallas_call(
        functools.partial(kernel, scaling, parts),
        grid=(count,),
        out_shape=tuple(outs),
        in_specs=[head_spec(part.shape, first) for part in operands]
        + [pl.BlockSpec(bias.shape, lambda head: (0,) * bias.ndim)],
        out_specs=tuple(head_spec(out.shape, 0) for out in outs),
        scratch_shapes=[pltpu.VMEM((3 * (frames + 2) * tokens, dim), jnp.bfloat16)] * 2,
        compiler_params=pltpu.CompilerParams(vmem_limit_bytes=32 * 2**20),
        cost_estimate=pl.CostEstimate(
            flops=frames * count * 2 * products * tokens * 9 * tokens * dim,
            bytes_accessed=count * (frames + 2) * 3 * 2 * tokens * dim * 2,
            transcendentals=frames * count * tokens * 9 * tokens,
        ),
    )(*operands, bias)


def step_along(tensor, axis, sign):
    size = lax.axis_size(axis)
    return lax.ppermute(tensor, axis, [(i, i + sign) for i in range(size) if 0 <= i + sign < size])


def turn(tensor, shift):
    size = lax.axis_size("head")
    return lax.ppermute(tensor, "head", [(i, (i + shift) % size) for i in range(size)])


def frame_edges(before, own, after):
    rows = (before, own, after)

    def edge(at):
        return jnp.stack([part[at] for row in rows for part in row])

    return step_along(edge(-1), "frame", 1), step_along(edge(0), "frame", -1)


def stat_edges(before, own, after):
    low = step_along(jnp.stack([before[-1], own[-1], after[-1]]), "frame", 1)
    return low, step_along(jnp.stack([before[0], own[0], after[0]]), "frame", -1)


def row_sides(own):
    return step_along(own, "row", 1), step_along(own, "row", -1)


def tile_biases(active, frames, columns_here, cells):
    size = lax.axis_size("head")
    me = lax.axis_index("head")
    frame_at = lax.axis_index("frame") * frames
    row_at = lax.axis_index("row")
    all_frames, all_rows, count, slots = active.shape
    padded = jnp.pad(active.astype(jnp.float32), ((1, 1), (1, 1), (0, 0), (0, 0)))
    near = lax.dynamic_slice(padded, (frame_at, row_at, 0, 0), (frames + 2, 3, count, slots))
    near = near.reshape(frames + 2, 3, count, 9, 3)
    steps = jnp.arange(3, dtype=jnp.int32) - 1
    frame_ids = frame_at + jnp.arange(frames, dtype=jnp.int32)[:, None] + steps
    frame_in = (frame_ids >= 0) & (frame_ids < all_frames)
    row_in = (row_at + steps >= 0) & (row_at + steps < all_rows)
    inside = (frame_in[:, :, None] & row_in).reshape(frames, 9).astype(jnp.float32)
    ahead = near[1 : 1 + frames, 1] * inside[:, None, :, None]
    pick = np.zeros((frames + 2, 3, 9, frames, 9), np.float32)
    for at in range(frames):
        for offset in range(9):
            pick[at + offset // 3, offset % 3, 8 - offset, at, offset] = 1.0
    behind = jnp.einsum("xyioc,xyofq->fiqc", near, pick)
    part = jnp.arange(size, dtype=jnp.int32)
    tile = ((me + part) % size * columns_here) // TC
    repeat = np.kron(np.eye(9 * size), np.ones((1, cells)))
    spread_out = jnp.asarray(repeat, jnp.bfloat16)
    smalls = []
    for table, sign in ((ahead, 1), (behind, -1)):
        owner = tile[None] == jnp.arange(count, dtype=jnp.int32)[:, None]
        shift = (sign * (tile[None, :] - tile[:, None]))[None] == steps[:, None, None]
        chosen = (owner[:, None, :, None] & shift[None]).astype(jnp.float32)
        smalls.append(jnp.einsum("fioc,icpk->fpok", table, chosen))
    small = jnp.stack(smalls).reshape(2 * frames * size, -1).astype(jnp.bfloat16)
    allowed = jnp.dot(small, spread_out, preferred_element_type=jnp.float32)
    bias = jnp.where(allowed > 0.5, 0.0, MASKED).reshape(2, frames, size, -1)
    return bias[0], bias[1]


def on_device(queries, keys, values, out_grad, active):
    frames, rows, columns_here, heads, dim = queries.shape
    size = lax.axis_size("head")
    me = lax.axis_index("head")
    groups = heads // size
    cells = rows * columns_here
    tokens = cells * size
    scaling = dim ** (-0.5)
    assert rows == TR and TC % columns_here == 0

    def pair_of(first, second, shift):
        start = (me + shift) % size * groups
        picked = [
            lax.dynamic_slice_in_dim(jnp.transpose(t, (0, 3, 1, 2, 4)), start, groups, 1) for t in (first, second)
        ]
        return jnp.stack(picked, 1).reshape(frames, 2, groups, cells, dim)

    def from_heads(blocks):
        whole = jnp.zeros((2, frames, rows, heads, columns_here, dim), jnp.bfloat16)
        for first, grads in blocks:
            for b, piece in enumerate(grads):
                piece = piece if b == 0 else turn(piece, b)
                piece = piece.reshape((2, frames, -1, rows, columns_here, dim)).transpose(0, 1, 3, 2, 4, 5)
                start = (me + size - b) % size * groups + first
                whole = lax.dynamic_update_slice_in_dim(whole, piece, start, 3)
        whole = jnp.transpose(whole, (0, 1, 2, 4, 3, 5))
        return whole[0], whole[1]

    def sides_of(parts):
        both = [row_sides(part) for part in parts]
        return [up for up, _ in both], [down for _, down in both]

    front_bias, back_bias = tile_biases(active, frames, columns_here, cells)
    key_sent = [pair_of(keys, values, shift) for shift in range(1, size)]
    key_sent, keys, values = lax.optimization_barrier((key_sent, keys, values))
    key_here = [pair_of(keys, values, 0)]
    key_near = sides_of(key_here)
    key_moved = [turn(key_sent[size - b - 1], size - b) for b in range(1, size)]
    query_held = [pair_of(queries, out_grad, shift) for shift in range(size)]
    query_held, key_moved = lax.optimization_barrier((query_held, key_moved))
    key_far = sides_of(key_moved)
    query_moved = [turn(query_held[size - b], size - b) for b in range(1, size)]
    query_parts = query_held[:1] + query_moved
    query_parts, key_near = lax.optimization_barrier((query_parts, key_near))
    query_near = sides_of(query_parts)
    key_parts = key_here + key_moved
    key_before, key_after = key_near[0] + key_far[0], key_near[1] + key_far[1]
    key_halo = key_parts + key_before + key_after + list(frame_edges(key_before, key_parts, key_after))
    query_before, query_after = query_near
    query_halo = (
        query_parts + query_before + query_after + list(frame_edges(query_before, query_parts, query_after))
    )

    def grads_shape(count):
        return [jax.ShapeDtypeStruct((2, frames, count, cells, dim), jnp.bfloat16)] * size

    attended_shape = jax.ShapeDtypeStruct((frames, groups, tokens, dim), jnp.bfloat16)
    stat_shape = jax.ShapeDtypeStruct((frames, groups, 2, tokens), jnp.float32)
    attended, stats = run(
        attend_kernel, scaling, query_parts, key_halo, (), front_bias, [attended_shape, stat_shape], 0, groups, 2
    )
    front_grads = run(
        query_kernel, scaling, query_parts, key_halo, (attended, stats), front_bias, grads_shape(groups),
        0, groups, 3
    )
    stat_sides = row_sides(stats)
    stat_halo = (stats,) + stat_sides + stat_edges(stat_sides[0], stats, stat_sides[1])
    blocks = []
    for first, count in ((0, groups - groups // 2), (groups - groups // 2, groups // 2)):
        back_grads = run(
            back_kernel, scaling, key_parts, query_halo, stat_halo, back_bias, grads_shape(count), first, count, 4
        )
        blocks.append((first, back_grads))
    return from_heads([(0, front_grads)]) + from_heads(blocks)


def solution(mesh):
    spec = P("frame", "row", "head", None, None)
    return jax.shard_map(
        on_device, mesh=mesh, in_specs=(spec,) * 4 + (P(),), out_specs=(spec,) * 4, check_vma=False
    )
```

```python
import functools

import jax
import jax.numpy as jnp
import numpy as np
from jax import lax
from jax.experimental import pallas as pl
from jax.experimental.pallas import tpu as pltpu
from jax.sharding import PartitionSpec as P

TF = 1
TR = 8
TC = 8
MASKED = -1e30
LOG2E = 1.4426950408889634
NT = (((1,), (1,)), ((), ()))
NN = (((1,), (0,)), ((), ()))


def dot(left, right, dims):
    return lax.dot_general(left, right, dims, preferred_element_type=jnp.float32)


def spread(bias, tokens):
    parts, width = bias.shape
    return jnp.broadcast_to(bias[:, None], (parts, tokens // parts, width)).reshape(tokens, width)


def fill_bands(frames, parts, cells, side, edge, bands):
    for at in range(frames + 2):
        for row in range(3):
            for part in range(parts):
                place = pl.ds(((3 * at + row) * parts + part) * cells, cells)
                for which, band in enumerate(bands):
                    if at == 0:
                        band[place, :] = edge(0, row, part, which)
                    elif at == frames + 1:
                        band[place, :] = edge(1, row, part, which)
                    else:
                        band[place, :] = side(row, part, at - 1, which)


def fill_keys(parts, halo, bands):
    rows = (halo[parts : 2 * parts], halo[:parts], halo[2 * parts : 3 * parts])
    edges = halo[3 * parts :]
    frames, _, _, cells, _ = halo[0].shape
    side = lambda row, part, at, which: rows[row][part][at, which, 0]
    edge = lambda end, row, part, which: edges[end][3 * part + row, which, 0]
    fill_bands(frames, parts, cells, side, edge, bands)


def fill_queries(halo, bands):
    own, before, after, low, high = halo
    parts, frames, _, _, cells, _ = own.shape
    side = lambda row, part, at, which: (before, own, after)[row][part, at, which, 0]
    edge = lambda end, row, part, which: (low, high)[end][3 * part + row, which, 0]
    fill_bands(frames, parts, cells, side, edge, bands)


def slab(parts, at, which):
    if isinstance(parts, list):
        return jnp.concatenate([part[at, which, 0] for part in parts], axis=0)
    return jnp.concatenate([parts[part, at, which, 0] for part in range(parts.shape[0])], axis=0)


def attend_kernel(scaling, parts, *refs):
    pair, halo = refs[0], refs[1 : 3 * parts + 3]
    bias, attended, stats, key_all, value_all = refs[3 * parts + 3 :]
    frames, _, tokens, _ = attended.shape
    fill_keys(parts, halo, (key_all, value_all))
    windows = [pl.ds(3 * at * tokens, 9 * tokens) for at in range(frames)]
    scores = [
        dot(slab(pair, at, 0), key_all[windows[at], :], NT) * (scaling * LOG2E) + spread(bias[at], tokens)
        for at in range(frames)
    ]
    highest = [jnp.max(part, axis=1, keepdims=True) for part in scores]
    raised = [jnp.exp2(part - top) for part, top in zip(scores, highest)]
    total = [jnp.sum(part, axis=1, keepdims=True) for part in raised]
    sums = [dot(raised[at].astype(jnp.bfloat16), value_all[windows[at], :], NN) for at in range(frames)]
    for at in range(frames):
        out = (sums[at] * (1.0 / total[at])).astype(jnp.bfloat16)
        grad = slab(pair, at, 1).astype(jnp.float32)
        grad_dot = jnp.sum(grad * out.astype(jnp.float32), axis=1, keepdims=True)
        attended[at, 0] = out
        lane = lax.broadcasted_iota(jnp.int32, (tokens, 128), 1)
        both = jnp.where(lane == 0, highest[at] + jnp.log2(total[at]), grad_dot)
        stats[at, 0] = jnp.transpose(both)[:2]


def store(grads, at, first, second):
    cells = grads[0].shape[-2]
    for part, out in enumerate(grads):
        own = slice(part * cells, (part + 1) * cells)
        out[0, at, 0] = first[own]
        out[1, at, 0] = second[own]


def query_kernel(scaling, parts, *refs):
    pair, halo = refs[0], refs[1 : 3 * parts + 3]
    attended, stats, bias = refs[3 * parts + 3 : 3 * parts + 6]
    grads, (key_all, value_all) = refs[3 * parts + 6 : -2], refs[-2:]
    frames, _, tokens, _ = attended.shape
    fill_keys(parts, halo, (key_all, value_all))
    windows = [pl.ds(3 * at * tokens, 9 * tokens) for at in range(frames)]

    def column(at, which):
        wide = jnp.broadcast_to(stats[at, 0, which : which + 1], (128, tokens))
        return jnp.transpose(wide)[:, :1]

    scores = [dot(slab(pair, at, 0), key_all[windows[at], :], NT) for at in range(frames)]
    grad_probs = [dot(slab(pair, at, 1), value_all[windows[at], :], NT) for at in range(frames)]
    for at in range(frames):
        shift = spread(bias[at], tokens) - column(at, 0)
        weights = jnp.exp2(scores[at] * (scaling * LOG2E) + shift)
        grad_scores = (weights * (grad_probs[at] - column(at, 1))).astype(jnp.bfloat16)
        query_grad = dot(grad_scores, key_all[windows[at], :], NN) * scaling
        store(grads, at, attended[at, 0], query_grad.astype(jnp.bfloat16))


def back_kernel(scaling, parts, *refs):
    pair, halo = list(refs[:parts]), refs[parts : parts + 5]
    own_st, before_st, after_st, low_st, high_st, bias = refs[parts + 5 : parts + 11]
    grads, (query_all, grad_all) = refs[parts + 11 : -2], refs[-2:]
    frames, _, _, tokens = own_st.shape
    fill_queries(halo, (query_all, grad_all))

    def stat_row(at, row, which):
        if at == 0:
            return low_st[row, 0, which : which + 1]
        if at == frames + 1:
            return high_st[row, 0, which : which + 1]
        return (before_st, own_st, after_st)[row][at - 1, 0, which : which + 1]

    def stat_band(at, which):
        rows = [stat_row(at + step, row, which) for step in range(3) for row in range(3)]
        return jnp.concatenate(rows, axis=1)

    windows = [pl.ds(3 * at * tokens, 9 * tokens) for at in range(frames)]
    scores = [dot(slab(pair, at, 0), query_all[windows[at], :], NT) for at in range(frames)]
    grad_probs = [dot(slab(pair, at, 1), grad_all[windows[at], :], NT) for at in range(frames)]
    for at in range(frames):
        shift = spread(bias[at] - stat_band(at, 0), tokens)
        weights = jnp.exp2(scores[at] * (scaling * LOG2E) + shift).astype(jnp.bfloat16)
        grad_scores = weights.astype(jnp.float32) * (grad_probs[at] - stat_band(at, 1))
        key_grad = dot(grad_scores.astype(jnp.bfloat16), query_all[windows[at], :], NN) * scaling
        value_grad = dot(weights, grad_all[windows[at], :], NN)
        store(grads, at, key_grad.astype(jnp.bfloat16), value_grad.astype(jnp.bfloat16))


def head_spec(shape, first):
    dim = len(shape) - 3
    block = shape[:dim] + (1,) + shape[dim + 1 :]
    return pl.BlockSpec(block, lambda head: (0,) * dim + (head + first,) + (0, 0))


def run(kernel, scaling, parts, operands, bias, outs, first, count, products):
    frames, (cells, dim) = bias.shape[0], operands[0].shape[-2:]
    tokens = parts * cells
    return pl.pallas_call(
        functools.partial(kernel, scaling, parts),
        grid=(count,),
        out_shape=tuple(outs),
        in_specs=[head_spec(part.shape, first) for part in operands]
        + [pl.BlockSpec(bias.shape, lambda head: (0,) * bias.ndim)],
        out_specs=tuple(head_spec(out.shape, 0) for out in outs),
        scratch_shapes=[pltpu.VMEM((3 * (frames + 2) * tokens, dim), jnp.bfloat16)] * 2,
        compiler_params=pltpu.CompilerParams(vmem_limit_bytes=32 * 2**20),
        cost_estimate=pl.CostEstimate(
            flops=frames * count * 2 * products * tokens * 9 * tokens * dim,
            bytes_accessed=count * (frames + 2) * 3 * 2 * tokens * dim * 2,
            transcendentals=frames * count * tokens * 9 * tokens,
        ),
    )(*operands, bias)


def step_along(tensor, axis, sign):
    size = lax.axis_size(axis)
    return lax.ppermute(tensor, axis, [(i, i + sign) for i in range(size) if 0 <= i + sign < size])


def turn(tensor, shift):
    size = lax.axis_size("head")
    return lax.ppermute(tensor, "head", [(i, (i + shift) % size) for i in range(size)])


def frame_edges(rows):
    low = step_along(jnp.stack([row[-1] for row in rows]), "frame", 1)
    return low, step_along(jnp.stack([row[0] for row in rows]), "frame", -1)


def row_sides(own):
    return step_along(own, "row", 1), step_along(own, "row", -1)


def tile_biases(active, frames, columns_here, cells):
    size = lax.axis_size("head")
    me = lax.axis_index("head")
    frame_at = lax.axis_index("frame") * frames
    row_at = lax.axis_index("row")
    all_frames, all_rows, count, slots = active.shape
    padded = jnp.pad(active.astype(jnp.float32), ((1, 1), (1, 1), (0, 0), (0, 0)))
    near = lax.dynamic_slice(padded, (frame_at, row_at, 0, 0), (frames + 2, 3, count, slots))
    near = near.reshape(frames + 2, 3, count, 9, 3)
    steps = jnp.arange(3, dtype=jnp.int32) - 1
    frame_ids = frame_at + jnp.arange(frames, dtype=jnp.int32)[:, None] + steps
    frame_in = (frame_ids >= 0) & (frame_ids < all_frames)
    row_in = (row_at + steps >= 0) & (row_at + steps < all_rows)
    inside = (frame_in[:, :, None] & row_in).reshape(frames, 9).astype(jnp.float32)
    ahead = near[1 : 1 + frames, 1] * inside[:, None, :, None]
    pick = np.zeros((frames + 2, 3, 9, frames, 9), np.float32)
    for at in range(frames):
        for offset in range(9):
            pick[at + offset // 3, offset % 3, 8 - offset, at, offset] = 1.0
    behind = jnp.einsum("xyioc,xyofq->fiqc", near, pick)
    part = jnp.arange(size, dtype=jnp.int32)
    tile = ((me + part) % size * columns_here) // TC
    repeat = np.kron(np.eye(9 * size), np.ones((1, cells)))
    spread_out = jnp.asarray(repeat, jnp.bfloat16)
    smalls = []
    for table, sign in ((ahead, 1), (behind, -1)):
        owner = tile[None] == jnp.arange(count, dtype=jnp.int32)[:, None]
        shift = (sign * (tile[None, :] - tile[:, None]))[None] == steps[:, None, None]
        chosen = (owner[:, None, :, None] & shift[None]).astype(jnp.float32)
        smalls.append(jnp.einsum("fioc,icpk->fpok", table, chosen))
    small = jnp.stack(smalls).reshape(2 * frames * size, -1).astype(jnp.bfloat16)

    def expand(held, which):
        allowed = jnp.dot(held, spread_out, preferred_element_type=jnp.float32)
        return jnp.where(allowed > 0.5, 0.0, MASKED).reshape(2, frames, size, -1)[which]

    return small, expand


def hold_kernel(source, out):
    out[...] = source[...]


def hold(source):
    return pl.pallas_call(
        hold_kernel,
        out_shape=jax.ShapeDtypeStruct(source.shape, source.dtype),
        cost_estimate=pl.CostEstimate(flops=3_000_000_000, bytes_accessed=0, transcendentals=0),
    )(source)


def on_device(queries, keys, values, out_grad, active):
    frames, rows, columns_here, heads, dim = queries.shape
    size = lax.axis_size("head")
    me = lax.axis_index("head")
    groups = heads // size
    cells = rows * columns_here
    tokens = cells * size
    scaling = dim ** (-0.5)
    assert rows == TR and TC % columns_here == 0

    def pair_of(first, second, shift):
        start = (me + shift) % size * groups
        picked = [
            lax.dynamic_slice_in_dim(jnp.transpose(t, (0, 3, 1, 2, 4)), start, groups, 1) for t in (first, second)
        ]
        return jnp.stack(picked, 1).reshape(frames, 2, groups, cells, dim)

    def from_heads(blocks):
        whole = jnp.zeros((2, frames, rows, heads, columns_here, dim), jnp.bfloat16)
        for first, grads in blocks:
            for b, piece in enumerate(grads):
                piece = piece if b == 0 else turn(piece, b)
                piece = piece.reshape((2, frames, -1, rows, columns_here, dim)).transpose(0, 1, 3, 2, 4, 5)
                start = (me + size - b) % size * groups + first
                whole = lax.dynamic_update_slice_in_dim(whole, piece, start, 3)
        whole = jnp.transpose(whole, (0, 1, 2, 4, 3, 5))
        return whole[0], whole[1]

    small, expand = tile_biases(active, frames, columns_here, cells)
    mark = hold(small)
    front_bias = expand(mark, 0)
    key_sent = [pair_of(keys, values, shift) for shift in range(1, size)]
    key_moved = [turn(key_sent[size - b - 1], size - b) for b in range(1, size)]
    query_held = [pair_of(queries, out_grad, shift) for shift in range(size)]
    query_held, key_moved = lax.optimization_barrier((query_held, key_moved))
    query_moved = [turn(query_held[size - b], size - b) for b in range(1, size)]
    key_here, front_bias = lax.optimization_barrier((pair_of(keys, values, 0), front_bias))
    key_parts = [key_here] + key_moved
    sides = [row_sides(part) for part in key_parts]
    query_all, sides[0] = lax.optimization_barrier((jnp.stack(query_held[:1] + query_moved), sides[0]))
    key_rows = [row for part, (before, after) in zip(key_parts, sides) for row in (before, part, after)]
    back_bias = expand(mark, 1)
    key_halo = key_parts + [before for before, _ in sides] + [after for _, after in sides]
    key_halo += frame_edges(key_rows)
    query_before, query_after = row_sides(query_all)
    rows_all = [row[b] for b in range(size) for row in (query_before, query_all, query_after)]
    query_halo = [query_all, query_before, query_after] + list(frame_edges(rows_all))

    def grads_shape(count):
        return [jax.ShapeDtypeStruct((2, frames, count, cells, dim), jnp.bfloat16)] * size

    attended_shape = jax.ShapeDtypeStruct((frames, groups, tokens, dim), jnp.bfloat16)
    stat_shape = jax.ShapeDtypeStruct((frames, groups, 2, tokens), jnp.float32)
    attended, stats = run(
        attend_kernel, scaling, size, [query_all] + key_halo, front_bias, [attended_shape, stat_shape], 0, groups, 2
    )
    stat_sides = row_sides(stats)
    attended, stat_sides = lax.optimization_barrier((attended, stat_sides))
    front_grads = run(
        query_kernel, scaling, size, [query_all] + key_halo + [attended, stats], front_bias, grads_shape(groups),
        0, groups, 3
    )
    stat_edges = frame_edges((stat_sides[0], stats, stat_sides[1]))
    front_grads, stat_edges = lax.optimization_barrier((front_grads, stat_edges))
    stat_halo = [stats] + list(stat_sides) + list(stat_edges)
    blocks = []
    for first, count in ((0, groups - groups // 2), (groups - groups // 2, groups // 2)):
        back_grads = run(
            back_kernel, scaling, size, key_parts + query_halo + stat_halo, back_bias, grads_shape(count),
            first, count, 4
        )
        blocks.append((first, back_grads))
    return from_heads([(0, front_grads)]) + from_heads(blocks)


def solution(mesh):
    spec = P("frame", "row", "head", None, None)
    return jax.shard_map(
        on_device, mesh=mesh, in_specs=(spec,) * 4 + (P(),), out_specs=(spec,) * 4, check_vma=False
    )
```

```python
import functools

import jax
import jax.numpy as jnp
import numpy as np
from jax import lax
from jax.experimental import pallas as pl
from jax.experimental.pallas import tpu as pltpu
from jax.sharding import PartitionSpec as P

TF = 1
TR = 8
TC = 8
MASKED = -1e30
LOG2E = 1.4426950408889634
NT = (((1,), (1,)), ((), ()))
NN = (((1,), (0,)), ((), ()))


def dot(left, right, dims):
    return lax.dot_general(left, right, dims, preferred_element_type=jnp.float32)


def spread(bias, tokens):
    parts, width = bias.shape
    return jnp.broadcast_to(bias[:, None], (parts, tokens // parts, width)).reshape(tokens, width)


def fill_bands(frames, parts, cells, side, edge, bands):
    for at in range(frames + 2):
        for row in range(3):
            for part in range(parts):
                place = pl.ds(((3 * at + row) * parts + part) * cells, cells)
                for which, band in enumerate(bands):
                    if at == 0:
                        band[place, :] = edge(0, row, part, which)
                    elif at == frames + 1:
                        band[place, :] = edge(1, row, part, which)
                    else:
                        band[place, :] = side(row, part, at - 1, which)


def fill_keys(parts, halo, bands):
    rows = (halo[parts : 2 * parts], halo[:parts], halo[2 * parts : 3 * parts])
    edges = halo[3 * parts :]
    frames, _, _, cells, _ = halo[0].shape
    side = lambda row, part, at, which: rows[row][part][at, which, 0]
    edge = lambda end, row, part, which: edges[end][3 * part + row, which, 0]
    fill_bands(frames, parts, cells, side, edge, bands)


def fill_queries(halo, bands):
    own, before, after, low, high = halo
    frames, parts, _, _, cells, _ = own.shape
    side = lambda row, part, at, which: (before, own, after)[row][at, part, which, 0]
    edge = lambda end, row, part, which: (low, high)[end][row, part, which, 0]
    fill_bands(frames, parts, cells, side, edge, bands)


def slab(parts, at, which):
    if isinstance(parts, list):
        return jnp.concatenate([part[at, which, 0] for part in parts], axis=0)
    return jnp.concatenate([parts[at, part, which, 0] for part in range(parts.shape[1])], axis=0)


def attend_kernel(scaling, parts, *refs):
    pair, halo = refs[0], refs[1 : 3 * parts + 3]
    bias, attended, stats, key_all, value_all = refs[3 * parts + 3 :]
    frames, _, tokens, _ = attended.shape
    fill_keys(parts, halo, (key_all, value_all))
    windows = [pl.ds(3 * at * tokens, 9 * tokens) for at in range(frames)]
    scores = [
        dot(slab(pair, at, 0), key_all[windows[at], :], NT) * (scaling * LOG2E) + spread(bias[at], tokens)
        for at in range(frames)
    ]
    highest = [jnp.max(part, axis=1, keepdims=True) for part in scores]
    raised = [jnp.exp2(part - top) for part, top in zip(scores, highest)]
    total = [jnp.sum(part, axis=1, keepdims=True) for part in raised]
    sums = [dot(raised[at].astype(jnp.bfloat16), value_all[windows[at], :], NN) for at in range(frames)]
    for at in range(frames):
        out = (sums[at] * (1.0 / total[at])).astype(jnp.bfloat16)
        grad = slab(pair, at, 1).astype(jnp.float32)
        grad_dot = jnp.sum(grad * out.astype(jnp.float32), axis=1, keepdims=True)
        attended[at, 0] = out
        lane = lax.broadcasted_iota(jnp.int32, (tokens, 128), 1)
        both = jnp.where(lane == 0, highest[at] + jnp.log2(total[at]), grad_dot)
        stats[at, 0] = jnp.transpose(both)[:2]


def store(grads, at, first, second):
    cells = grads[0].shape[-2]
    for part, out in enumerate(grads):
        own = slice(part * cells, (part + 1) * cells)
        out[0, at, 0] = first[own]
        out[1, at, 0] = second[own]


def query_kernel(scaling, parts, *refs):
    pair, halo = refs[0], refs[1 : 3 * parts + 3]
    attended, stats, bias = refs[3 * parts + 3 : 3 * parts + 6]
    grads, (key_all, value_all) = refs[3 * parts + 6 : -2], refs[-2:]
    frames, _, tokens, _ = attended.shape
    fill_keys(parts, halo, (key_all, value_all))
    windows = [pl.ds(3 * at * tokens, 9 * tokens) for at in range(frames)]

    def column(at, which):
        wide = jnp.broadcast_to(stats[at, 0, which : which + 1], (128, tokens))
        return jnp.transpose(wide)[:, :1]

    scores = [dot(slab(pair, at, 0), key_all[windows[at], :], NT) for at in range(frames)]
    grad_probs = [dot(slab(pair, at, 1), value_all[windows[at], :], NT) for at in range(frames)]
    for at in range(frames):
        shift = spread(bias[at], tokens) - column(at, 0)
        weights = jnp.exp2(scores[at] * (scaling * LOG2E) + shift)
        grad_scores = (weights * (grad_probs[at] - column(at, 1))).astype(jnp.bfloat16)
        query_grad = dot(grad_scores, key_all[windows[at], :], NN) * scaling
        store(grads, at, attended[at, 0], query_grad.astype(jnp.bfloat16))


def back_kernel(scaling, parts, *refs):
    pair, halo = list(refs[:parts]), refs[parts : parts + 5]
    own_st, before_st, after_st, low_st, high_st, bias = refs[parts + 5 : parts + 11]
    grads, (query_all, grad_all) = refs[parts + 11 : -2], refs[-2:]
    frames, _, _, tokens = own_st.shape
    fill_queries(halo, (query_all, grad_all))

    def stat_row(at, row, which):
        if at == 0:
            return low_st[row, 0, which : which + 1]
        if at == frames + 1:
            return high_st[row, 0, which : which + 1]
        return (before_st, own_st, after_st)[row][at - 1, 0, which : which + 1]

    def stat_band(at, which):
        rows = [stat_row(at + step, row, which) for step in range(3) for row in range(3)]
        return jnp.concatenate(rows, axis=1)

    windows = [pl.ds(3 * at * tokens, 9 * tokens) for at in range(frames)]
    scores = [dot(slab(pair, at, 0), query_all[windows[at], :], NT) for at in range(frames)]
    grad_probs = [dot(slab(pair, at, 1), grad_all[windows[at], :], NT) for at in range(frames)]
    for at in range(frames):
        shift = spread(bias[at] - stat_band(at, 0), tokens)
        weights = jnp.exp2(scores[at] * (scaling * LOG2E) + shift).astype(jnp.bfloat16)
        grad_scores = weights.astype(jnp.float32) * (grad_probs[at] - stat_band(at, 1))
        key_grad = dot(grad_scores.astype(jnp.bfloat16), query_all[windows[at], :], NN) * scaling
        value_grad = dot(weights, grad_all[windows[at], :], NN)
        store(grads, at, key_grad.astype(jnp.bfloat16), value_grad.astype(jnp.bfloat16))


def head_spec(shape, first):
    dim = len(shape) - 3
    block = shape[:dim] + (1,) + shape[dim + 1 :]
    return pl.BlockSpec(block, lambda head: (0,) * dim + (head + first,) + (0, 0))


def run(kernel, scaling, parts, operands, bias, outs, first, count, products):
    frames, (cells, dim) = bias.shape[0], operands[0].shape[-2:]
    tokens = parts * cells
    return pl.pallas_call(
        functools.partial(kernel, scaling, parts),
        grid=(count,),
        out_shape=tuple(outs),
        in_specs=[head_spec(part.shape, first) for part in operands]
        + [pl.BlockSpec(bias.shape, lambda head: (0,) * bias.ndim)],
        out_specs=tuple(head_spec(out.shape, 0) for out in outs),
        scratch_shapes=[pltpu.VMEM((3 * (frames + 2) * tokens, dim), jnp.bfloat16)] * 2,
        compiler_params=pltpu.CompilerParams(vmem_limit_bytes=32 * 2**20),
        cost_estimate=pl.CostEstimate(
            flops=frames * count * 2 * products * tokens * 9 * tokens * dim,
            bytes_accessed=count * (frames + 2) * 3 * 2 * tokens * dim * 2,
            transcendentals=frames * count * tokens * 9 * tokens,
        ),
    )(*operands, bias)


def step_along(tensor, axis, sign):
    size = lax.axis_size(axis)
    return lax.ppermute(tensor, axis, [(i, i + sign) for i in range(size) if 0 <= i + sign < size])


def turn(tensor, shift):
    size = lax.axis_size("head")
    return lax.ppermute(tensor, "head", [(i, (i + shift) % size) for i in range(size)])


def frame_edges(rows):
    low = step_along(jnp.stack([row[-1] for row in rows]), "frame", 1)
    return low, step_along(jnp.stack([row[0] for row in rows]), "frame", -1)


def edges_kernel(before, own, after, first, last, sems):
    copies = []
    for row, source in enumerate((before, own, after)):
        for side, (out, at) in enumerate(((first, 0), (last, source.shape[0] - 1))):
            copies.append(pltpu.make_async_copy(source.at[at], out.at[row], sems.at[row, side]))
    for copy in copies:
        copy.start()
    for copy in copies:
        copy.wait()


def stacked_edges(before, own, after):
    edge = jax.ShapeDtypeStruct((3,) + own.shape[1:], own.dtype)
    anywhere = pl.BlockSpec(memory_space=pl.ANY)
    first, last = pl.pallas_call(
        edges_kernel,
        out_shape=(edge, edge),
        in_specs=[anywhere] * 3,
        out_specs=(anywhere, anywhere),
        scratch_shapes=[pltpu.SemaphoreType.DMA((3, 2))],
        cost_estimate=pl.CostEstimate(flops=0, bytes_accessed=4 * edge.size * 2, transcendentals=0),
    )(before, own, after)
    return step_along(last, "frame", 1), step_along(first, "frame", -1)


def row_sides(own):
    return step_along(own, "row", 1), step_along(own, "row", -1)


def tile_biases(active, frames, columns_here, cells):
    size = lax.axis_size("head")
    me = lax.axis_index("head")
    frame_at = lax.axis_index("frame") * frames
    row_at = lax.axis_index("row")
    all_frames, all_rows, count, slots = active.shape
    padded = jnp.pad(active.astype(jnp.float32), ((1, 1), (1, 1), (0, 0), (0, 0)))
    near = lax.dynamic_slice(padded, (frame_at, row_at, 0, 0), (frames + 2, 3, count, slots))
    near = near.reshape(frames + 2, 3, count, 9, 3)
    steps = jnp.arange(3, dtype=jnp.int32) - 1
    frame_ids = frame_at + jnp.arange(frames, dtype=jnp.int32)[:, None] + steps
    frame_in = (frame_ids >= 0) & (frame_ids < all_frames)
    row_in = (row_at + steps >= 0) & (row_at + steps < all_rows)
    inside = (frame_in[:, :, None] & row_in).reshape(frames, 9).astype(jnp.float32)
    ahead = near[1 : 1 + frames, 1] * inside[:, None, :, None]
    pick = np.zeros((frames + 2, 3, 9, frames, 9), np.float32)
    for at in range(frames):
        for offset in range(9):
            pick[at + offset // 3, offset % 3, 8 - offset, at, offset] = 1.0
    behind = jnp.einsum("xyioc,xyofq->fiqc", near, pick)
    part = jnp.arange(size, dtype=jnp.int32)
    tile = ((me + part) % size * columns_here) // TC
    repeat = np.kron(np.eye(9 * size), np.ones((1, cells)))
    spread_out = jnp.asarray(repeat, jnp.bfloat16)
    smalls = []
    for table, sign in ((ahead, 1), (behind, -1)):
        owner = tile[None] == jnp.arange(count, dtype=jnp.int32)[:, None]
        shift = (sign * (tile[None, :] - tile[:, None]))[None] == steps[:, None, None]
        chosen = (owner[:, None, :, None] & shift[None]).astype(jnp.float32)
        smalls.append(jnp.einsum("fioc,icpk->fpok", table, chosen))
    small = jnp.stack(smalls).reshape(2 * frames * size, -1).astype(jnp.bfloat16)
    allowed = jnp.dot(small, spread_out, preferred_element_type=jnp.float32)
    bias = jnp.where(allowed > 0.5, 0.0, MASKED).reshape(2, frames, size, -1)
    return bias[0], bias[1]


def on_device(queries, keys, values, out_grad, active):
    frames, rows, columns_here, heads, dim = queries.shape
    size = lax.axis_size("head")
    me = lax.axis_index("head")
    groups = heads // size
    cells = rows * columns_here
    tokens = cells * size
    scaling = dim ** (-0.5)
    assert rows == TR and TC % columns_here == 0

    def pair_of(first, second, shift):
        start = (me + shift) % size * groups
        picked = [
            lax.dynamic_slice_in_dim(jnp.transpose(t, (0, 3, 1, 2, 4)), start, groups, 1) for t in (first, second)
        ]
        return jnp.stack(picked, 1).reshape(frames, 2, groups, cells, dim)

    def from_heads(blocks):
        whole = jnp.zeros((2, frames, rows, heads, columns_here, dim), jnp.bfloat16)
        for first, grads in blocks:
            for b, piece in enumerate(grads):
                piece = piece if b == 0 else turn(piece, b)
                piece = piece.reshape((2, frames, -1, rows, columns_here, dim)).transpose(0, 1, 3, 2, 4, 5)
                start = (me + size - b) % size * groups + first
                whole = lax.dynamic_update_slice_in_dim(whole, piece, start, 3)
        whole = jnp.transpose(whole, (0, 1, 2, 4, 3, 5))
        return whole[0], whole[1]

    front_bias, back_bias = tile_biases(active, frames, columns_here, cells)
    key_here = pair_of(keys, values, 0)
    key_near = row_sides(key_here)
    key_sent = [pair_of(keys, values, shift) for shift in range(1, size)]
    key_moved = [turn(key_sent[size - b - 1], size - b) for b in range(1, size)]
    query_held = [pair_of(queries, out_grad, shift) for shift in range(size)]
    query_held, key_moved = lax.optimization_barrier((query_held, key_moved))
    key_far = [row_sides(part) for part in key_moved]
    query_moved = [turn(query_held[size - b], size - b) for b in range(1, size)]
    query_all = jnp.stack(query_held[:1] + query_moved, 1)
    query_all, key_near = lax.optimization_barrier((query_all, key_near))
    query_before, query_after = row_sides(query_all)
    key_parts, sides = [key_here] + key_moved, [key_near] + key_far
    key_halo = key_parts + [before for before, _ in sides] + [after for _, after in sides]
    key_halo += frame_edges([row for part, (up, down) in zip(key_parts, sides) for row in (up, part, down)])
    query_halo = [query_all, query_before, query_after]
    query_halo += stacked_edges(query_before, query_all, query_after)

    def grads_shape(count):
        return [jax.ShapeDtypeStruct((2, frames, count, cells, dim), jnp.bfloat16)] * size

    attended_shape = jax.ShapeDtypeStruct((frames, groups, tokens, dim), jnp.bfloat16)
    stat_shape = jax.ShapeDtypeStruct((frames, groups, 2, tokens), jnp.float32)
    attended, stats = run(
        attend_kernel, scaling, size, [query_all] + key_halo, front_bias, [attended_shape, stat_shape], 0, groups, 2
    )
    front_grads = run(
        query_kernel, scaling, size, [query_all] + key_halo + [attended, stats], front_bias, grads_shape(groups),
        0, groups, 3
    )
    stat_sides = row_sides(stats)
    stat_halo = [stats] + list(stat_sides) + list(frame_edges((stat_sides[0], stats, stat_sides[1])))
    halves = ((0, groups - groups // 2), (groups - groups // 2, groups // 2))
    back_blocks = []
    for first, count in halves:
        back_grads = run(
            back_kernel, scaling, size, key_parts + query_halo + stat_halo, back_bias, grads_shape(count),
            first, count, 4
        )
        back_blocks.append((first, back_grads))
    return from_heads([(0, front_grads)]) + from_heads(back_blocks)


def solution(mesh):
    spec = P("frame", "row", "head", None, None)
    return jax.shard_map(
        on_device, mesh=mesh, in_specs=(spec,) * 4 + (P(),), out_specs=(spec,) * 4, check_vma=False
    )
```

```python
import functools

import jax
import jax.numpy as jnp
import numpy as np
from jax import lax
from jax.experimental import pallas as pl
from jax.experimental.pallas import tpu as pltpu
from jax.sharding import PartitionSpec as P

TF = 1
TR = 8
TC = 8
MASKED = -1e30
LOG2E = 1.4426950408889634
NT = (((1,), (1,)), ((), ()))
NN = (((1,), (0,)), ((), ()))


def dot(left, right, dims):
    return lax.dot_general(left, right, dims, preferred_element_type=jnp.float32)


def spread(bias, tokens):
    parts, width = bias.shape
    return jnp.broadcast_to(bias[:, None], (parts, tokens // parts, width)).reshape(tokens, width)


def fill_bands(frames, parts, cells, side, edge, bands):
    for at in range(frames + 2):
        for row in range(3):
            for part in range(parts):
                place = pl.ds(((3 * at + row) * parts + part) * cells, cells)
                for which, band in enumerate(bands):
                    if at == 0:
                        band[place, :] = edge(0, row, part, which)
                    elif at == frames + 1:
                        band[place, :] = edge(1, row, part, which)
                    else:
                        band[place, :] = side(row, part, at - 1, which)


def fill_keys(parts, halo, bands):
    rows = (halo[parts : 2 * parts], halo[:parts], halo[2 * parts : 3 * parts])
    edges = halo[3 * parts :]
    frames, _, _, cells, _ = halo[0].shape
    side = lambda row, part, at, which: rows[row][part][at, which, 0]
    edge = lambda end, row, part, which: edges[end][3 * part + row, which, 0]
    fill_bands(frames, parts, cells, side, edge, bands)


def fill_queries(halo, bands):
    own, before, after, low, high = halo
    frames, parts, _, _, cells, _ = own.shape
    side = lambda row, part, at, which: (before, own, after)[row][at, part, which, 0]
    edge = lambda end, row, part, which: (low, high)[end][3 * part + row, which, 0]
    fill_bands(frames, parts, cells, side, edge, bands)


def slab(parts, at, which):
    if isinstance(parts, list):
        return jnp.concatenate([part[at, which, 0] for part in parts], axis=0)
    return jnp.concatenate([parts[at, part, which, 0] for part in range(parts.shape[1])], axis=0)


def attend_kernel(scaling, parts, *refs):
    pair, halo = refs[0], refs[1 : 3 * parts + 3]
    bias, attended, stats, key_all, value_all = refs[3 * parts + 3 :]
    frames, _, tokens, _ = attended.shape
    fill_keys(parts, halo, (key_all, value_all))
    windows = [pl.ds(3 * at * tokens, 9 * tokens) for at in range(frames)]
    scores = [
        dot(slab(pair, at, 0), key_all[windows[at], :], NT) * (scaling * LOG2E) + spread(bias[at], tokens)
        for at in range(frames)
    ]
    highest = [jnp.max(part, axis=1, keepdims=True) for part in scores]
    raised = [jnp.exp2(part - top) for part, top in zip(scores, highest)]
    total = [jnp.sum(part, axis=1, keepdims=True) for part in raised]
    sums = [dot(raised[at].astype(jnp.bfloat16), value_all[windows[at], :], NN) for at in range(frames)]
    for at in range(frames):
        out = (sums[at] * (1.0 / total[at])).astype(jnp.bfloat16)
        grad = slab(pair, at, 1).astype(jnp.float32)
        grad_dot = jnp.sum(grad * out.astype(jnp.float32), axis=1, keepdims=True)
        attended[at, 0] = out
        lane = lax.broadcasted_iota(jnp.int32, (tokens, 128), 1)
        both = jnp.where(lane == 0, highest[at] + jnp.log2(total[at]), grad_dot)
        stats[at, 0] = jnp.transpose(both)[:2]


def store(grads, at, first, second):
    cells = grads[0].shape[-2]
    for part, out in enumerate(grads):
        own = slice(part * cells, (part + 1) * cells)
        out[0, at, 0] = first[own]
        out[1, at, 0] = second[own]


def query_kernel(scaling, parts, *refs):
    pair, halo = refs[0], refs[1 : 3 * parts + 3]
    attended, stats, bias = refs[3 * parts + 3 : 3 * parts + 6]
    grads, (key_all, value_all) = refs[3 * parts + 6 : -2], refs[-2:]
    frames, _, tokens, _ = attended.shape
    fill_keys(parts, halo, (key_all, value_all))
    windows = [pl.ds(3 * at * tokens, 9 * tokens) for at in range(frames)]

    def column(at, which):
        wide = jnp.broadcast_to(stats[at, 0, which : which + 1], (128, tokens))
        return jnp.transpose(wide)[:, :1]

    scores = [dot(slab(pair, at, 0), key_all[windows[at], :], NT) for at in range(frames)]
    grad_probs = [dot(slab(pair, at, 1), value_all[windows[at], :], NT) for at in range(frames)]
    for at in range(frames):
        shift = spread(bias[at], tokens) - column(at, 0)
        weights = jnp.exp2(scores[at] * (scaling * LOG2E) + shift)
        grad_scores = (weights * (grad_probs[at] - column(at, 1))).astype(jnp.bfloat16)
        query_grad = dot(grad_scores, key_all[windows[at], :], NN) * scaling
        store(grads, at, attended[at, 0], query_grad.astype(jnp.bfloat16))


def back_kernel(scaling, parts, *refs):
    pair, halo = list(refs[:parts]), refs[parts : parts + 5]
    own_st, before_st, after_st, low_st, high_st, bias = refs[parts + 5 : parts + 11]
    grads, (query_all, grad_all) = refs[parts + 11 : -2], refs[-2:]
    frames, _, _, tokens = own_st.shape
    fill_queries(halo, (query_all, grad_all))

    def stat_row(at, row, which):
        if at == 0:
            return low_st[row, 0, which : which + 1]
        if at == frames + 1:
            return high_st[row, 0, which : which + 1]
        return (before_st, own_st, after_st)[row][at - 1, 0, which : which + 1]

    def stat_band(at, which):
        rows = [stat_row(at + step, row, which) for step in range(3) for row in range(3)]
        return jnp.concatenate(rows, axis=1)

    windows = [pl.ds(3 * at * tokens, 9 * tokens) for at in range(frames)]
    scores = [dot(slab(pair, at, 0), query_all[windows[at], :], NT) for at in range(frames)]
    grad_probs = [dot(slab(pair, at, 1), grad_all[windows[at], :], NT) for at in range(frames)]
    for at in range(frames):
        shift = spread(bias[at] - stat_band(at, 0), tokens)
        weights = jnp.exp2(scores[at] * (scaling * LOG2E) + shift).astype(jnp.bfloat16)
        grad_scores = weights.astype(jnp.float32) * (grad_probs[at] - stat_band(at, 1))
        key_grad = dot(grad_scores.astype(jnp.bfloat16), query_all[windows[at], :], NN) * scaling
        value_grad = dot(weights, grad_all[windows[at], :], NN)
        store(grads, at, key_grad.astype(jnp.bfloat16), value_grad.astype(jnp.bfloat16))


def head_spec(shape, first):
    dim = len(shape) - 3
    block = shape[:dim] + (1,) + shape[dim + 1 :]
    return pl.BlockSpec(block, lambda head: (0,) * dim + (head + first,) + (0, 0))


def run(kernel, scaling, parts, operands, bias, outs, first, count, products):
    frames, (cells, dim) = bias.shape[0], operands[0].shape[-2:]
    tokens = parts * cells
    return pl.pallas_call(
        functools.partial(kernel, scaling, parts),
        grid=(count,),
        out_shape=tuple(outs),
        in_specs=[head_spec(part.shape, first) for part in operands]
        + [pl.BlockSpec(bias.shape, lambda head: (0,) * bias.ndim)],
        out_specs=tuple(head_spec(out.shape, 0) for out in outs),
        scratch_shapes=[pltpu.VMEM((3 * (frames + 2) * tokens, dim), jnp.bfloat16)] * 2,
        compiler_params=pltpu.CompilerParams(vmem_limit_bytes=16 * 2**20),
        cost_estimate=pl.CostEstimate(
            flops=frames * count * 2 * products * tokens * 9 * tokens * dim,
            bytes_accessed=count * (frames + 2) * 3 * 2 * tokens * dim * 2,
            transcendentals=frames * count * tokens * 9 * tokens,
        ),
    )(*operands, bias)


def step_along(tensor, axis, sign):
    size = lax.axis_size(axis)
    return lax.ppermute(tensor, axis, [(i, i + sign) for i in range(size) if 0 <= i + sign < size])


def turn(tensor, shift):
    size = lax.axis_size("head")
    return lax.ppermute(tensor, "head", [(i, (i + shift) % size) for i in range(size)])


def frame_edges(rows):
    low = step_along(jnp.stack([row[-1] for row in rows]), "frame", 1)
    return low, step_along(jnp.stack([row[0] for row in rows]), "frame", -1)


def row_sides(own):
    return step_along(own, "row", 1), step_along(own, "row", -1)


def tile_biases(active, frames, columns_here, cells):
    size = lax.axis_size("head")
    me = lax.axis_index("head")
    frame_at = lax.axis_index("frame") * frames
    row_at = lax.axis_index("row")
    all_frames, all_rows, count, slots = active.shape
    padded = jnp.pad(active.astype(jnp.float32), ((1, 1), (1, 1), (0, 0), (0, 0)))
    near = lax.dynamic_slice(padded, (frame_at, row_at, 0, 0), (frames + 2, 3, count, slots))
    near = near.reshape(frames + 2, 3, count, 9, 3)
    steps = jnp.arange(3, dtype=jnp.int32) - 1
    frame_ids = frame_at + jnp.arange(frames, dtype=jnp.int32)[:, None] + steps
    frame_in = (frame_ids >= 0) & (frame_ids < all_frames)
    row_in = (row_at + steps >= 0) & (row_at + steps < all_rows)
    inside = (frame_in[:, :, None] & row_in).reshape(frames, 9).astype(jnp.float32)
    ahead = near[1 : 1 + frames, 1] * inside[:, None, :, None]
    pick = np.zeros((frames + 2, 3, 9, frames, 9), np.float32)
    for at in range(frames):
        for offset in range(9):
            pick[at + offset // 3, offset % 3, 8 - offset, at, offset] = 1.0
    behind = jnp.einsum("xyioc,xyofq->fiqc", near, pick)
    part = jnp.arange(size, dtype=jnp.int32)
    tile = ((me + part) % size * columns_here) // TC
    repeat = np.kron(np.eye(9 * size), np.ones((1, cells)))
    spread_out = jnp.asarray(repeat, jnp.bfloat16)
    smalls = []
    for table, sign in ((ahead, 1), (behind, -1)):
        owner = tile[None] == jnp.arange(count, dtype=jnp.int32)[:, None]
        shift = (sign * (tile[None, :] - tile[:, None]))[None] == steps[:, None, None]
        chosen = (owner[:, None, :, None] & shift[None]).astype(jnp.float32)
        smalls.append(jnp.einsum("fioc,icpk->fpok", table, chosen))
    small = jnp.stack(smalls).reshape(2 * frames * size, -1).astype(jnp.bfloat16)
    allowed = jnp.dot(small, spread_out, preferred_element_type=jnp.float32)
    bias = jnp.where(allowed > 0.5, 0.0, MASKED).reshape(2, frames, size, -1)
    return bias[0], bias[1]


def on_device(queries, keys, values, out_grad, active):
    frames, rows, columns_here, heads, dim = queries.shape
    size = lax.axis_size("head")
    me = lax.axis_index("head")
    groups = heads // size
    cells = rows * columns_here
    tokens = cells * size
    scaling = dim ** (-0.5)
    assert rows == TR and TC % columns_here == 0

    def pair_of(first, second, shift):
        start = (me + shift) % size * groups
        picked = [
            lax.dynamic_slice_in_dim(jnp.transpose(t, (0, 3, 1, 2, 4)), start, groups, 1) for t in (first, second)
        ]
        return jnp.stack(picked, 1).reshape(frames, 2, groups, cells, dim)

    def from_heads(blocks):
        whole = jnp.zeros((2, frames, rows, heads, columns_here, dim), jnp.bfloat16)
        for first, grads in blocks:
            for b, piece in enumerate(grads):
                piece = piece if b == 0 else turn(piece, b)
                piece = piece.reshape((2, frames, -1, rows, columns_here, dim)).transpose(0, 1, 3, 2, 4, 5)
                start = (me + size - b) % size * groups + first
                whole = lax.dynamic_update_slice_in_dim(whole, piece, start, 3)
        whole = jnp.transpose(whole, (0, 1, 2, 4, 3, 5))
        return whole[0], whole[1]

    front_bias, back_bias = tile_biases(active, frames, columns_here, cells)
    key_here = pair_of(keys, values, 0)
    key_near = row_sides(key_here)
    key_sent = [pair_of(keys, values, shift) for shift in range(1, size)]
    key_moved = [turn(key_sent[size - b - 1], size - b) for b in range(1, size)]
    query_held = [pair_of(queries, out_grad, shift) for shift in range(size)]
    query_held, key_moved = lax.optimization_barrier((query_held, key_moved))
    key_far = [row_sides(part) for part in key_moved]
    query_moved = [turn(query_held[size - b], size - b) for b in range(1, size)]
    query_all = jnp.stack(query_held[:1] + query_moved, 1)
    query_all, key_near = lax.optimization_barrier((query_all, key_near))
    query_before, query_after = row_sides(query_all)
    key_parts, sides = [key_here] + key_moved, [key_near] + key_far
    key_halo = key_parts + [before for before, _ in sides] + [after for _, after in sides]
    key_halo += frame_edges([row for part, (up, down) in zip(key_parts, sides) for row in (up, part, down)])
    query_halo = [query_all, query_before, query_after]
    query_rows = (query_before, query_all, query_after)
    query_halo += frame_edges([row[:, b] for b in range(size) for row in query_rows])

    def grads_shape(count):
        return [jax.ShapeDtypeStruct((2, frames, count, cells, dim), jnp.bfloat16)] * size

    attended_shape = jax.ShapeDtypeStruct((frames, groups, tokens, dim), jnp.bfloat16)
    stat_shape = jax.ShapeDtypeStruct((frames, groups, 2, tokens), jnp.float32)
    attended, stats = run(
        attend_kernel, scaling, size, [query_all] + key_halo, front_bias, [attended_shape, stat_shape], 0, groups, 2
    )
    front_grads = run(
        query_kernel, scaling, size, [query_all] + key_halo + [attended, stats], front_bias, grads_shape(groups),
        0, groups, 3
    )
    stat_sides = row_sides(stats)
    stat_halo = [stats] + list(stat_sides) + list(frame_edges((stat_sides[0], stats, stat_sides[1])))
    halves = ((0, groups - groups // 2), (groups - groups // 2, groups // 2))
    back_blocks = []
    for first, count in halves:
        back_grads = run(
            back_kernel, scaling, size, key_parts + query_halo + stat_halo, back_bias, grads_shape(count),
            first, count, 4
        )
        back_blocks.append((first, back_grads))
    return from_heads([(0, front_grads)]) + from_heads(back_blocks)


def solution(mesh):
    spec = P("frame", "row", "head", None, None)
    return jax.shard_map(
        on_device, mesh=mesh, in_specs=(spec,) * 4 + (P(),), out_specs=(spec,) * 4, check_vma=False
    )
```

```python
import functools

import jax
import jax.numpy as jnp
import numpy as np
from jax import lax
from jax.experimental import pallas as pl
from jax.experimental.pallas import tpu as pltpu
from jax.sharding import PartitionSpec as P

TF = 1
TR = 8
TC = 8
MASKED = -1e30
LOG2E = 1.4426950408889634
NT = (((1,), (1,)), ((), ()))
NN = (((1,), (0,)), ((), ()))


def dot(left, right, dims):
    return lax.dot_general(left, right, dims, preferred_element_type=jnp.float32)


def spread(bias, tokens):
    parts, width = bias.shape
    return jnp.broadcast_to(bias[:, None], (parts, tokens // parts, width)).reshape(tokens, width)


def fill_bands(frames, parts, cells, side, edge, bands):
    for at in range(frames + 2):
        for row in range(3):
            for part in range(parts):
                place = pl.ds(((3 * at + row) * parts + part) * cells, cells)
                for which, band in enumerate(bands):
                    if at == 0:
                        band[place, :] = edge(0, row, part, which)
                    elif at == frames + 1:
                        band[place, :] = edge(1, row, part, which)
                    else:
                        band[place, :] = side(row, part, at - 1, which)


def fill_halo(parts, halo, bands):
    rows = (halo[parts : 2 * parts], halo[:parts], halo[2 * parts : 3 * parts])
    edges = halo[3 * parts :]
    frames, _, _, cells, _ = halo[0].shape
    side = lambda row, part, at, which: rows[row][part][at, which, 0]
    edge = lambda end, row, part, which: edges[end][3 * part + row, which, 0]
    fill_bands(frames, parts, cells, side, edge, bands)


def slab(parts, at, which):
    return jnp.concatenate([part[at, which, 0] for part in parts], axis=0)


def attend_kernel(scaling, parts, *refs):
    pair, halo = refs[:parts], refs[parts : 4 * parts + 2]
    bias, attended, stats, key_all, value_all = refs[4 * parts + 2 :]
    frames, _, tokens, _ = attended.shape
    fill_halo(parts, halo, (key_all, value_all))
    windows = [pl.ds(3 * at * tokens, 9 * tokens) for at in range(frames)]
    scores = [
        dot(slab(pair, at, 0), key_all[windows[at], :], NT) * (scaling * LOG2E) + spread(bias[at], tokens)
        for at in range(frames)
    ]
    highest = [jnp.max(part, axis=1, keepdims=True) for part in scores]
    raised = [jnp.exp2(part - top) for part, top in zip(scores, highest)]
    total = [jnp.sum(part, axis=1, keepdims=True) for part in raised]
    sums = [dot(raised[at].astype(jnp.bfloat16), value_all[windows[at], :], NN) for at in range(frames)]
    for at in range(frames):
        out = (sums[at] * (1.0 / total[at])).astype(jnp.bfloat16)
        grad = slab(pair, at, 1).astype(jnp.float32)
        grad_dot = jnp.sum(grad * out.astype(jnp.float32), axis=1, keepdims=True)
        attended[at, 0] = out
        lane = lax.broadcasted_iota(jnp.int32, (tokens, 128), 1)
        both = jnp.where(lane == 0, highest[at] + jnp.log2(total[at]), grad_dot)
        stats[at, 0] = jnp.transpose(both)[:2]


def store(grads, at, first, second):
    cells = grads[0].shape[-2]
    for part, out in enumerate(grads):
        own = slice(part * cells, (part + 1) * cells)
        out[0, at, 0] = first[own]
        out[1, at, 0] = second[own]


def query_kernel(scaling, parts, *refs):
    pair, halo = refs[:parts], refs[parts : 4 * parts + 2]
    attended, stats, bias = refs[4 * parts + 2 : 4 * parts + 5]
    grads, (key_all, value_all) = refs[4 * parts + 5 : -2], refs[-2:]
    frames, _, tokens, _ = attended.shape
    fill_halo(parts, halo, (key_all, value_all))
    windows = [pl.ds(3 * at * tokens, 9 * tokens) for at in range(frames)]

    def column(at, which):
        wide = jnp.broadcast_to(stats[at, 0, which : which + 1], (128, tokens))
        return jnp.transpose(wide)[:, :1]

    scores = [dot(slab(pair, at, 0), key_all[windows[at], :], NT) for at in range(frames)]
    grad_probs = [dot(slab(pair, at, 1), value_all[windows[at], :], NT) for at in range(frames)]
    for at in range(frames):
        shift = spread(bias[at], tokens) - column(at, 0)
        weights = jnp.exp2(scores[at] * (scaling * LOG2E) + shift)
        grad_scores = (weights * (grad_probs[at] - column(at, 1))).astype(jnp.bfloat16)
        query_grad = dot(grad_scores, key_all[windows[at], :], NN) * scaling
        store(grads, at, attended[at, 0], query_grad.astype(jnp.bfloat16))


def back_kernel(scaling, parts, *refs):
    pair, halo = refs[:parts], refs[parts : 4 * parts + 2]
    own_st, before_st, after_st, low_st, high_st, bias = refs[4 * parts + 2 : 4 * parts + 8]
    grads, (query_all, grad_all) = refs[4 * parts + 8 : -2], refs[-2:]
    frames, _, _, tokens = own_st.shape
    fill_halo(parts, halo, (query_all, grad_all))

    def stat_row(at, row, which):
        if at == 0:
            return low_st[row, 0, which : which + 1]
        if at == frames + 1:
            return high_st[row, 0, which : which + 1]
        return (before_st, own_st, after_st)[row][at - 1, 0, which : which + 1]

    def stat_band(at, which):
        rows = [stat_row(at + step, row, which) for step in range(3) for row in range(3)]
        return jnp.concatenate(rows, axis=1)

    windows = [pl.ds(3 * at * tokens, 9 * tokens) for at in range(frames)]
    scores = [dot(slab(pair, at, 0), query_all[windows[at], :], NT) for at in range(frames)]
    grad_probs = [dot(slab(pair, at, 1), grad_all[windows[at], :], NT) for at in range(frames)]
    for at in range(frames):
        shift = spread(bias[at] - stat_band(at, 0), tokens)
        weights = jnp.exp2(scores[at] * (scaling * LOG2E) + shift).astype(jnp.bfloat16)
        grad_scores = weights.astype(jnp.float32) * (grad_probs[at] - stat_band(at, 1))
        key_grad = dot(grad_scores.astype(jnp.bfloat16), query_all[windows[at], :], NN) * scaling
        value_grad = dot(weights, grad_all[windows[at], :], NN)
        store(grads, at, key_grad.astype(jnp.bfloat16), value_grad.astype(jnp.bfloat16))


def head_spec(shape, first, half=0):
    dim = len(shape) - 3
    if dim == 2 and shape[1] == 4:
        block = (shape[0], 2, 1) + shape[3:]
        return pl.BlockSpec(block, lambda head: (0, half, head + first, 0, 0))
    block = shape[:dim] + (1,) + shape[dim + 1 :]
    return pl.BlockSpec(block, lambda head: (0,) * dim + (head + first,) + (0, 0))


def run(kernel, scaling, parts, operands, bias, outs, first, count, products):
    frames, (cells, dim) = bias.shape[0], operands[0][0].shape[-2:]
    operands = [part if isinstance(part, tuple) else (part, 0) for part in operands]
    tokens = parts * cells
    return pl.pallas_call(
        functools.partial(kernel, scaling, parts),
        grid=(count,),
        out_shape=tuple(outs),
        in_specs=[head_spec(part.shape, first, half) for part, half in operands]
        + [pl.BlockSpec(bias.shape, lambda head: (0,) * bias.ndim)],
        out_specs=tuple(head_spec(out.shape, 0) for out in outs),
        scratch_shapes=[pltpu.VMEM((3 * (frames + 2) * tokens, dim), jnp.bfloat16)] * 2,
        compiler_params=pltpu.CompilerParams(vmem_limit_bytes=16 * 2**20),
        cost_estimate=pl.CostEstimate(
            flops=frames * count * 2 * products * tokens * 9 * tokens * dim,
            bytes_accessed=count * (frames + 2) * 3 * 2 * tokens * dim * 2,
            transcendentals=frames * count * tokens * 9 * tokens,
        ),
    )(*[part for part, _ in operands], bias)


def step_along(tensor, axis, sign):
    size = lax.axis_size(axis)
    return lax.ppermute(tensor, axis, [(i, i + sign) for i in range(size) if 0 <= i + sign < size])


def turn(tensor, shift):
    size = lax.axis_size("head")
    return lax.ppermute(tensor, "head", [(i, (i + shift) % size) for i in range(size)])


def frame_edges(rows):
    low = step_along(jnp.stack([row[-1] for row in rows]), "frame", 1)
    return low, step_along(jnp.stack([row[0] for row in rows]), "frame", -1)


def row_sides(own):
    return step_along(own, "row", 1), step_along(own, "row", -1)


def tile_biases(active, frames, columns_here, cells):
    size = lax.axis_size("head")
    me = lax.axis_index("head")
    frame_at = lax.axis_index("frame") * frames
    row_at = lax.axis_index("row")
    all_frames, all_rows, count, slots = active.shape
    padded = jnp.pad(active.astype(jnp.float32), ((1, 1), (1, 1), (0, 0), (0, 0)))
    near = lax.dynamic_slice(padded, (frame_at, row_at, 0, 0), (frames + 2, 3, count, slots))
    near = near.reshape(frames + 2, 3, count, 9, 3)
    steps = jnp.arange(3, dtype=jnp.int32) - 1
    frame_ids = frame_at + jnp.arange(frames, dtype=jnp.int32)[:, None] + steps
    frame_in = (frame_ids >= 0) & (frame_ids < all_frames)
    row_in = (row_at + steps >= 0) & (row_at + steps < all_rows)
    inside = (frame_in[:, :, None] & row_in).reshape(frames, 9).astype(jnp.float32)
    ahead = near[1 : 1 + frames, 1] * inside[:, None, :, None]
    pick = np.zeros((frames + 2, 3, 9, frames, 9), np.float32)
    for at in range(frames):
        for offset in range(9):
            pick[at + offset // 3, offset % 3, 8 - offset, at, offset] = 1.0
    behind = jnp.einsum("xyioc,xyofq->fiqc", near, pick)
    part = jnp.arange(size, dtype=jnp.int32)
    tile = ((me + part) % size * columns_here) // TC
    repeat = np.kron(np.eye(9 * size), np.ones((1, cells)))
    spread_out = jnp.asarray(repeat, jnp.bfloat16)
    smalls = []
    for table, sign in ((ahead, 1), (behind, -1)):
        owner = tile[None] == jnp.arange(count, dtype=jnp.int32)[:, None]
        shift = (sign * (tile[None, :] - tile[:, None]))[None] == steps[:, None, None]
        chosen = (owner[:, None, :, None] & shift[None]).astype(jnp.float32)
        smalls.append(jnp.einsum("fioc,icpk->fpok", table, chosen))
    small = jnp.stack(smalls).reshape(2 * frames * size, -1).astype(jnp.bfloat16)
    allowed = jnp.dot(small, spread_out, preferred_element_type=jnp.float32)
    bias = jnp.where(allowed > 0.5, 0.0, MASKED).reshape(2, frames, size, -1)
    return bias[0], bias[1]


def on_device(queries, keys, values, out_grad, active):
    frames, rows, columns_here, heads, dim = queries.shape
    size = lax.axis_size("head")
    me = lax.axis_index("head")
    groups = heads // size
    cells = rows * columns_here
    tokens = cells * size
    scaling = dim ** (-0.5)
    assert rows == TR and TC % columns_here == 0

    def group_of(tensors, shift):
        start = (me + shift) % size * groups
        picked = [lax.dynamic_slice_in_dim(jnp.transpose(t, (0, 3, 1, 2, 4)), start, groups, 1) for t in tensors]
        return jnp.stack(picked, 1).reshape(frames, len(tensors), groups, cells, dim)

    def from_heads(blocks):
        whole = jnp.zeros((2, frames, rows, heads, columns_here, dim), jnp.bfloat16)
        for first, grads in blocks:
            for b, piece in enumerate(grads):
                piece = piece if b == 0 else turn(piece, b)
                piece = piece.reshape((2, frames, -1, rows, columns_here, dim)).transpose(0, 1, 3, 2, 4, 5)
                start = (me + size - b) % size * groups + first
                whole = lax.dynamic_update_slice_in_dim(whole, piece, start, 3)
        whole = jnp.transpose(whole, (0, 1, 2, 4, 3, 5))
        return whole[0], whole[1]

    front_bias, back_bias = tile_biases(active, frames, columns_here, cells)

    here = group_of((keys, values, queries, out_grad), 0)
    near = row_sides(here)
    key_sent = [group_of((keys, values), shift) for shift in range(1, size)]
    key_moved = [turn(key_sent[size - b - 1], size - b) for b in range(1, size)]
    query_sent = [group_of((queries, out_grad), shift) for shift in range(1, size)]
    query_sent, key_moved = lax.optimization_barrier((query_sent, key_moved))
    query_moved = [turn(query_sent[size - b - 1], size - b) for b in range(1, size)]

    def halo_of(moved, half):
        sides = [near] + [row_sides(part) for part in moved]
        rows = [[side[at] for side in sides] for at in range(2)]
        rows.insert(1, [here] + moved)
        cut = [[part[:, 2 * half : 2 * half + 2] if at == 0 else part for at, part in enumerate(row)] for row in rows]
        edges = frame_edges([row[part] for part in range(size) for row in cut])
        marked = [[(part, half if at == 0 else 0) for at, part in enumerate(row)] for row in rows]
        return marked[1], marked[1] + marked[0] + marked[2] + [(edge, 0) for edge in edges]

    key_parts, key_halo = halo_of(key_moved, 0)
    query_parts, query_halo = halo_of(query_moved, 1)

    def grads_shape(count):
        return [jax.ShapeDtypeStruct((2, frames, count, cells, dim), jnp.bfloat16)] * size

    attended_shape = jax.ShapeDtypeStruct((frames, groups, tokens, dim), jnp.bfloat16)
    stat_shape = jax.ShapeDtypeStruct((frames, groups, 2, tokens), jnp.float32)
    attended, stats = run(
        attend_kernel, scaling, size, query_parts + key_halo, front_bias, [attended_shape, stat_shape], 0, groups, 2
    )
    front_grads = run(
        query_kernel, scaling, size, query_parts + key_halo + [attended, stats], front_bias, grads_shape(groups),
        0, groups, 3
    )
    stat_sides = row_sides(stats)
    stat_halo = [stats] + list(stat_sides) + list(frame_edges((stat_sides[0], stats, stat_sides[1])))
    halves = ((0, groups - groups // 2), (groups - groups // 2, groups // 2))
    back_blocks = []
    for first, count in halves:
        back_grads = run(
            back_kernel, scaling, size, key_parts + query_halo + stat_halo, back_bias, grads_shape(count),
            first, count, 4
        )
        back_blocks.append((first, back_grads))
    return from_heads([(0, front_grads)]) + from_heads(back_blocks)


def solution(mesh):
    spec = P("frame", "row", "head", None, None)
    return jax.shard_map(
        on_device, mesh=mesh, in_specs=(spec,) * 4 + (P(),), out_specs=(spec,) * 4, check_vma=False
    )
```

```python
import functools

import jax
import jax.numpy as jnp
import numpy as np
from jax import lax
from jax.experimental import pallas as pl
from jax.experimental.pallas import tpu as pltpu
from jax.sharding import PartitionSpec as P

TF = 1
TR = 8
TC = 8
MASKED = -1e30
LOG2E = 1.4426950408889634
NT = (((1,), (1,)), ((), ()))
NN = (((1,), (0,)), ((), ()))


def dot(left, right, dims):
    return lax.dot_general(left, right, dims, preferred_element_type=jnp.float32)


def spread(bias, tokens):
    parts, width = bias.shape
    return jnp.broadcast_to(bias[:, None], (parts, tokens // parts, width)).reshape(tokens, width)


def fill_bands(frames, parts, cells, side, edge, bands):
    for at in range(frames + 2):
        for row in range(3):
            for part in range(parts):
                place = pl.ds(((3 * at + row) * parts + part) * cells, cells)
                for which, band in enumerate(bands):
                    if at == 0:
                        band[place, :] = edge(0, row, part, which)
                    elif at == frames + 1:
                        band[place, :] = edge(1, row, part, which)
                    else:
                        band[place, :] = side(row, part, at - 1, which)


def fill_keys(parts, halo, bands):
    rows = (halo[parts : 2 * parts], halo[:parts], halo[2 * parts : 3 * parts])
    edges = halo[3 * parts :]
    frames, _, _, cells, _ = halo[0].shape
    side = lambda row, part, at, which: rows[row][part][at, which, 0]
    edge = lambda end, row, part, which: edges[end][3 * part + row, which, 0]
    fill_bands(frames, parts, cells, side, edge, bands)


def fill_queries(halo, bands):
    own, before, after, low, high = halo
    frames, parts, _, _, cells, _ = own.shape
    side = lambda row, part, at, which: (before, own, after)[row][at, part, which, 0]
    edge = lambda end, row, part, which: (low, high)[end][3 * part + row, which, 0]
    fill_bands(frames, parts, cells, side, edge, bands)


def slab(parts, at, which):
    if isinstance(parts, list):
        return jnp.concatenate([part[at, which, 0] for part in parts], axis=0)
    return jnp.concatenate([parts[at, part, which, 0] for part in range(parts.shape[1])], axis=0)


def attend_kernel(scaling, parts, *refs):
    pair, halo = refs[0], refs[1 : 3 * parts + 3]
    bias, attended, stats, key_all, value_all = refs[3 * parts + 3 :]
    frames, _, tokens, _ = attended.shape
    fill_keys(parts, halo, (key_all, value_all))
    windows = [pl.ds(3 * at * tokens, 9 * tokens) for at in range(frames)]
    scores = [
        dot(slab(pair, at, 0), key_all[windows[at], :], NT) * (scaling * LOG2E) + spread(bias[at], tokens)
        for at in range(frames)
    ]
    highest = [jnp.max(part, axis=1, keepdims=True) for part in scores]
    raised = [jnp.exp2(part - top) for part, top in zip(scores, highest)]
    total = [jnp.sum(part, axis=1, keepdims=True) for part in raised]
    sums = [dot(raised[at].astype(jnp.bfloat16), value_all[windows[at], :], NN) for at in range(frames)]
    for at in range(frames):
        out = (sums[at] * (1.0 / total[at])).astype(jnp.bfloat16)
        grad = slab(pair, at, 1).astype(jnp.float32)
        grad_dot = jnp.sum(grad * out.astype(jnp.float32), axis=1, keepdims=True)
        attended[at, 0] = out
        lane = lax.broadcasted_iota(jnp.int32, (tokens, 128), 1)
        both = jnp.where(lane == 0, highest[at] + jnp.log2(total[at]), grad_dot)
        stats[at, 0] = jnp.transpose(both)[:2]


def store(grads, at, first, second):
    cells = grads[0].shape[-2]
    for part, out in enumerate(grads):
        own = slice(part * cells, (part + 1) * cells)
        out[0, at, 0] = first[own]
        out[1, at, 0] = second[own]


def query_kernel(scaling, parts, *refs):
    pair, halo = refs[0], refs[1 : 3 * parts + 3]
    attended, stats, bias = refs[3 * parts + 3 : 3 * parts + 6]
    grads, (key_all, value_all) = refs[3 * parts + 6 : -2], refs[-2:]
    frames, _, tokens, _ = attended.shape
    fill_keys(parts, halo, (key_all, value_all))
    windows = [pl.ds(3 * at * tokens, 9 * tokens) for at in range(frames)]

    def column(at, which):
        wide = jnp.broadcast_to(stats[at, 0, which : which + 1], (128, tokens))
        return jnp.transpose(wide)[:, :1]

    scores = [dot(slab(pair, at, 0), key_all[windows[at], :], NT) for at in range(frames)]
    grad_probs = [dot(slab(pair, at, 1), value_all[windows[at], :], NT) for at in range(frames)]
    for at in range(frames):
        shift = spread(bias[at], tokens) - column(at, 0)
        weights = jnp.exp2(scores[at] * (scaling * LOG2E) + shift)
        grad_scores = (weights * (grad_probs[at] - column(at, 1))).astype(jnp.bfloat16)
        query_grad = dot(grad_scores, key_all[windows[at], :], NN) * scaling
        store(grads, at, attended[at, 0], query_grad.astype(jnp.bfloat16))


def back_kernel(scaling, parts, *refs):
    pair, halo = list(refs[:parts]), refs[parts : parts + 5]
    own_st, before_st, after_st, low_st, high_st, bias = refs[parts + 5 : parts + 11]
    grads, (query_all, grad_all) = refs[parts + 11 : -2], refs[-2:]
    frames, _, _, tokens = own_st.shape
    fill_queries(halo, (query_all, grad_all))

    def stat_row(at, row, which):
        if at == 0:
            return low_st[row, 0, which : which + 1]
        if at == frames + 1:
            return high_st[row, 0, which : which + 1]
        return (before_st, own_st, after_st)[row][at - 1, 0, which : which + 1]

    def stat_band(at, which):
        rows = [stat_row(at + step, row, which) for step in range(3) for row in range(3)]
        return jnp.concatenate(rows, axis=1)

    windows = [pl.ds(3 * at * tokens, 9 * tokens) for at in range(frames)]
    scores = [dot(slab(pair, at, 0), query_all[windows[at], :], NT) for at in range(frames)]
    grad_probs = [dot(slab(pair, at, 1), grad_all[windows[at], :], NT) for at in range(frames)]
    for at in range(frames):
        shift = spread(bias[at] - stat_band(at, 0), tokens)
        weights = jnp.exp2(scores[at] * (scaling * LOG2E) + shift).astype(jnp.bfloat16)
        grad_scores = weights.astype(jnp.float32) * (grad_probs[at] - stat_band(at, 1))
        key_grad = dot(grad_scores.astype(jnp.bfloat16), query_all[windows[at], :], NN) * scaling
        value_grad = dot(weights, grad_all[windows[at], :], NN)
        store(grads, at, key_grad.astype(jnp.bfloat16), value_grad.astype(jnp.bfloat16))


def head_spec(shape, first):
    dim = len(shape) - 3
    block = shape[:dim] + (1,) + shape[dim + 1 :]
    return pl.BlockSpec(block, lambda head: (0,) * dim + (head + first,) + (0, 0))


def run(kernel, scaling, parts, operands, bias, outs, first, count, products):
    frames, (cells, dim) = bias.shape[0], operands[0].shape[-2:]
    tokens = parts * cells
    return pl.pallas_call(
        functools.partial(kernel, scaling, parts),
        grid=(count,),
        out_shape=tuple(outs),
        in_specs=[head_spec(part.shape, first) for part in operands]
        + [pl.BlockSpec(bias.shape, lambda head: (0,) * bias.ndim)],
        out_specs=tuple(head_spec(out.shape, 0) for out in outs),
        scratch_shapes=[pltpu.VMEM((3 * (frames + 2) * tokens, dim), jnp.bfloat16)] * 2,
        compiler_params=pltpu.CompilerParams(vmem_limit_bytes=16 * 2**20),
        cost_estimate=pl.CostEstimate(
            flops=7 * frames * count * 2 * products * tokens * 9 * tokens * dim,
            bytes_accessed=count * (frames + 2) * 3 * 2 * tokens * dim * 2,
            transcendentals=frames * count * tokens * 9 * tokens,
        ),
    )(*operands, bias)


def step_along(tensor, axis, sign):
    size = lax.axis_size(axis)
    return lax.ppermute(tensor, axis, [(i, i + sign) for i in range(size) if 0 <= i + sign < size])


def turn(tensor, shift):
    size = lax.axis_size("head")
    return lax.ppermute(tensor, "head", [(i, (i + shift) % size) for i in range(size)])


def frame_edges(rows):
    low = step_along(jnp.stack([row[-1] for row in rows]), "frame", 1)
    return low, step_along(jnp.stack([row[0] for row in rows]), "frame", -1)


def row_sides(own):
    return step_along(own, "row", 1), step_along(own, "row", -1)


def tile_biases(active, frames, columns_here, cells):
    size = lax.axis_size("head")
    me = lax.axis_index("head")
    frame_at = lax.axis_index("frame") * frames
    row_at = lax.axis_index("row")
    all_frames, all_rows, count, slots = active.shape
    padded = jnp.pad(active.astype(jnp.float32), ((1, 1), (1, 1), (0, 0), (0, 0)))
    near = lax.dynamic_slice(padded, (frame_at, row_at, 0, 0), (frames + 2, 3, count, slots))
    near = near.reshape(frames + 2, 3, count, 9, 3)
    steps = jnp.arange(3, dtype=jnp.int32) - 1
    frame_ids = frame_at + jnp.arange(frames, dtype=jnp.int32)[:, None] + steps
    frame_in = (frame_ids >= 0) & (frame_ids < all_frames)
    row_in = (row_at + steps >= 0) & (row_at + steps < all_rows)
    inside = (frame_in[:, :, None] & row_in).reshape(frames, 9).astype(jnp.float32)
    ahead = near[1 : 1 + frames, 1] * inside[:, None, :, None]
    pick = np.zeros((frames + 2, 3, 9, frames, 9), np.float32)
    for at in range(frames):
        for offset in range(9):
            pick[at + offset // 3, offset % 3, 8 - offset, at, offset] = 1.0
    behind = jnp.einsum("xyioc,xyofq->fiqc", near, pick)
    part = jnp.arange(size, dtype=jnp.int32)
    tile = ((me + part) % size * columns_here) // TC
    repeat = np.kron(np.eye(9 * size), np.ones((1, cells)))
    spread_out = jnp.asarray(repeat, jnp.bfloat16)
    smalls = []
    for table, sign in ((ahead, 1), (behind, -1)):
        owner = tile[None] == jnp.arange(count, dtype=jnp.int32)[:, None]
        shift = (sign * (tile[None, :] - tile[:, None]))[None] == steps[:, None, None]
        chosen = (owner[:, None, :, None] & shift[None]).astype(jnp.float32)
        smalls.append(jnp.einsum("fioc,icpk->fpok", table, chosen))
    small = jnp.stack(smalls).reshape(2 * frames * size, -1).astype(jnp.bfloat16)
    allowed = jnp.dot(small, spread_out, preferred_element_type=jnp.float32)
    bias = jnp.where(allowed > 0.5, 0.0, MASKED).reshape(2, frames, size, -1)
    return bias[0], bias[1]


def on_device(queries, keys, values, out_grad, active):
    frames, rows, columns_here, heads, dim = queries.shape
    size = lax.axis_size("head")
    me = lax.axis_index("head")
    groups = heads // size
    cells = rows * columns_here
    tokens = cells * size
    scaling = dim ** (-0.5)
    assert rows == TR and TC % columns_here == 0

    def pair_of(first, second, shift):
        start = (me + shift) % size * groups
        picked = [
            lax.dynamic_slice_in_dim(jnp.transpose(t, (0, 3, 1, 2, 4)), start, groups, 1) for t in (first, second)
        ]
        return jnp.stack(picked, 1).reshape(frames, 2, groups, cells, dim)

    def from_heads(blocks):
        whole = jnp.zeros((2, frames, rows, heads, columns_here, dim), jnp.bfloat16)
        for first, grads in blocks:
            for b, piece in enumerate(grads):
                piece = piece if b == 0 else turn(piece, b)
                piece = piece.reshape((2, frames, -1, rows, columns_here, dim)).transpose(0, 1, 3, 2, 4, 5)
                start = (me + size - b) % size * groups + first
                whole = lax.dynamic_update_slice_in_dim(whole, piece, start, 3)
        whole = jnp.transpose(whole, (0, 1, 2, 4, 3, 5))
        return whole[0], whole[1]

    front_bias, back_bias = tile_biases(active, frames, columns_here, cells)
    key_here, front_bias = lax.optimization_barrier((pair_of(keys, values, 0), front_bias))
    key_near = row_sides(key_here)
    key_sent = [pair_of(keys, values, shift) for shift in range(1, size)]
    key_moved = [turn(key_sent[size - b - 1], size - b) for b in range(1, size)]
    query_held = [pair_of(queries, out_grad, shift) for shift in range(size)]
    key_far = [row_sides(part) for part in key_moved]
    query_held, key_moved, key_near = lax.optimization_barrier((query_held, key_moved, key_near))
    query_moved = [turn(query_held[size - b], size - b) for b in range(1, size)]
    query_all = jnp.stack(query_held[:1] + query_moved, 1)
    query_all, key_near = lax.optimization_barrier((query_all, key_near))
    query_before, query_after = row_sides(query_all)
    key_parts, sides = [key_here] + key_moved, [key_near] + key_far
    key_halo = key_parts + [before for before, _ in sides] + [after for _, after in sides]
    key_halo += frame_edges([row for part, (up, down) in zip(key_parts, sides) for row in (up, part, down)])
    query_halo = [query_all, query_before, query_after]
    query_rows = (query_before, query_all, query_after)
    query_halo += frame_edges([row[:, b] for b in range(size) for row in query_rows])

    def grads_shape(count):
        return [jax.ShapeDtypeStruct((2, frames, count, cells, dim), jnp.bfloat16)] * size

    attended_shape = jax.ShapeDtypeStruct((frames, groups, tokens, dim), jnp.bfloat16)
    stat_shape = jax.ShapeDtypeStruct((frames, groups, 2, tokens), jnp.float32)
    attended, stats = run(
        attend_kernel, scaling, size, [query_all] + key_halo, front_bias, [attended_shape, stat_shape], 0, groups, 2
    )
    front_grads = run(
        query_kernel, scaling, size, [query_all] + key_halo + [attended, stats], front_bias, grads_shape(groups),
        0, groups, 3
    )
    stat_sides = row_sides(stats)
    stat_halo = [stats] + list(stat_sides) + list(frame_edges((stat_sides[0], stats, stat_sides[1])))
    halves = ((0, groups - groups // 2), (groups - groups // 2, groups // 2))
    back_blocks = []
    for first, count in halves:
        back_grads = run(
            back_kernel, scaling, size, key_parts + query_halo + stat_halo, back_bias, grads_shape(count),
            first, count, 4
        )
        back_blocks.append((first, back_grads))
    return from_heads([(0, front_grads)]) + from_heads(back_blocks)


def solution(mesh):
    spec = P("frame", "row", "head", None, None)
    return jax.shard_map(
        on_device, mesh=mesh, in_specs=(spec,) * 4 + (P(),), out_specs=(spec,) * 4, check_vma=False
    )
```

```python
import functools

import jax
import jax.numpy as jnp
import numpy as np
from jax import lax
from jax.experimental import pallas as pl
from jax.experimental.pallas import tpu as pltpu
from jax.sharding import PartitionSpec as P

TF = 1
TR = 8
TC = 8
MASKED = -1e30
LOG2E = 1.4426950408889634
NT = (((1,), (1,)), ((), ()))
NN = (((1,), (0,)), ((), ()))


def dot(left, right, dims):
    return lax.dot_general(left, right, dims, preferred_element_type=jnp.float32)


def spread(bias, tokens):
    parts, width = bias.shape
    return jnp.broadcast_to(bias[:, None], (parts, tokens // parts, width)).reshape(tokens, width)


def fill_bands(frames, parts, cells, side, edge, bands):
    for at in range(frames + 2):
        for row in range(3):
            for part in range(parts):
                place = pl.ds(((3 * at + row) * parts + part) * cells, cells)
                for which, band in enumerate(bands):
                    if at == 0:
                        band[place, :] = edge(0, row, part, which)
                    elif at == frames + 1:
                        band[place, :] = edge(1, row, part, which)
                    else:
                        band[place, :] = side(row, part, at - 1, which)


def fill_keys(parts, halo, bands):
    rows = (halo[parts : 2 * parts], halo[:parts], halo[2 * parts : 3 * parts])
    edges = halo[3 * parts :]
    frames, _, _, cells, _ = halo[0].shape
    side = lambda row, part, at, which: rows[row][part][at, which, 0]
    edge = lambda end, row, part, which: edges[end][3 * part + row, which, 0]
    fill_bands(frames, parts, cells, side, edge, bands)


def fill_queries(halo, bands):
    own, before, after, low, high = halo
    frames, parts, _, _, cells, _ = own.shape
    side = lambda row, part, at, which: (before, own, after)[row][at, part, which, 0]
    edge = lambda end, row, part, which: (low, high)[end][3 * part + row, which, 0]
    fill_bands(frames, parts, cells, side, edge, bands)


def slab(parts, at, which):
    if isinstance(parts, list):
        return jnp.concatenate([part[at, which, 0] for part in parts], axis=0)
    return jnp.concatenate([parts[at, part, which, 0] for part in range(parts.shape[1])], axis=0)


def attend_kernel(scaling, parts, *refs):
    pair, halo = refs[0], refs[1 : 3 * parts + 3]
    bias, attended, stats, key_all, value_all = refs[3 * parts + 3 :]
    frames, _, tokens, _ = attended.shape
    fill_keys(parts, halo, (key_all, value_all))
    windows = [pl.ds(3 * at * tokens, 9 * tokens) for at in range(frames)]
    scores = [
        dot(slab(pair, at, 0), key_all[windows[at], :], NT) * (scaling * LOG2E) + spread(bias[at], tokens)
        for at in range(frames)
    ]
    highest = [jnp.max(part, axis=1, keepdims=True) for part in scores]
    raised = [jnp.exp2(part - top) for part, top in zip(scores, highest)]
    total = [jnp.sum(part, axis=1, keepdims=True) for part in raised]
    sums = [dot(raised[at].astype(jnp.bfloat16), value_all[windows[at], :], NN) for at in range(frames)]
    for at in range(frames):
        out = (sums[at] * (1.0 / total[at])).astype(jnp.bfloat16)
        grad = slab(pair, at, 1).astype(jnp.float32)
        grad_dot = jnp.sum(grad * out.astype(jnp.float32), axis=1, keepdims=True)
        attended[at, 0] = out
        lane = lax.broadcasted_iota(jnp.int32, (tokens, 128), 1)
        both = jnp.where(lane == 0, highest[at] + jnp.log2(total[at]), grad_dot)
        stats[at, 0] = jnp.transpose(both)[:2]


def store(grads, at, first, second):
    cells = grads[0].shape[-2]
    for part, out in enumerate(grads):
        own = slice(part * cells, (part + 1) * cells)
        out[0, at, 0] = first[own]
        out[1, at, 0] = second[own]


def query_kernel(scaling, parts, *refs):
    pair, halo = refs[0], refs[1 : 3 * parts + 3]
    attended, stats, bias = refs[3 * parts + 3 : 3 * parts + 6]
    grads, (key_all, value_all) = refs[3 * parts + 6 : -2], refs[-2:]
    frames, _, tokens, _ = attended.shape
    fill_keys(parts, halo, (key_all, value_all))
    windows = [pl.ds(3 * at * tokens, 9 * tokens) for at in range(frames)]

    def column(at, which):
        wide = jnp.broadcast_to(stats[at, 0, which : which + 1], (128, tokens))
        return jnp.transpose(wide)[:, :1]

    scores = [dot(slab(pair, at, 0), key_all[windows[at], :], NT) for at in range(frames)]
    grad_probs = [dot(slab(pair, at, 1), value_all[windows[at], :], NT) for at in range(frames)]
    for at in range(frames):
        shift = spread(bias[at], tokens) - column(at, 0)
        weights = jnp.exp2(scores[at] * (scaling * LOG2E) + shift)
        grad_scores = (weights * (grad_probs[at] - column(at, 1))).astype(jnp.bfloat16)
        query_grad = dot(grad_scores, key_all[windows[at], :], NN) * scaling
        store(grads, at, attended[at, 0], query_grad.astype(jnp.bfloat16))


def back_kernel(scaling, parts, *refs):
    pair, halo = list(refs[:parts]), refs[parts : parts + 5]
    own_st, before_st, after_st, low_st, high_st, bias = refs[parts + 5 : parts + 11]
    grads, (query_all, grad_all) = refs[parts + 11 : -2], refs[-2:]
    frames, _, _, tokens = own_st.shape
    fill_queries(halo, (query_all, grad_all))

    def stat_row(at, row, which):
        if at == 0:
            return low_st[row, 0, which : which + 1]
        if at == frames + 1:
            return high_st[row, 0, which : which + 1]
        return (before_st, own_st, after_st)[row][at - 1, 0, which : which + 1]

    def stat_band(at, which):
        rows = [stat_row(at + step, row, which) for step in range(3) for row in range(3)]
        return jnp.concatenate(rows, axis=1)

    windows = [pl.ds(3 * at * tokens, 9 * tokens) for at in range(frames)]
    scores = [dot(slab(pair, at, 0), query_all[windows[at], :], NT) for at in range(frames)]
    grad_probs = [dot(slab(pair, at, 1), grad_all[windows[at], :], NT) for at in range(frames)]
    for at in range(frames):
        shift = spread(bias[at] - stat_band(at, 0), tokens)
        weights = jnp.exp2(scores[at] * (scaling * LOG2E) + shift).astype(jnp.bfloat16)
        grad_scores = weights.astype(jnp.float32) * (grad_probs[at] - stat_band(at, 1))
        key_grad = dot(grad_scores.astype(jnp.bfloat16), query_all[windows[at], :], NN) * scaling
        value_grad = dot(weights, grad_all[windows[at], :], NN)
        store(grads, at, key_grad.astype(jnp.bfloat16), value_grad.astype(jnp.bfloat16))


def head_spec(shape, first):
    dim = len(shape) - 3
    block = shape[:dim] + (1,) + shape[dim + 1 :]
    return pl.BlockSpec(block, lambda head: (0,) * dim + (head + first,) + (0, 0))


def run(kernel, scaling, parts, operands, bias, outs, first, count, products):
    frames, (cells, dim) = bias.shape[0], operands[0].shape[-2:]
    tokens = parts * cells
    return pl.pallas_call(
        functools.partial(kernel, scaling, parts),
        grid=(count,),
        out_shape=tuple(outs),
        in_specs=[head_spec(part.shape, first) for part in operands]
        + [pl.BlockSpec(bias.shape, lambda head: (0,) * bias.ndim)],
        out_specs=tuple(head_spec(out.shape, 0) for out in outs),
        scratch_shapes=[pltpu.VMEM((3 * (frames + 2) * tokens, dim), jnp.bfloat16)] * 2,
        compiler_params=pltpu.CompilerParams(vmem_limit_bytes=16 * 2**20),
        cost_estimate=pl.CostEstimate(
            flops=7 * frames * count * 2 * products * tokens * 9 * tokens * dim,
            bytes_accessed=count * (frames + 2) * 3 * 2 * tokens * dim * 2,
            transcendentals=frames * count * tokens * 9 * tokens,
        ),
    )(*operands, bias)


def step_along(tensor, axis, sign):
    size = lax.axis_size(axis)
    return lax.ppermute(tensor, axis, [(i, i + sign) for i in range(size) if 0 <= i + sign < size])


def turn(tensor, shift):
    size = lax.axis_size("head")
    return lax.ppermute(tensor, "head", [(i, (i + shift) % size) for i in range(size)])


def frame_edges(rows):
    low = step_along(jnp.stack([row[-1] for row in rows]), "frame", 1)
    return low, step_along(jnp.stack([row[0] for row in rows]), "frame", -1)


def row_sides(own):
    return step_along(own, "row", 1), step_along(own, "row", -1)


def tile_biases(active, frames, columns_here, cells):
    size = lax.axis_size("head")
    me = lax.axis_index("head")
    frame_at = lax.axis_index("frame") * frames
    row_at = lax.axis_index("row")
    all_frames, all_rows, count, slots = active.shape
    padded = jnp.pad(active.astype(jnp.float32), ((1, 1), (1, 1), (0, 0), (0, 0)))
    near = lax.dynamic_slice(padded, (frame_at, row_at, 0, 0), (frames + 2, 3, count, slots))
    near = near.reshape(frames + 2, 3, count, 9, 3)
    steps = jnp.arange(3, dtype=jnp.int32) - 1
    frame_ids = frame_at + jnp.arange(frames, dtype=jnp.int32)[:, None] + steps
    frame_in = (frame_ids >= 0) & (frame_ids < all_frames)
    row_in = (row_at + steps >= 0) & (row_at + steps < all_rows)
    inside = (frame_in[:, :, None] & row_in).reshape(frames, 9).astype(jnp.float32)
    ahead = near[1 : 1 + frames, 1] * inside[:, None, :, None]
    pick = np.zeros((frames + 2, 3, 9, frames, 9), np.float32)
    for at in range(frames):
        for offset in range(9):
            pick[at + offset // 3, offset % 3, 8 - offset, at, offset] = 1.0
    behind = jnp.einsum("xyioc,xyofq->fiqc", near, pick)
    part = jnp.arange(size, dtype=jnp.int32)
    tile = ((me + part) % size * columns_here) // TC
    repeat = np.kron(np.eye(9 * size), np.ones((1, cells)))
    spread_out = jnp.asarray(repeat, jnp.bfloat16)
    smalls = []
    for table, sign in ((ahead, 1), (behind, -1)):
        owner = tile[None] == jnp.arange(count, dtype=jnp.int32)[:, None]
        shift = (sign * (tile[None, :] - tile[:, None]))[None] == steps[:, None, None]
        chosen = (owner[:, None, :, None] & shift[None]).astype(jnp.float32)
        smalls.append(jnp.einsum("fioc,icpk->fpok", table, chosen))
    small = jnp.stack(smalls).reshape(2 * frames * size, -1).astype(jnp.bfloat16)
    allowed = jnp.dot(small, spread_out, preferred_element_type=jnp.float32)
    bias = jnp.where(allowed > 0.5, 0.0, MASKED).reshape(2, frames, size, -1)
    return bias[0], bias[1]


def on_device(queries, keys, values, out_grad, active):
    frames, rows, columns_here, heads, dim = queries.shape
    size = lax.axis_size("head")
    me = lax.axis_index("head")
    groups = heads // size
    cells = rows * columns_here
    tokens = cells * size
    scaling = dim ** (-0.5)
    assert rows == TR and TC % columns_here == 0

    def pair_of(first, second, shift):
        start = (me + shift) % size * groups
        picked = [
            lax.dynamic_slice_in_dim(jnp.transpose(t, (0, 3, 1, 2, 4)), start, groups, 1) for t in (first, second)
        ]
        return jnp.stack(picked, 1).reshape(frames, 2, groups, cells, dim)

    def move(blocks):
        return [
            (first, [piece if b == 0 else turn(piece, b) for b, piece in enumerate(grads)]) for first, grads in blocks
        ]

    def assemble(blocks):
        whole = jnp.zeros((2, frames, rows, heads, columns_here, dim), jnp.bfloat16)
        for first, pieces in blocks:
            for b, piece in enumerate(pieces):
                piece = piece.reshape((2, frames, -1, rows, columns_here, dim)).transpose(0, 1, 3, 2, 4, 5)
                start = (me + size - b) % size * groups + first
                whole = lax.dynamic_update_slice_in_dim(whole, piece, start, 3)
        whole = jnp.transpose(whole, (0, 1, 2, 4, 3, 5))
        return whole[0], whole[1]

    front_bias, back_bias = tile_biases(active, frames, columns_here, cells)
    key_here = pair_of(keys, values, 0)
    key_near = row_sides(key_here)
    key_sent = [pair_of(keys, values, shift) for shift in range(1, size)]
    key_moved = [turn(key_sent[size - b - 1], size - b) for b in range(1, size)]
    query_held = [pair_of(queries, out_grad, shift) for shift in range(size)]
    query_held, key_moved = lax.optimization_barrier((query_held, key_moved))
    key_far = [row_sides(part) for part in key_moved]
    query_moved = [turn(query_held[size - b], size - b) for b in range(1, size)]
    query_all = jnp.stack(query_held[:1] + query_moved, 1)
    query_all, key_near = lax.optimization_barrier((query_all, key_near))
    query_before, query_after = row_sides(query_all)
    key_parts, sides = [key_here] + key_moved, [key_near] + key_far
    key_halo = key_parts + [before for before, _ in sides] + [after for _, after in sides]
    key_halo += frame_edges([row for part, (up, down) in zip(key_parts, sides) for row in (up, part, down)])
    query_halo = [query_all, query_before, query_after]
    query_rows = (query_before, query_all, query_after)
    query_halo += frame_edges([row[:, b] for b in range(size) for row in query_rows])

    def grads_shape(count):
        return [jax.ShapeDtypeStruct((2, frames, count, cells, dim), jnp.bfloat16)] * size

    attended_shape = jax.ShapeDtypeStruct((frames, groups, tokens, dim), jnp.bfloat16)
    stat_shape = jax.ShapeDtypeStruct((frames, groups, 2, tokens), jnp.float32)
    attended, stats = run(
        attend_kernel, scaling, size, [query_all] + key_halo, front_bias, [attended_shape, stat_shape], 0, groups, 2
    )
    halves = ((0, groups - groups // 2), (groups - groups // 2, groups // 2))
    stat_sides = row_sides(stats)
    front_blocks, shown = [], stats
    for first, count in halves:
        front_grads = run(
            query_kernel, scaling, size, [query_all] + key_halo + [attended, shown], front_bias,
            grads_shape(count), first, count, 3
        )
        front_blocks.append((first, front_grads))
        shown, stat_sides = lax.optimization_barrier((shown, stat_sides))
    stat_halo = [stats] + list(stat_sides) + list(frame_edges((stat_sides[0], stats, stat_sides[1])))
    front_blocks = move(front_blocks)
    back_blocks = []
    for first, count in halves:
        back_grads = run(
            back_kernel, scaling, size, key_parts + query_halo + stat_halo, back_bias, grads_shape(count),
            first, count, 4
        )
        back_bias, back_grads = lax.optimization_barrier((back_bias, back_grads))
        back_blocks.append((first, back_grads))
    back_blocks = move(back_blocks)
    first, pieces = back_blocks[0]
    front_blocks, pieces[-1] = lax.optimization_barrier((front_blocks, pieces[-1]))
    return assemble(front_blocks) + assemble(back_blocks)


def solution(mesh):
    spec = P("frame", "row", "head", None, None)
    return jax.shard_map(
        on_device, mesh=mesh, in_specs=(spec,) * 4 + (P(),), out_specs=(spec,) * 4, check_vma=False
    )
```

```python
import functools

import jax
import jax.numpy as jnp
import numpy as np
from jax import lax
from jax.experimental import pallas as pl
from jax.experimental.pallas import tpu as pltpu
from jax.sharding import PartitionSpec as P

TF = 1
TR = 8
TC = 8
MASKED = -1e30
LOG2E = 1.4426950408889634
NT = (((1,), (1,)), ((), ()))
NN = (((1,), (0,)), ((), ()))


def dot(left, right, dims):
    return lax.dot_general(left, right, dims, preferred_element_type=jnp.float32)


def spread(bias, tokens):
    parts, width = bias.shape
    return jnp.broadcast_to(bias[:, None], (parts, tokens // parts, width)).reshape(tokens, width)


def fill_bands(frames, parts, cells, side, edge, bands):
    for at in range(frames + 2):
        for row in range(3):
            for part in range(parts):
                place = pl.ds(((3 * at + row) * parts + part) * cells, cells)
                for which, band in enumerate(bands):
                    if at == 0:
                        band[place, :] = edge(0, row, part, which)
                    elif at == frames + 1:
                        band[place, :] = edge(1, row, part, which)
                    else:
                        band[place, :] = side(row, part, at - 1, which)


def fill_keys(parts, halo, bands):
    rows = (halo[parts : 2 * parts], halo[:parts], halo[2 * parts : 3 * parts])
    edges = halo[3 * parts :]
    frames, _, _, cells, _ = halo[0].shape
    side = lambda row, part, at, which: rows[row][part][at, which, 0]
    edge = lambda end, row, part, which: edges[end][3 * part + row, which, 0]
    fill_bands(frames, parts, cells, side, edge, bands)


def fill_queries(halo, bands):
    own, before, after, low, high = halo
    frames, parts, _, _, cells, _ = own.shape
    side = lambda row, part, at, which: (before, own, after)[row][at, part, which, 0]
    edge = lambda end, row, part, which: (low, high)[end][3 * part + row, which, 0]
    fill_bands(frames, parts, cells, side, edge, bands)


def slab(parts, at, which):
    if isinstance(parts, list):
        return jnp.concatenate([part[at, which, 0] for part in parts], axis=0)
    return jnp.concatenate([parts[at, part, which, 0] for part in range(parts.shape[1])], axis=0)


def attend_kernel(scaling, parts, *refs):
    pair, halo = refs[0], refs[1 : 3 * parts + 3]
    bias, attended, stats, key_all, value_all = refs[3 * parts + 3 :]
    frames, _, tokens, _ = attended.shape
    fill_keys(parts, halo, (key_all, value_all))
    windows = [pl.ds(3 * at * tokens, 9 * tokens) for at in range(frames)]
    scores = [
        dot(slab(pair, at, 0), key_all[windows[at], :], NT) * (scaling * LOG2E) + spread(bias[at], tokens)
        for at in range(frames)
    ]
    highest = [jnp.max(part, axis=1, keepdims=True) for part in scores]
    raised = [jnp.exp2(part - top) for part, top in zip(scores, highest)]
    total = [jnp.sum(part, axis=1, keepdims=True) for part in raised]
    sums = [dot(raised[at].astype(jnp.bfloat16), value_all[windows[at], :], NN) for at in range(frames)]
    for at in range(frames):
        out = (sums[at] * (1.0 / total[at])).astype(jnp.bfloat16)
        grad = slab(pair, at, 1).astype(jnp.float32)
        grad_dot = jnp.sum(grad * out.astype(jnp.float32), axis=1, keepdims=True)
        attended[at, 0] = out
        lane = lax.broadcasted_iota(jnp.int32, (tokens, 128), 1)
        both = jnp.where(lane == 0, highest[at] + jnp.log2(total[at]), grad_dot)
        stats[at, 0] = jnp.transpose(both)[:2]


def store(grads, at, first, second):
    cells = grads[0].shape[-2]
    for part, out in enumerate(grads):
        own = slice(part * cells, (part + 1) * cells)
        out[0, at, 0] = first[own]
        out[1, at, 0] = second[own]


def query_kernel(scaling, parts, *refs):
    pair, halo = refs[0], refs[1 : 3 * parts + 3]
    attended, stats, bias = refs[3 * parts + 3 : 3 * parts + 6]
    grads, (key_all, value_all) = refs[3 * parts + 6 : -2], refs[-2:]
    frames, _, tokens, _ = attended.shape
    fill_keys(parts, halo, (key_all, value_all))
    windows = [pl.ds(3 * at * tokens, 9 * tokens) for at in range(frames)]

    def column(at, which):
        wide = jnp.broadcast_to(stats[at, 0, which : which + 1], (128, tokens))
        return jnp.transpose(wide)[:, :1]

    scores = [dot(slab(pair, at, 0), key_all[windows[at], :], NT) for at in range(frames)]
    grad_probs = [dot(slab(pair, at, 1), value_all[windows[at], :], NT) for at in range(frames)]
    for at in range(frames):
        shift = spread(bias[at], tokens) - column(at, 0)
        weights = jnp.exp2(scores[at] * (scaling * LOG2E) + shift)
        grad_scores = (weights * (grad_probs[at] - column(at, 1))).astype(jnp.bfloat16)
        query_grad = dot(grad_scores, key_all[windows[at], :], NN) * scaling
        store(grads, at, attended[at, 0], query_grad.astype(jnp.bfloat16))


def back_kernel(scaling, parts, *refs):
    pair, halo = list(refs[:parts]), refs[parts : parts + 5]
    own_st, before_st, after_st, low_st, high_st, bias = refs[parts + 5 : parts + 11]
    grads, (query_all, grad_all) = refs[parts + 11 : -2], refs[-2:]
    frames, _, _, tokens = own_st.shape
    fill_queries(halo, (query_all, grad_all))

    def stat_row(at, row, which):
        if at == 0:
            return low_st[row, 0, which : which + 1]
        if at == frames + 1:
            return high_st[row, 0, which : which + 1]
        return (before_st, own_st, after_st)[row][at - 1, 0, which : which + 1]

    def stat_band(at, which):
        rows = [stat_row(at + step, row, which) for step in range(3) for row in range(3)]
        return jnp.concatenate(rows, axis=1)

    windows = [pl.ds(3 * at * tokens, 9 * tokens) for at in range(frames)]
    scores = [dot(slab(pair, at, 0), query_all[windows[at], :], NT) for at in range(frames)]
    grad_probs = [dot(slab(pair, at, 1), grad_all[windows[at], :], NT) for at in range(frames)]
    for at in range(frames):
        shift = spread(bias[at] - stat_band(at, 0), tokens)
        weights = jnp.exp2(scores[at] * (scaling * LOG2E) + shift).astype(jnp.bfloat16)
        grad_scores = weights.astype(jnp.float32) * (grad_probs[at] - stat_band(at, 1))
        key_grad = dot(grad_scores.astype(jnp.bfloat16), query_all[windows[at], :], NN) * scaling
        value_grad = dot(weights, grad_all[windows[at], :], NN)
        store(grads, at, key_grad.astype(jnp.bfloat16), value_grad.astype(jnp.bfloat16))


def head_spec(shape, first):
    dim = len(shape) - 3
    block = shape[:dim] + (1,) + shape[dim + 1 :]
    return pl.BlockSpec(block, lambda head: (0,) * dim + (head + first,) + (0, 0))


def run(kernel, scaling, parts, operands, bias, outs, first, count, products):
    frames, (cells, dim) = bias.shape[0], operands[0].shape[-2:]
    tokens = parts * cells
    return pl.pallas_call(
        functools.partial(kernel, scaling, parts),
        grid=(count,),
        out_shape=tuple(outs),
        in_specs=[head_spec(part.shape, first) for part in operands]
        + [pl.BlockSpec(bias.shape, lambda head: (0,) * bias.ndim)],
        out_specs=tuple(head_spec(out.shape, 0) for out in outs),
        scratch_shapes=[pltpu.VMEM((3 * (frames + 2) * tokens, dim), jnp.bfloat16)] * 2,
        compiler_params=pltpu.CompilerParams(vmem_limit_bytes=16 * 2**20),
        cost_estimate=pl.CostEstimate(
            flops=7 * frames * count * 2 * products * tokens * 9 * tokens * dim,
            bytes_accessed=count * (frames + 2) * 3 * 2 * tokens * dim * 2,
            transcendentals=frames * count * tokens * 9 * tokens,
        ),
    )(*operands, bias)


def step_along(tensor, axis, sign):
    size = lax.axis_size(axis)
    return lax.ppermute(tensor, axis, [(i, i + sign) for i in range(size) if 0 <= i + sign < size])


def turn(tensor, shift):
    size = lax.axis_size("head")
    return lax.ppermute(tensor, "head", [(i, (i + shift) % size) for i in range(size)])


def frame_edges(rows):
    low = step_along(jnp.stack([row[-1] for row in rows]), "frame", 1)
    return low, step_along(jnp.stack([row[0] for row in rows]), "frame", -1)


def row_sides(own):
    return step_along(own, "row", 1), step_along(own, "row", -1)


def tile_biases(active, frames, columns_here, cells):
    size = lax.axis_size("head")
    me = lax.axis_index("head")
    frame_at = lax.axis_index("frame") * frames
    row_at = lax.axis_index("row")
    all_frames, all_rows, count, slots = active.shape
    padded = jnp.pad(active.astype(jnp.float32), ((1, 1), (1, 1), (0, 0), (0, 0)))
    near = lax.dynamic_slice(padded, (frame_at, row_at, 0, 0), (frames + 2, 3, count, slots))
    near = near.reshape(frames + 2, 3, count, 9, 3)
    steps = jnp.arange(3, dtype=jnp.int32) - 1
    frame_ids = frame_at + jnp.arange(frames, dtype=jnp.int32)[:, None] + steps
    frame_in = (frame_ids >= 0) & (frame_ids < all_frames)
    row_in = (row_at + steps >= 0) & (row_at + steps < all_rows)
    inside = (frame_in[:, :, None] & row_in).reshape(frames, 9).astype(jnp.float32)
    ahead = near[1 : 1 + frames, 1] * inside[:, None, :, None]
    pick = np.zeros((frames + 2, 3, 9, frames, 9), np.float32)
    for at in range(frames):
        for offset in range(9):
            pick[at + offset // 3, offset % 3, 8 - offset, at, offset] = 1.0
    behind = jnp.einsum("xyioc,xyofq->fiqc", near, pick)
    part = jnp.arange(size, dtype=jnp.int32)
    tile = ((me + part) % size * columns_here) // TC
    repeat = np.kron(np.eye(9 * size), np.ones((1, cells)))
    spread_out = jnp.asarray(repeat, jnp.bfloat16)
    smalls = []
    for table, sign in ((ahead, 1), (behind, -1)):
        owner = tile[None] == jnp.arange(count, dtype=jnp.int32)[:, None]
        shift = (sign * (tile[None, :] - tile[:, None]))[None] == steps[:, None, None]
        chosen = (owner[:, None, :, None] & shift[None]).astype(jnp.float32)
        smalls.append(jnp.einsum("fioc,icpk->fpok", table, chosen))
    small = jnp.stack(smalls).reshape(2 * frames * size, -1).astype(jnp.bfloat16)
    allowed = jnp.dot(small, spread_out, preferred_element_type=jnp.float32)
    bias = jnp.where(allowed > 0.5, 0.0, MASKED).reshape(2, frames, size, -1)
    return bias[0], bias[1]


def on_device(queries, keys, values, out_grad, active):
    frames, rows, columns_here, heads, dim = queries.shape
    size = lax.axis_size("head")
    me = lax.axis_index("head")
    groups = heads // size
    cells = rows * columns_here
    tokens = cells * size
    scaling = dim ** (-0.5)
    assert rows == TR and TC % columns_here == 0

    def pair_of(first, second, shift):
        start = (me + shift) % size * groups
        picked = [
            lax.dynamic_slice_in_dim(jnp.transpose(t, (0, 3, 1, 2, 4)), start, groups, 1) for t in (first, second)
        ]
        return jnp.stack(picked, 1).reshape(frames, 2, groups, cells, dim)

    def move(blocks):
        return [
            (first, [piece if b == 0 else turn(piece, b) for b, piece in enumerate(grads)]) for first, grads in blocks
        ]

    def assemble(blocks):
        whole = jnp.zeros((2, frames, rows, heads, columns_here, dim), jnp.bfloat16)
        for first, pieces in blocks:
            for b, piece in enumerate(pieces):
                piece = piece.reshape((2, frames, -1, rows, columns_here, dim)).transpose(0, 1, 3, 2, 4, 5)
                start = (me + size - b) % size * groups + first
                whole = lax.dynamic_update_slice_in_dim(whole, piece, start, 3)
        whole = jnp.transpose(whole, (0, 1, 2, 4, 3, 5))
        return whole[0], whole[1]

    front_bias, back_bias = tile_biases(active, frames, columns_here, cells)
    key_here, front_bias = lax.optimization_barrier((pair_of(keys, values, 0), front_bias))
    key_near = row_sides(key_here)
    key_sent = [pair_of(keys, values, shift) for shift in range(1, size)]
    key_moved = [turn(key_sent[size - b - 1], size - b) for b in range(1, size)]
    query_held = [pair_of(queries, out_grad, shift) for shift in range(size)]
    query_held, key_moved = lax.optimization_barrier((query_held, key_moved))
    key_far = [row_sides(part) for part in key_moved]
    query_moved = [turn(query_held[size - b], size - b) for b in range(1, size)]
    query_all = jnp.stack(query_held[:1] + query_moved, 1)
    query_before, query_after = row_sides(query_all)
    key_parts, sides = [key_here] + key_moved, [key_near] + key_far
    key_halo = key_parts + [before for before, _ in sides] + [after for _, after in sides]
    key_halo += frame_edges([row for part, (up, down) in zip(key_parts, sides) for row in (up, part, down)])
    query_halo = [query_all, query_before, query_after]
    query_rows = (query_before, query_all, query_after)
    query_halo += frame_edges([row[:, b] for b in range(size) for row in query_rows])

    def grads_shape(count):
        return [jax.ShapeDtypeStruct((2, frames, count, cells, dim), jnp.bfloat16)] * size

    attended_shape = jax.ShapeDtypeStruct((frames, groups, tokens, dim), jnp.bfloat16)
    stat_shape = jax.ShapeDtypeStruct((frames, groups, 2, tokens), jnp.float32)
    attended, stats = run(
        attend_kernel, scaling, size, [query_all] + key_halo, front_bias, [attended_shape, stat_shape], 0, groups, 2
    )
    halves = ((0, groups - groups // 2), (groups - groups // 2, groups // 2))
    stat_sides = row_sides(stats)
    front_blocks, shown = [], stats
    for first, count in halves:
        front_grads = run(
            query_kernel, scaling, size, [query_all] + key_halo + [attended, shown], front_bias,
            grads_shape(count), first, count, 3
        )
        front_blocks.append((first, front_grads))
        shown, stat_sides = lax.optimization_barrier((shown, stat_sides))
    stat_halo = [stats] + list(stat_sides) + list(frame_edges((stat_sides[0], stats, stat_sides[1])))
    front_blocks = move(front_blocks)
    back_blocks = []
    for first, count in halves:
        back_grads = run(
            back_kernel, scaling, size, key_parts + query_halo + stat_halo, back_bias, grads_shape(count),
            first, count, 4
        )
        back_bias, back_grads = lax.optimization_barrier((back_bias, back_grads))
        back_blocks.append((first, back_grads))
    back_blocks = move(back_blocks)
    first, pieces = back_blocks[0]
    front_blocks, pieces[-1] = lax.optimization_barrier((front_blocks, pieces[-1]))
    return assemble(front_blocks) + assemble(back_blocks)


def solution(mesh):
    spec = P("frame", "row", "head", None, None)
    return jax.shard_map(
        on_device, mesh=mesh, in_specs=(spec,) * 4 + (P(),), out_specs=(spec,) * 4, check_vma=False
    )
```

```python
import functools

import jax
import jax.numpy as jnp
import numpy as np
from jax import lax
from jax.experimental import pallas as pl
from jax.experimental.pallas import tpu as pltpu
from jax.sharding import PartitionSpec as P

TF = 1
TR = 8
TC = 8
MASKED = -1e30
LOG2E = 1.4426950408889634
NT = (((1,), (1,)), ((), ()))
NN = (((1,), (0,)), ((), ()))


def dot(left, right, dims):
    return lax.dot_general(left, right, dims, preferred_element_type=jnp.float32)


def spread(bias, tokens):
    parts, width = bias.shape
    return jnp.broadcast_to(bias[:, None], (parts, tokens // parts, width)).reshape(tokens, width)


def fill_bands(frames, parts, cells, side, edge, bands):
    for at in range(frames + 2):
        for row in range(3):
            for part in range(parts):
                place = pl.ds(((3 * at + row) * parts + part) * cells, cells)
                for which, band in enumerate(bands):
                    if at == 0:
                        band[place, :] = edge(0, row, part, which)
                    elif at == frames + 1:
                        band[place, :] = edge(1, row, part, which)
                    else:
                        band[place, :] = side(row, part, at - 1, which)


def fill_keys(parts, halo, bands):
    rows = (halo[parts : 2 * parts], halo[:parts], halo[2 * parts : 3 * parts])
    edges = halo[3 * parts :]
    frames, _, _, cells, _ = halo[0].shape
    side = lambda row, part, at, which: rows[row][part][at, which, 0]
    edge = lambda end, row, part, which: edges[end][3 * part + row, which, 0]
    fill_bands(frames, parts, cells, side, edge, bands)


def fill_queries(halo, bands):
    own, before, after, low, high = halo
    frames, parts, _, _, cells, _ = own.shape
    side = lambda row, part, at, which: (before, own, after)[row][at, part, which, 0]
    edge = lambda end, row, part, which: (low, high)[end][3 * part + row, which, 0]
    fill_bands(frames, parts, cells, side, edge, bands)


def slab(parts, at, which):
    if isinstance(parts, list):
        return jnp.concatenate([part[at, which, 0] for part in parts], axis=0)
    return jnp.concatenate([parts[at, part, which, 0] for part in range(parts.shape[1])], axis=0)


def attend_kernel(scaling, parts, *refs):
    pair, halo = refs[0], refs[1 : 3 * parts + 3]
    bias, attended, stats, key_all, value_all = refs[3 * parts + 3 :]
    frames, _, tokens, _ = attended.shape
    fill_keys(parts, halo, (key_all, value_all))
    windows = [pl.ds(3 * at * tokens, 9 * tokens) for at in range(frames)]
    scores = [
        dot(slab(pair, at, 0), key_all[windows[at], :], NT) * (scaling * LOG2E) + spread(bias[at], tokens)
        for at in range(frames)
    ]
    highest = [jnp.max(part, axis=1, keepdims=True) for part in scores]
    raised = [jnp.exp2(part - top) for part, top in zip(scores, highest)]
    total = [jnp.sum(part, axis=1, keepdims=True) for part in raised]
    sums = [dot(raised[at].astype(jnp.bfloat16), value_all[windows[at], :], NN) for at in range(frames)]
    for at in range(frames):
        out = (sums[at] * (1.0 / total[at])).astype(jnp.bfloat16)
        grad = slab(pair, at, 1).astype(jnp.float32)
        grad_dot = jnp.sum(grad * out.astype(jnp.float32), axis=1, keepdims=True)
        attended[at, 0] = out
        lane = lax.broadcasted_iota(jnp.int32, (tokens, 128), 1)
        both = jnp.where(lane == 0, highest[at] + jnp.log2(total[at]), grad_dot)
        stats[at, 0] = jnp.transpose(both)[:2]


def store(grads, at, first, second):
    cells = grads[0].shape[-2]
    for part, out in enumerate(grads):
        own = slice(part * cells, (part + 1) * cells)
        out[0, at, 0] = first[own]
        out[1, at, 0] = second[own]


def query_kernel(scaling, parts, *refs):
    pair, halo = refs[0], refs[1 : 3 * parts + 3]
    attended, stats, bias = refs[3 * parts + 3 : 3 * parts + 6]
    grads, (key_all, value_all) = refs[3 * parts + 6 : -2], refs[-2:]
    frames, _, tokens, _ = attended.shape
    fill_keys(parts, halo, (key_all, value_all))
    windows = [pl.ds(3 * at * tokens, 9 * tokens) for at in range(frames)]

    def column(at, which):
        wide = jnp.broadcast_to(stats[at, 0, which : which + 1], (128, tokens))
        return jnp.transpose(wide)[:, :1]

    scores = [dot(slab(pair, at, 0), key_all[windows[at], :], NT) for at in range(frames)]
    grad_probs = [dot(slab(pair, at, 1), value_all[windows[at], :], NT) for at in range(frames)]
    for at in range(frames):
        shift = spread(bias[at], tokens) - column(at, 0)
        weights = jnp.exp2(scores[at] * (scaling * LOG2E) + shift)
        grad_scores = (weights * (grad_probs[at] - column(at, 1))).astype(jnp.bfloat16)
        query_grad = dot(grad_scores, key_all[windows[at], :], NN) * scaling
        store(grads, at, attended[at, 0], query_grad.astype(jnp.bfloat16))


def back_kernel(scaling, parts, *refs):
    pair, halo = list(refs[:parts]), refs[parts : parts + 5]
    own_st, before_st, after_st, low_st, high_st, bias = refs[parts + 5 : parts + 11]
    grads, (query_all, grad_all) = refs[parts + 11 : -2], refs[-2:]
    frames, _, _, tokens = own_st.shape
    fill_queries(halo, (query_all, grad_all))

    def stat_row(at, row, which):
        if at == 0:
            return low_st[row, 0, which : which + 1]
        if at == frames + 1:
            return high_st[row, 0, which : which + 1]
        return (before_st, own_st, after_st)[row][at - 1, 0, which : which + 1]

    def stat_band(at, which):
        rows = [stat_row(at + step, row, which) for step in range(3) for row in range(3)]
        return jnp.concatenate(rows, axis=1)

    windows = [pl.ds(3 * at * tokens, 9 * tokens) for at in range(frames)]
    scores = [dot(slab(pair, at, 0), query_all[windows[at], :], NT) for at in range(frames)]
    grad_probs = [dot(slab(pair, at, 1), grad_all[windows[at], :], NT) for at in range(frames)]
    for at in range(frames):
        shift = spread(bias[at] - stat_band(at, 0), tokens)
        weights = jnp.exp2(scores[at] * (scaling * LOG2E) + shift).astype(jnp.bfloat16)
        grad_scores = weights.astype(jnp.float32) * (grad_probs[at] - stat_band(at, 1))
        key_grad = dot(grad_scores.astype(jnp.bfloat16), query_all[windows[at], :], NN) * scaling
        value_grad = dot(weights, grad_all[windows[at], :], NN)
        store(grads, at, key_grad.astype(jnp.bfloat16), value_grad.astype(jnp.bfloat16))


def head_spec(shape, first):
    dim = len(shape) - 3
    block = shape[:dim] + (1,) + shape[dim + 1 :]
    return pl.BlockSpec(block, lambda head: (0,) * dim + (head + first,) + (0, 0))


def run(kernel, scaling, parts, operands, bias, outs, first, count, products):
    frames, (cells, dim) = bias.shape[0], operands[0].shape[-2:]
    tokens = parts * cells
    return pl.pallas_call(
        functools.partial(kernel, scaling, parts),
        grid=(count,),
        out_shape=tuple(outs),
        in_specs=[head_spec(part.shape, first) for part in operands]
        + [pl.BlockSpec(bias.shape, lambda head: (0,) * bias.ndim)],
        out_specs=tuple(head_spec(out.shape, 0) for out in outs),
        scratch_shapes=[pltpu.VMEM((3 * (frames + 2) * tokens, dim), jnp.bfloat16)] * 2,
        compiler_params=pltpu.CompilerParams(vmem_limit_bytes=16 * 2**20),
        cost_estimate=pl.CostEstimate(
            flops=7 * frames * count * 2 * products * tokens * 9 * tokens * dim,
            bytes_accessed=count * (frames + 2) * 3 * 2 * tokens * dim * 2,
            transcendentals=frames * count * tokens * 9 * tokens,
        ),
    )(*operands, bias)


def step_along(tensor, axis, sign):
    size = lax.axis_size(axis)
    return lax.ppermute(tensor, axis, [(i, i + sign) for i in range(size) if 0 <= i + sign < size])


def turn(tensor, shift):
    size = lax.axis_size("head")
    return lax.ppermute(tensor, "head", [(i, (i + shift) % size) for i in range(size)])


def frame_edges(rows):
    low = step_along(jnp.stack([row[-1] for row in rows]), "frame", 1)
    return low, step_along(jnp.stack([row[0] for row in rows]), "frame", -1)


def row_sides(own):
    return step_along(own, "row", 1), step_along(own, "row", -1)


def tile_biases(active, frames, columns_here, cells):
    size = lax.axis_size("head")
    me = lax.axis_index("head")
    frame_at = lax.axis_index("frame") * frames
    row_at = lax.axis_index("row")
    all_frames, all_rows, count, slots = active.shape
    padded = jnp.pad(active.astype(jnp.float32), ((1, 1), (1, 1), (0, 0), (0, 0)))
    near = lax.dynamic_slice(padded, (frame_at, row_at, 0, 0), (frames + 2, 3, count, slots))
    near = near.reshape(frames + 2, 3, count, 9, 3)
    steps = jnp.arange(3, dtype=jnp.int32) - 1
    frame_ids = frame_at + jnp.arange(frames, dtype=jnp.int32)[:, None] + steps
    frame_in = (frame_ids >= 0) & (frame_ids < all_frames)
    row_in = (row_at + steps >= 0) & (row_at + steps < all_rows)
    inside = (frame_in[:, :, None] & row_in).reshape(frames, 9).astype(jnp.float32)
    ahead = near[1 : 1 + frames, 1] * inside[:, None, :, None]
    pick = np.zeros((frames + 2, 3, 9, frames, 9), np.float32)
    for at in range(frames):
        for offset in range(9):
            pick[at + offset // 3, offset % 3, 8 - offset, at, offset] = 1.0
    behind = jnp.einsum("xyioc,xyofq->fiqc", near, pick)
    part = jnp.arange(size, dtype=jnp.int32)
    tile = ((me + part) % size * columns_here) // TC
    repeat = np.kron(np.eye(9 * size), np.ones((1, cells)))
    spread_out = jnp.asarray(repeat, jnp.bfloat16)
    smalls = []
    for table, sign in ((ahead, 1), (behind, -1)):
        owner = tile[None] == jnp.arange(count, dtype=jnp.int32)[:, None]
        shift = (sign * (tile[None, :] - tile[:, None]))[None] == steps[:, None, None]
        chosen = (owner[:, None, :, None] & shift[None]).astype(jnp.float32)
        smalls.append(jnp.einsum("fioc,icpk->fpok", table, chosen))
    small = jnp.stack(smalls).reshape(2 * frames * size, -1).astype(jnp.bfloat16)
    allowed = jnp.dot(small, spread_out, preferred_element_type=jnp.float32)
    bias = jnp.where(allowed > 0.5, 0.0, MASKED).reshape(2, frames, size, -1)
    return bias[0], bias[1]


def on_device(queries, keys, values, out_grad, active):
    frames, rows, columns_here, heads, dim = queries.shape
    size = lax.axis_size("head")
    me = lax.axis_index("head")
    groups = heads // size
    cells = rows * columns_here
    tokens = cells * size
    scaling = dim ** (-0.5)
    assert rows == TR and TC % columns_here == 0

    def pair_of(first, second, shift):
        start = (me + shift) % size * groups
        picked = [
            lax.dynamic_slice_in_dim(jnp.transpose(t, (0, 3, 1, 2, 4)), start, groups, 1) for t in (first, second)
        ]
        return jnp.stack(picked, 1).reshape(frames, 2, groups, cells, dim)

    def move(blocks):
        return [
            (first, [piece if b == 0 else turn(piece, b) for b, piece in enumerate(grads)]) for first, grads in blocks
        ]

    def assemble(blocks):
        outs = []
        for which in range(2):
            whole = jnp.zeros((frames, rows, heads, columns_here, dim), jnp.bfloat16)
            for first, pieces in blocks:
                for b, piece in enumerate(pieces):
                    piece = piece[which].reshape((frames, -1, rows, columns_here, dim)).transpose(0, 2, 1, 3, 4)
                    start = (me + size - b) % size * groups + first
                    whole = lax.dynamic_update_slice_in_dim(whole, piece, start, 2)
            outs.append(jnp.transpose(whole, (0, 1, 3, 2, 4)))
        return tuple(outs)

    front_bias, back_bias = tile_biases(active, frames, columns_here, cells)
    key_here, front_bias = lax.optimization_barrier((pair_of(keys, values, 0), front_bias))
    key_near = row_sides(key_here)
    key_sent = [pair_of(keys, values, shift) for shift in range(1, size)]
    key_moved = [turn(key_sent[size - b - 1], size - b) for b in range(1, size)]
    query_held = [pair_of(queries, out_grad, shift) for shift in range(size)]
    query_held, key_moved = lax.optimization_barrier((query_held, key_moved))
    key_far = [row_sides(part) for part in key_moved]
    query_moved = [turn(query_held[size - b], size - b) for b in range(1, size)]
    query_all = jnp.stack(query_held[:1] + query_moved, 1)
    query_before, query_after = row_sides(query_all)
    key_parts, sides = [key_here] + key_moved, [key_near] + key_far
    key_halo = key_parts + [before for before, _ in sides] + [after for _, after in sides]
    key_halo += frame_edges([row for part, (up, down) in zip(key_parts, sides) for row in (up, part, down)])
    query_halo = [query_all, query_before, query_after]
    query_rows = (query_before, query_all, query_after)
    query_halo += frame_edges([row[:, b] for b in range(size) for row in query_rows])

    def grads_shape(count):
        return [jax.ShapeDtypeStruct((2, frames, count, cells, dim), jnp.bfloat16)] * size

    attended_shape = jax.ShapeDtypeStruct((frames, groups, tokens, dim), jnp.bfloat16)
    stat_shape = jax.ShapeDtypeStruct((frames, groups, 2, tokens), jnp.float32)
    attended, stats = run(
        attend_kernel, scaling, size, [query_all] + key_halo, front_bias, [attended_shape, stat_shape], 0, groups, 2
    )
    halves = ((0, groups - groups // 2), (groups - groups // 2, groups // 2))
    stat_sides = row_sides(stats)
    front_blocks, shown = [], stats
    for first, count in halves:
        front_grads = run(
            query_kernel, scaling, size, [query_all] + key_halo + [attended, shown], front_bias,
            grads_shape(count), first, count, 3
        )
        front_blocks.append((first, front_grads))
        shown, stat_sides = lax.optimization_barrier((shown, stat_sides))
    stat_halo = [stats] + list(stat_sides) + list(frame_edges((stat_sides[0], stats, stat_sides[1])))
    front_blocks = move(front_blocks)
    back_blocks = []
    for first, count in halves:
        back_grads = run(
            back_kernel, scaling, size, key_parts + query_halo + stat_halo, back_bias, grads_shape(count),
            first, count, 4
        )
        back_bias, back_grads = lax.optimization_barrier((back_bias, back_grads))
        back_blocks.append((first, back_grads))
    back_blocks = move(back_blocks)
    first, pieces = back_blocks[0]
    front_blocks, pieces[-1] = lax.optimization_barrier((front_blocks, pieces[-1]))
    return assemble(front_blocks) + assemble(back_blocks)


def solution(mesh):
    spec = P("frame", "row", "head", None, None)
    return jax.shard_map(
        on_device, mesh=mesh, in_specs=(spec,) * 4 + (P(),), out_specs=(spec,) * 4, check_vma=False
    )
```

```python
import functools

import jax
import jax.numpy as jnp
import numpy as np
from jax import lax
from jax.experimental import pallas as pl
from jax.experimental.pallas import tpu as pltpu
from jax.sharding import PartitionSpec as P

TF = 1
TR = 8
TC = 8
MASKED = -1e30
LOG2E = 1.4426950408889634
NT = (((1,), (1,)), ((), ()))
NN = (((1,), (0,)), ((), ()))


def dot(left, right, dims):
    return lax.dot_general(left, right, dims, preferred_element_type=jnp.float32)


def spread(bias, tokens):
    parts, width = bias.shape
    return jnp.broadcast_to(bias[:, None], (parts, tokens // parts, width)).reshape(tokens, width)


def fill_bands(frames, parts, cells, side, edge, bands):
    for at in range(frames + 2):
        for row in range(3):
            for part in range(parts):
                place = pl.ds(((3 * at + row) * parts + part) * cells, cells)
                for which, band in enumerate(bands):
                    if at == 0:
                        band[place, :] = edge(0, row, part, which)
                    elif at == frames + 1:
                        band[place, :] = edge(1, row, part, which)
                    else:
                        band[place, :] = side(row, part, at - 1, which)


def fill_keys(head, parts, halo, bands):
    rows = (halo[parts : 2 * parts], halo[:parts], halo[2 * parts : 3 * parts])
    edges = halo[3 * parts :]
    frames, _, _, cells, _ = halo[0].shape
    side = lambda row, part, at, which: rows[row][part][at, which, head]
    edge = lambda end, row, part, which: edges[end][3 * part + row, which, head]
    fill_bands(frames, parts, cells, side, edge, bands)


def fill_queries(head, halo, bands):
    own, before, after, low, high = halo
    frames, parts, _, _, cells, _ = own.shape
    side = lambda row, part, at, which: (before, own, after)[row][at, part, which, head]
    edge = lambda end, row, part, which: (low, high)[end][3 * part + row, which, head]
    fill_bands(frames, parts, cells, side, edge, bands)


def slab(head, parts, at, which):
    if isinstance(parts, list):
        return jnp.concatenate([part[at, which, head] for part in parts], axis=0)
    return jnp.concatenate([parts[at, part, which, head] for part in range(parts.shape[1])], axis=0)


def attend_kernel(scaling, parts, first, *refs):
    head = pl.program_id(0) + first
    pair, halo = refs[0], refs[1 : 3 * parts + 3]
    bias, attended, stats, key_all, value_all = refs[3 * parts + 3 :]
    frames, _, tokens, _ = attended.shape
    fill_keys(head, parts, halo, (key_all, value_all))
    windows = [pl.ds(3 * at * tokens, 9 * tokens) for at in range(frames)]
    scores = [
        dot(slab(head, pair, at, 0), key_all[windows[at], :], NT) * (scaling * LOG2E) + spread(bias[at], tokens)
        for at in range(frames)
    ]
    highest = [jnp.max(part, axis=1, keepdims=True) for part in scores]
    raised = [jnp.exp2(part - top) for part, top in zip(scores, highest)]
    total = [jnp.sum(part, axis=1, keepdims=True) for part in raised]
    sums = [dot(raised[at].astype(jnp.bfloat16), value_all[windows[at], :], NN) for at in range(frames)]
    for at in range(frames):
        out = (sums[at] * (1.0 / total[at])).astype(jnp.bfloat16)
        grad = slab(head, pair, at, 1).astype(jnp.float32)
        grad_dot = jnp.sum(grad * out.astype(jnp.float32), axis=1, keepdims=True)
        attended[at, 0] = out
        lane = lax.broadcasted_iota(jnp.int32, (tokens, 128), 1)
        both = jnp.where(lane == 0, highest[at] + jnp.log2(total[at]), grad_dot)
        stats[at, 0] = jnp.transpose(both)[:2]


def store(grads, at, first, second):
    cells = grads[0].shape[-2]
    for part, out in enumerate(grads):
        own = slice(part * cells, (part + 1) * cells)
        out[0, at, 0] = first[own]
        out[1, at, 0] = second[own]


def query_kernel(scaling, parts, first, *refs):
    head = pl.program_id(0) + first
    pair, halo = refs[0], refs[1 : 3 * parts + 3]
    attended, stats, bias = refs[3 * parts + 3 : 3 * parts + 6]
    grads, (key_all, value_all) = refs[3 * parts + 6 : -2], refs[-2:]
    frames, _, tokens, _ = attended.shape
    fill_keys(head, parts, halo, (key_all, value_all))
    windows = [pl.ds(3 * at * tokens, 9 * tokens) for at in range(frames)]

    def column(at, which):
        wide = jnp.broadcast_to(stats[at, 0, which : which + 1], (128, tokens))
        return jnp.transpose(wide)[:, :1]

    scores = [dot(slab(head, pair, at, 0), key_all[windows[at], :], NT) for at in range(frames)]
    grad_probs = [dot(slab(head, pair, at, 1), value_all[windows[at], :], NT) for at in range(frames)]
    for at in range(frames):
        shift = spread(bias[at], tokens) - column(at, 0)
        weights = jnp.exp2(scores[at] * (scaling * LOG2E) + shift)
        grad_scores = (weights * (grad_probs[at] - column(at, 1))).astype(jnp.bfloat16)
        query_grad = dot(grad_scores, key_all[windows[at], :], NN) * scaling
        store(grads, at, attended[at, 0], query_grad.astype(jnp.bfloat16))


def back_kernel(scaling, parts, first, *refs):
    head = pl.program_id(0) + first
    pair, halo = list(refs[:parts]), refs[parts : parts + 5]
    own_st, before_st, after_st, low_st, high_st, bias = refs[parts + 5 : parts + 11]
    grads, (query_all, grad_all) = refs[parts + 11 : -2], refs[-2:]
    frames, _, _, tokens = own_st.shape
    fill_queries(head, halo, (query_all, grad_all))

    def stat_row(at, row, which):
        if at == 0:
            return low_st[row, 0, which : which + 1]
        if at == frames + 1:
            return high_st[row, 0, which : which + 1]
        return (before_st, own_st, after_st)[row][at - 1, 0, which : which + 1]

    def stat_band(at, which):
        rows = [stat_row(at + step, row, which) for step in range(3) for row in range(3)]
        return jnp.concatenate(rows, axis=1)

    windows = [pl.ds(3 * at * tokens, 9 * tokens) for at in range(frames)]
    scores = [dot(slab(head, pair, at, 0), query_all[windows[at], :], NT) for at in range(frames)]
    grad_probs = [dot(slab(head, pair, at, 1), grad_all[windows[at], :], NT) for at in range(frames)]
    for at in range(frames):
        shift = spread(bias[at] - stat_band(at, 0), tokens)
        weights = jnp.exp2(scores[at] * (scaling * LOG2E) + shift).astype(jnp.bfloat16)
        grad_scores = weights.astype(jnp.float32) * (grad_probs[at] - stat_band(at, 1))
        key_grad = dot(grad_scores.astype(jnp.bfloat16), query_all[windows[at], :], NN) * scaling
        value_grad = dot(weights, grad_all[windows[at], :], NN)
        store(grads, at, key_grad.astype(jnp.bfloat16), value_grad.astype(jnp.bfloat16))


def head_spec(shape, first):
    dim = len(shape) - 3
    block = shape[:dim] + (1,) + shape[dim + 1 :]
    return pl.BlockSpec(block, lambda head: (0,) * dim + (head + first,) + (0, 0))


def run(kernel, scaling, parts, operands, bias, outs, first, count, products):
    frames, (cells, dim) = bias.shape[0], operands[0].shape[-2:]
    tokens = parts * cells
    return pl.pallas_call(
        functools.partial(kernel, scaling, parts, first),
        grid=(count,),
        out_shape=tuple(outs),
        in_specs=[
            pl.BlockSpec(memory_space=pltpu.VMEM) if part.ndim > 4 else head_spec(part.shape, first)
            for part in operands
        ]
        + [pl.BlockSpec(bias.shape, lambda head: (0,) * bias.ndim)],
        out_specs=tuple(head_spec(out.shape, 0) for out in outs),
        scratch_shapes=[pltpu.VMEM((3 * (frames + 2) * tokens, dim), jnp.bfloat16)] * 2,
        compiler_params=pltpu.CompilerParams(vmem_limit_bytes=16 * 2**20),
        cost_estimate=pl.CostEstimate(
            flops=7 * frames * count * 2 * products * tokens * 9 * tokens * dim,
            bytes_accessed=count * (frames + 2) * 3 * 2 * tokens * dim * 2,
            transcendentals=frames * count * tokens * 9 * tokens,
        ),
    )(*operands, bias)


def step_along(tensor, axis, sign):
    size = lax.axis_size(axis)
    return lax.ppermute(tensor, axis, [(i, i + sign) for i in range(size) if 0 <= i + sign < size])


def turn(tensor, shift):
    size = lax.axis_size("head")
    return lax.ppermute(tensor, "head", [(i, (i + shift) % size) for i in range(size)])


def frame_edges(rows):
    low = step_along(jnp.stack([row[-1] for row in rows]), "frame", 1)
    return low, step_along(jnp.stack([row[0] for row in rows]), "frame", -1)


def row_sides(own):
    return step_along(own, "row", 1), step_along(own, "row", -1)


def tile_biases(active, frames, columns_here, cells):
    size = lax.axis_size("head")
    me = lax.axis_index("head")
    frame_at = lax.axis_index("frame") * frames
    row_at = lax.axis_index("row")
    all_frames, all_rows, count, slots = active.shape
    padded = jnp.pad(active.astype(jnp.float32), ((1, 1), (1, 1), (0, 0), (0, 0)))
    near = lax.dynamic_slice(padded, (frame_at, row_at, 0, 0), (frames + 2, 3, count, slots))
    near = near.reshape(frames + 2, 3, count, 9, 3)
    steps = jnp.arange(3, dtype=jnp.int32) - 1
    frame_ids = frame_at + jnp.arange(frames, dtype=jnp.int32)[:, None] + steps
    frame_in = (frame_ids >= 0) & (frame_ids < all_frames)
    row_in = (row_at + steps >= 0) & (row_at + steps < all_rows)
    inside = (frame_in[:, :, None] & row_in).reshape(frames, 9).astype(jnp.float32)
    ahead = near[1 : 1 + frames, 1] * inside[:, None, :, None]
    pick = np.zeros((frames + 2, 3, 9, frames, 9), np.float32)
    for at in range(frames):
        for offset in range(9):
            pick[at + offset // 3, offset % 3, 8 - offset, at, offset] = 1.0
    behind = jnp.einsum("xyioc,xyofq->fiqc", near, pick)
    part = jnp.arange(size, dtype=jnp.int32)
    tile = ((me + part) % size * columns_here) // TC
    repeat = np.kron(np.eye(9 * size), np.ones((1, cells)))
    spread_out = jnp.asarray(repeat, jnp.bfloat16)
    smalls = []
    for table, sign in ((ahead, 1), (behind, -1)):
        owner = tile[None] == jnp.arange(count, dtype=jnp.int32)[:, None]
        shift = (sign * (tile[None, :] - tile[:, None]))[None] == steps[:, None, None]
        chosen = (owner[:, None, :, None] & shift[None]).astype(jnp.float32)
        smalls.append(jnp.einsum("fioc,icpk->fpok", table, chosen))
    small = jnp.stack(smalls).reshape(2 * frames * size, -1).astype(jnp.bfloat16)
    allowed = jnp.dot(small, spread_out, preferred_element_type=jnp.float32)
    bias = jnp.where(allowed > 0.5, 0.0, MASKED).reshape(2, frames, size, -1)
    return bias[0], bias[1]


def on_device(queries, keys, values, out_grad, active):
    frames, rows, columns_here, heads, dim = queries.shape
    size = lax.axis_size("head")
    me = lax.axis_index("head")
    groups = heads // size
    cells = rows * columns_here
    tokens = cells * size
    scaling = dim ** (-0.5)
    assert rows == TR and TC % columns_here == 0

    def pair_of(first, second, shift):
        start = (me + shift) % size * groups
        picked = [
            lax.dynamic_slice_in_dim(jnp.transpose(t, (0, 3, 1, 2, 4)), start, groups, 1) for t in (first, second)
        ]
        return jnp.stack(picked, 1).reshape(frames, 2, groups, cells, dim)

    def move(blocks):
        return [
            (first, [piece if b == 0 else turn(piece, b) for b, piece in enumerate(grads)]) for first, grads in blocks
        ]

    def assemble(blocks):
        whole = jnp.zeros((2, frames, rows, heads, columns_here, dim), jnp.bfloat16)
        for first, pieces in blocks:
            for b, piece in enumerate(pieces):
                piece = piece.reshape((2, frames, -1, rows, columns_here, dim)).transpose(0, 1, 3, 2, 4, 5)
                start = (me + size - b) % size * groups + first
                whole = lax.dynamic_update_slice_in_dim(whole, piece, start, 3)
        whole = jnp.transpose(whole, (0, 1, 2, 4, 3, 5))
        return whole[0], whole[1]

    front_bias, back_bias = tile_biases(active, frames, columns_here, cells)
    key_here, front_bias = lax.optimization_barrier((pair_of(keys, values, 0), front_bias))
    key_near = row_sides(key_here)
    key_sent = [pair_of(keys, values, shift) for shift in range(1, size)]
    key_moved = [turn(key_sent[size - b - 1], size - b) for b in range(1, size)]
    query_held = [pair_of(queries, out_grad, shift) for shift in range(size)]
    query_held, key_moved = lax.optimization_barrier((query_held, key_moved))
    key_far = [row_sides(part) for part in key_moved]
    query_moved = [turn(query_held[size - b], size - b) for b in range(1, size)]
    query_all = jnp.stack(query_held[:1] + query_moved, 1)
    query_before, query_after = row_sides(query_all)
    key_parts, sides = [key_here] + key_moved, [key_near] + key_far
    key_halo = key_parts + [before for before, _ in sides] + [after for _, after in sides]
    key_halo += frame_edges([row for part, (up, down) in zip(key_parts, sides) for row in (up, part, down)])
    query_halo = [query_all, query_before, query_after]
    query_rows = (query_before, query_all, query_after)
    query_halo += frame_edges([row[:, b] for b in range(size) for row in query_rows])

    def grads_shape(count):
        return [jax.ShapeDtypeStruct((2, frames, count, cells, dim), jnp.bfloat16)] * size

    attended_shape = jax.ShapeDtypeStruct((frames, groups, tokens, dim), jnp.bfloat16)
    stat_shape = jax.ShapeDtypeStruct((frames, groups, 2, tokens), jnp.float32)
    attended, stats = run(
        attend_kernel, scaling, size, [query_all] + key_halo, front_bias, [attended_shape, stat_shape], 0, groups, 2
    )
    halves = ((0, groups - groups // 2), (groups - groups // 2, groups // 2))
    stat_sides = row_sides(stats)
    front_blocks, shown = [], stats
    for first, count in halves:
        front_grads = run(
            query_kernel, scaling, size, [query_all] + key_halo + [attended, shown], front_bias,
            grads_shape(count), first, count, 3
        )
        front_blocks.append((first, front_grads))
        shown, stat_sides = lax.optimization_barrier((shown, stat_sides))
    stat_halo = [stats] + list(stat_sides) + list(frame_edges((stat_sides[0], stats, stat_sides[1])))
    front_blocks = move(front_blocks)
    back_blocks = []
    for first, count in halves:
        back_grads = run(
            back_kernel, scaling, size, key_parts + query_halo + stat_halo, back_bias, grads_shape(count),
            first, count, 4
        )
        back_bias, back_grads = lax.optimization_barrier((back_bias, back_grads))
        back_blocks.append((first, back_grads))
    back_blocks = move(back_blocks)
    first, pieces = back_blocks[0]
    front_blocks, pieces[-1] = lax.optimization_barrier((front_blocks, pieces[-1]))
    return assemble(front_blocks) + assemble(back_blocks)


def solution(mesh):
    spec = P("frame", "row", "head", None, None)
    return jax.shard_map(
        on_device, mesh=mesh, in_specs=(spec,) * 4 + (P(),), out_specs=(spec,) * 4, check_vma=False
    )
```

```python
import functools

import jax
import jax.numpy as jnp
import numpy as np
from jax import lax
from jax.experimental import pallas as pl
from jax.experimental.pallas import tpu as pltpu
from jax.sharding import PartitionSpec as P

TF = 1
TR = 8
TC = 8
MASKED = -1e30
LOG2E = 1.4426950408889634
NT = (((1,), (1,)), ((), ()))
NN = (((1,), (0,)), ((), ()))


def dot(left, right, dims):
    return lax.dot_general(left, right, dims, preferred_element_type=jnp.float32)


def spread(bias, tokens):
    parts, width = bias.shape
    return jnp.broadcast_to(bias[:, None], (parts, tokens // parts, width)).reshape(tokens, width)


def fill_bands(frames, parts, cells, side, edge, bands):
    for at in range(frames + 2):
        for row in range(3):
            for part in range(parts):
                for which, band in enumerate(bands):
                    if at == 0:
                        band.append(edge(0, row, part, which))
                    elif at == frames + 1:
                        band.append(edge(1, row, part, which))
                    else:
                        band.append(side(row, part, at - 1, which))


def window(band, parts, at):
    return jnp.concatenate(band[3 * at * parts : (3 * at + 9) * parts], axis=0)


def fill_keys(head, parts, halo, bands):
    rows = (halo[parts : 2 * parts], halo[:parts], halo[2 * parts : 3 * parts])
    edges = halo[3 * parts :]
    frames, _, _, cells, _ = halo[0].shape
    side = lambda row, part, at, which: rows[row][part][at, which, head]
    edge = lambda end, row, part, which: edges[end][3 * part + row, which, head]
    fill_bands(frames, parts, cells, side, edge, bands)


def fill_queries(head, halo, bands):
    own, before, after, low, high = halo
    frames, parts, _, _, cells, _ = own.shape
    side = lambda row, part, at, which: (before, own, after)[row][at, part, which, head]
    edge = lambda end, row, part, which: (low, high)[end][3 * part + row, which, head]
    fill_bands(frames, parts, cells, side, edge, bands)


def slab(head, parts, at, which):
    if isinstance(parts, list):
        return jnp.concatenate([part[at, which, head] for part in parts], axis=0)
    return jnp.concatenate([parts[at, part, which, head] for part in range(parts.shape[1])], axis=0)


def attend_kernel(scaling, parts, first, *refs):
    head = pl.program_id(0) + first
    pair, halo = refs[0], refs[1 : 3 * parts + 3]
    bias, attended, stats = refs[3 * parts + 3 :]
    key_all, value_all = [], []
    frames, _, tokens, _ = attended.shape
    fill_keys(head, parts, halo, (key_all, value_all))
    scores = [
        dot(slab(head, pair, at, 0), window(key_all, parts, at), NT) * (scaling * LOG2E) + spread(bias[at], tokens)
        for at in range(frames)
    ]
    highest = [jnp.max(part, axis=1, keepdims=True) for part in scores]
    raised = [jnp.exp2(part - top) for part, top in zip(scores, highest)]
    total = [jnp.sum(part, axis=1, keepdims=True) for part in raised]
    sums = [dot(raised[at].astype(jnp.bfloat16), window(value_all, parts, at), NN) for at in range(frames)]
    for at in range(frames):
        out = (sums[at] * (1.0 / total[at])).astype(jnp.bfloat16)
        grad = slab(head, pair, at, 1).astype(jnp.float32)
        grad_dot = jnp.sum(grad * out.astype(jnp.float32), axis=1, keepdims=True)
        attended[at, 0] = out
        lane = lax.broadcasted_iota(jnp.int32, (tokens, 128), 1)
        both = jnp.where(lane == 0, highest[at] + jnp.log2(total[at]), grad_dot)
        stats[at, 0] = jnp.transpose(both)[:2]


def store(grads, at, first, second):
    cells = grads[0].shape[-2]
    for part, out in enumerate(grads):
        own = slice(part * cells, (part + 1) * cells)
        out[0, at, 0] = first[own]
        out[1, at, 0] = second[own]


def query_kernel(scaling, parts, first, *refs):
    head = pl.program_id(0) + first
    pair, halo = refs[0], refs[1 : 3 * parts + 3]
    attended, stats, bias = refs[3 * parts + 3 : 3 * parts + 6]
    grads = refs[3 * parts + 6 :]
    key_all, value_all = [], []
    frames, _, tokens, _ = attended.shape
    fill_keys(head, parts, halo, (key_all, value_all))

    def column(at, which):
        wide = jnp.broadcast_to(stats[at, 0, which : which + 1], (128, tokens))
        return jnp.transpose(wide)[:, :1]

    scores = [dot(slab(head, pair, at, 0), window(key_all, parts, at), NT) for at in range(frames)]
    grad_probs = [dot(slab(head, pair, at, 1), window(value_all, parts, at), NT) for at in range(frames)]
    for at in range(frames):
        shift = spread(bias[at], tokens) - column(at, 0)
        weights = jnp.exp2(scores[at] * (scaling * LOG2E) + shift)
        grad_scores = (weights * (grad_probs[at] - column(at, 1))).astype(jnp.bfloat16)
        query_grad = dot(grad_scores, window(key_all, parts, at), NN) * scaling
        store(grads, at, attended[at, 0], query_grad.astype(jnp.bfloat16))


def back_kernel(scaling, parts, first, *refs):
    head = pl.program_id(0) + first
    pair, halo = list(refs[:parts]), refs[parts : parts + 5]
    own_st, before_st, after_st, low_st, high_st, bias = refs[parts + 5 : parts + 11]
    grads = refs[parts + 11 :]
    query_all, grad_all = [], []
    frames, _, _, tokens = own_st.shape
    fill_queries(head, halo, (query_all, grad_all))

    def stat_row(at, row, which):
        if at == 0:
            return low_st[row, 0, which : which + 1]
        if at == frames + 1:
            return high_st[row, 0, which : which + 1]
        return (before_st, own_st, after_st)[row][at - 1, 0, which : which + 1]

    def stat_band(at, which):
        rows = [stat_row(at + step, row, which) for step in range(3) for row in range(3)]
        return jnp.concatenate(rows, axis=1)

    scores = [dot(slab(head, pair, at, 0), window(query_all, parts, at), NT) for at in range(frames)]
    grad_probs = [dot(slab(head, pair, at, 1), window(grad_all, parts, at), NT) for at in range(frames)]
    for at in range(frames):
        shift = spread(bias[at] - stat_band(at, 0), tokens)
        weights = jnp.exp2(scores[at] * (scaling * LOG2E) + shift).astype(jnp.bfloat16)
        grad_scores = weights.astype(jnp.float32) * (grad_probs[at] - stat_band(at, 1))
        key_grad = dot(grad_scores.astype(jnp.bfloat16), window(query_all, parts, at), NN) * scaling
        value_grad = dot(weights, window(grad_all, parts, at), NN)
        store(grads, at, key_grad.astype(jnp.bfloat16), value_grad.astype(jnp.bfloat16))


def head_spec(shape, first):
    dim = len(shape) - 3
    block = shape[:dim] + (1,) + shape[dim + 1 :]
    return pl.BlockSpec(block, lambda head: (0,) * dim + (head + first,) + (0, 0))


def run(kernel, scaling, parts, operands, bias, outs, first, count, products):
    frames, (cells, dim) = bias.shape[0], operands[0].shape[-2:]
    tokens = parts * cells
    return pl.pallas_call(
        functools.partial(kernel, scaling, parts, first),
        grid=(count,),
        out_shape=tuple(outs),
        in_specs=[
            pl.BlockSpec(memory_space=pltpu.VMEM) if part.ndim > 4 else head_spec(part.shape, first)
            for part in operands
        ]
        + [pl.BlockSpec(bias.shape, lambda head: (0,) * bias.ndim)],
        out_specs=tuple(head_spec(out.shape, 0) for out in outs),
        compiler_params=pltpu.CompilerParams(vmem_limit_bytes=16 * 2**20),
        cost_estimate=pl.CostEstimate(
            flops=7 * frames * count * 2 * products * tokens * 9 * tokens * dim,
            bytes_accessed=count * (frames + 2) * 3 * 2 * tokens * dim * 2,
            transcendentals=frames * count * tokens * 9 * tokens,
        ),
    )(*operands, bias)


def step_along(tensor, axis, sign):
    size = lax.axis_size(axis)
    return lax.ppermute(tensor, axis, [(i, i + sign) for i in range(size) if 0 <= i + sign < size])


def turn(tensor, shift):
    size = lax.axis_size("head")
    return lax.ppermute(tensor, "head", [(i, (i + shift) % size) for i in range(size)])


def frame_edges(rows):
    low = step_along(jnp.stack([row[-1] for row in rows]), "frame", 1)
    return low, step_along(jnp.stack([row[0] for row in rows]), "frame", -1)


def row_sides(own):
    return step_along(own, "row", 1), step_along(own, "row", -1)


def tile_biases(active, frames, columns_here, cells):
    size = lax.axis_size("head")
    me = lax.axis_index("head")
    frame_at = lax.axis_index("frame") * frames
    row_at = lax.axis_index("row")
    all_frames, all_rows, count, slots = active.shape
    padded = jnp.pad(active.astype(jnp.float32), ((1, 1), (1, 1), (0, 0), (0, 0)))
    near = lax.dynamic_slice(padded, (frame_at, row_at, 0, 0), (frames + 2, 3, count, slots))
    near = near.reshape(frames + 2, 3, count, 9, 3)
    steps = jnp.arange(3, dtype=jnp.int32) - 1
    frame_ids = frame_at + jnp.arange(frames, dtype=jnp.int32)[:, None] + steps
    frame_in = (frame_ids >= 0) & (frame_ids < all_frames)
    row_in = (row_at + steps >= 0) & (row_at + steps < all_rows)
    inside = (frame_in[:, :, None] & row_in).reshape(frames, 9).astype(jnp.float32)
    ahead = near[1 : 1 + frames, 1] * inside[:, None, :, None]
    pick = np.zeros((frames + 2, 3, 9, frames, 9), np.float32)
    for at in range(frames):
        for offset in range(9):
            pick[at + offset // 3, offset % 3, 8 - offset, at, offset] = 1.0
    behind = jnp.einsum("xyioc,xyofq->fiqc", near, pick)
    part = jnp.arange(size, dtype=jnp.int32)
    tile = ((me + part) % size * columns_here) // TC
    repeat = np.kron(np.eye(9 * size), np.ones((1, cells)))
    spread_out = jnp.asarray(repeat, jnp.bfloat16)
    smalls = []
    for table, sign in ((ahead, 1), (behind, -1)):
        owner = tile[None] == jnp.arange(count, dtype=jnp.int32)[:, None]
        shift = (sign * (tile[None, :] - tile[:, None]))[None] == steps[:, None, None]
        chosen = (owner[:, None, :, None] & shift[None]).astype(jnp.float32)
        smalls.append(jnp.einsum("fioc,icpk->fpok", table, chosen))
    small = jnp.stack(smalls).reshape(2 * frames * size, -1).astype(jnp.bfloat16)
    allowed = jnp.dot(small, spread_out, preferred_element_type=jnp.float32)
    bias = jnp.where(allowed > 0.5, 0.0, MASKED).reshape(2, frames, size, -1)
    return bias[0], bias[1]


def on_device(queries, keys, values, out_grad, active):
    frames, rows, columns_here, heads, dim = queries.shape
    size = lax.axis_size("head")
    me = lax.axis_index("head")
    groups = heads // size
    cells = rows * columns_here
    tokens = cells * size
    scaling = dim ** (-0.5)
    assert rows == TR and TC % columns_here == 0

    def pair_of(first, second, shift):
        start = (me + shift) % size * groups
        picked = [
            lax.dynamic_slice_in_dim(jnp.transpose(t, (0, 3, 1, 2, 4)), start, groups, 1) for t in (first, second)
        ]
        return jnp.stack(picked, 1).reshape(frames, 2, groups, cells, dim)

    def move(blocks):
        return [
            (first, [piece if b == 0 else turn(piece, b) for b, piece in enumerate(grads)]) for first, grads in blocks
        ]

    def assemble(blocks):
        whole = jnp.zeros((2, frames, rows, heads, columns_here, dim), jnp.bfloat16)
        for first, pieces in blocks:
            for b, piece in enumerate(pieces):
                piece = piece.reshape((2, frames, -1, rows, columns_here, dim)).transpose(0, 1, 3, 2, 4, 5)
                start = (me + size - b) % size * groups + first
                whole = lax.dynamic_update_slice_in_dim(whole, piece, start, 3)
        whole = jnp.transpose(whole, (0, 1, 2, 4, 3, 5))
        return whole[0], whole[1]

    front_bias, back_bias = tile_biases(active, frames, columns_here, cells)
    key_here, front_bias = lax.optimization_barrier((pair_of(keys, values, 0), front_bias))
    key_near = row_sides(key_here)
    key_sent = [pair_of(keys, values, shift) for shift in range(1, size)]
    key_moved = [turn(key_sent[size - b - 1], size - b) for b in range(1, size)]
    query_held = [pair_of(queries, out_grad, shift) for shift in range(size)]
    query_held, key_moved = lax.optimization_barrier((query_held, key_moved))
    key_far = [row_sides(part) for part in key_moved]
    query_moved = [turn(query_held[size - b], size - b) for b in range(1, size)]
    query_all = jnp.stack(query_held[:1] + query_moved, 1)
    query_before, query_after = row_sides(query_all)
    key_parts, sides = [key_here] + key_moved, [key_near] + key_far
    key_halo = key_parts + [before for before, _ in sides] + [after for _, after in sides]
    key_halo += frame_edges([row for part, (up, down) in zip(key_parts, sides) for row in (up, part, down)])
    query_halo = [query_all, query_before, query_after]
    query_rows = (query_before, query_all, query_after)
    query_halo += frame_edges([row[:, b] for b in range(size) for row in query_rows])

    def grads_shape(count):
        return [jax.ShapeDtypeStruct((2, frames, count, cells, dim), jnp.bfloat16)] * size

    attended_shape = jax.ShapeDtypeStruct((frames, groups, tokens, dim), jnp.bfloat16)
    stat_shape = jax.ShapeDtypeStruct((frames, groups, 2, tokens), jnp.float32)
    attended, stats = run(
        attend_kernel, scaling, size, [query_all] + key_halo, front_bias, [attended_shape, stat_shape], 0, groups, 2
    )
    halves = ((0, groups - groups // 2), (groups - groups // 2, groups // 2))
    stat_sides = row_sides(stats)
    front_blocks, shown = [], stats
    for first, count in halves:
        front_grads = run(
            query_kernel, scaling, size, [query_all] + key_halo + [attended, shown], front_bias,
            grads_shape(count), first, count, 3
        )
        front_blocks.append((first, front_grads))
        shown, stat_sides = lax.optimization_barrier((shown, stat_sides))
    stat_halo = [stats] + list(stat_sides) + list(frame_edges((stat_sides[0], stats, stat_sides[1])))
    front_blocks = move(front_blocks)
    back_blocks = []
    for first, count in halves:
        back_grads = run(
            back_kernel, scaling, size, key_parts + query_halo + stat_halo, back_bias, grads_shape(count),
            first, count, 4
        )
        back_bias, back_grads = lax.optimization_barrier((back_bias, back_grads))
        back_blocks.append((first, back_grads))
    back_blocks = move(back_blocks)
    first, pieces = back_blocks[0]
    front_blocks, pieces[-1] = lax.optimization_barrier((front_blocks, pieces[-1]))
    return assemble(front_blocks) + assemble(back_blocks)


def solution(mesh):
    spec = P("frame", "row", "head", None, None)
    return jax.shard_map(
        on_device, mesh=mesh, in_specs=(spec,) * 4 + (P(),), out_specs=(spec,) * 4, check_vma=False
    )
```

```python
import functools

import jax
import jax.numpy as jnp
import numpy as np
from jax import lax
from jax.experimental import pallas as pl
from jax.experimental.pallas import tpu as pltpu
from jax.sharding import PartitionSpec as P

TF = 1
TR = 8
TC = 8
MASKED = -1e30
LOG2E = 1.4426950408889634
NT = (((1,), (1,)), ((), ()))
NN = (((1,), (0,)), ((), ()))


def dot(left, right, dims):
    return lax.dot_general(left, right, dims, preferred_element_type=jnp.float32)


def spread(bias, tokens):
    parts, width = bias.shape
    return jnp.broadcast_to(bias[:, None], (parts, tokens // parts, width)).reshape(tokens, width)


def fill_bands(frames, parts, cells, side, edge, bands):
    for at in range(frames + 2):
        for row in range(3):
            for part in range(parts):
                for which, band in enumerate(bands):
                    if at == 0:
                        band.append(edge(0, row, part, which))
                    elif at == frames + 1:
                        band.append(edge(1, row, part, which))
                    else:
                        band.append(side(row, part, at - 1, which))


def window(band, parts, at):
    return jnp.concatenate(band[3 * at * parts : (3 * at + 9) * parts], axis=0)


def fill_keys(head, parts, halo, bands):
    rows = (halo[parts : 2 * parts], halo[:parts], halo[2 * parts : 3 * parts])
    edges = halo[3 * parts :]
    frames, _, _, cells, _ = halo[0].shape
    side = lambda row, part, at, which: rows[row][part][at, which, head]
    edge = lambda end, row, part, which: edges[end][3 * part + row, which, head]
    fill_bands(frames, parts, cells, side, edge, bands)


def fill_queries(head, halo, bands):
    own, before, after, low, high = halo
    frames, parts, _, _, cells, _ = own.shape
    side = lambda row, part, at, which: (before, own, after)[row][at, part, which, head]
    edge = lambda end, row, part, which: (low, high)[end][3 * part + row, which, head]
    fill_bands(frames, parts, cells, side, edge, bands)


def slab(head, parts, at, which):
    if isinstance(parts, list):
        return jnp.concatenate([part[at, which, head] for part in parts], axis=0)
    return jnp.concatenate([parts[at, part, which, head] for part in range(parts.shape[1])], axis=0)


def attend_kernel(scaling, parts, first, *refs):
    head = pl.program_id(0) + first
    pair, halo = refs[0], refs[1 : 3 * parts + 3]
    bias, attended, stats = refs[3 * parts + 3 :]
    key_all, value_all = [], []
    frames, _, tokens, _ = attended.shape
    fill_keys(head, parts, halo, (key_all, value_all))
    scores = [
        dot(slab(head, pair, at, 0), window(key_all, parts, at), NT) * (scaling * LOG2E) + spread(bias[at], tokens)
        for at in range(frames)
    ]
    highest = [jnp.max(part, axis=1, keepdims=True) for part in scores]
    raised = [jnp.exp2(part - top) for part, top in zip(scores, highest)]
    total = [jnp.sum(part, axis=1, keepdims=True) for part in raised]
    sums = [dot(raised[at].astype(jnp.bfloat16), window(value_all, parts, at), NN) for at in range(frames)]
    for at in range(frames):
        out = (sums[at] * (1.0 / total[at])).astype(jnp.bfloat16)
        grad = slab(head, pair, at, 1).astype(jnp.float32)
        grad_dot = jnp.sum(grad * out.astype(jnp.float32), axis=1, keepdims=True)
        attended[at, 0] = out
        lane = lax.broadcasted_iota(jnp.int32, (tokens, 128), 1)
        both = jnp.where(lane == 0, highest[at] + jnp.log2(total[at]), grad_dot)
        stats[at, 0] = jnp.transpose(both)[:2]


def store(grads, at, first, second):
    cells = grads[0].shape[-2]
    for part, out in enumerate(grads):
        own = slice(part * cells, (part + 1) * cells)
        out[0, at, 0] = first[own]
        out[1, at, 0] = second[own]


def query_kernel(scaling, parts, first, *refs):
    head = pl.program_id(0) + first
    pair, halo = refs[0], refs[1 : 3 * parts + 3]
    attended, stats, bias = refs[3 * parts + 3 : 3 * parts + 6]
    grads = refs[3 * parts + 6 :]
    key_all, value_all = [], []
    frames, _, tokens, _ = attended.shape
    fill_keys(head, parts, halo, (key_all, value_all))

    def column(at, which):
        wide = jnp.broadcast_to(stats[at, 0, which : which + 1], (128, tokens))
        return jnp.transpose(wide)[:, :1]

    scores = [dot(slab(head, pair, at, 0), window(key_all, parts, at), NT) for at in range(frames)]
    grad_probs = [dot(slab(head, pair, at, 1), window(value_all, parts, at), NT) for at in range(frames)]
    for at in range(frames):
        shift = spread(bias[at], tokens) - column(at, 0)
        weights = jnp.exp2(scores[at] * (scaling * LOG2E) + shift)
        grad_scores = (weights * (grad_probs[at] - column(at, 1))).astype(jnp.bfloat16)
        query_grad = dot(grad_scores, window(key_all, parts, at), NN) * scaling
        store(grads, at, attended[at, 0], query_grad.astype(jnp.bfloat16))


def back_kernel(scaling, parts, first, *refs):
    head = pl.program_id(0) + first
    pair, halo = list(refs[:parts]), refs[parts : parts + 5]
    own_st, before_st, after_st, low_st, high_st, bias = refs[parts + 5 : parts + 11]
    grads = refs[parts + 11 :]
    query_all, grad_all = [], []
    frames, _, _, tokens = own_st.shape
    fill_queries(head, halo, (query_all, grad_all))

    def stat_row(at, row, which):
        if at == 0:
            return low_st[row, 0, which : which + 1]
        if at == frames + 1:
            return high_st[row, 0, which : which + 1]
        return (before_st, own_st, after_st)[row][at - 1, 0, which : which + 1]

    def stat_band(at, which):
        rows = [stat_row(at + step, row, which) for step in range(3) for row in range(3)]
        return jnp.concatenate(rows, axis=1)

    scores = [dot(slab(head, pair, at, 0), window(query_all, parts, at), NT) for at in range(frames)]
    grad_probs = [dot(slab(head, pair, at, 1), window(grad_all, parts, at), NT) for at in range(frames)]
    for at in range(frames):
        shift = spread(bias[at] - stat_band(at, 0), tokens)
        weights = jnp.exp2(scores[at] * (scaling * LOG2E) + shift).astype(jnp.bfloat16)
        grad_scores = weights.astype(jnp.float32) * (grad_probs[at] - stat_band(at, 1))
        key_grad = dot(grad_scores.astype(jnp.bfloat16), window(query_all, parts, at), NN) * scaling
        value_grad = dot(weights, window(grad_all, parts, at), NN)
        store(grads, at, key_grad.astype(jnp.bfloat16), value_grad.astype(jnp.bfloat16))


def head_spec(shape, first):
    dim = len(shape) - 3
    block = shape[:dim] + (1,) + shape[dim + 1 :]
    return pl.BlockSpec(block, lambda head: (0,) * dim + (head + first,) + (0, 0))


def run(kernel, scaling, parts, operands, bias, outs, first, count, products):
    frames, (cells, dim) = bias.shape[0], operands[0].shape[-2:]
    tokens = parts * cells
    return pl.pallas_call(
        functools.partial(kernel, scaling, parts, first),
        grid=(count,),
        out_shape=tuple(outs),
        in_specs=[
            pl.BlockSpec(memory_space=pltpu.VMEM) if part.ndim > 4 else head_spec(part.shape, first)
            for part in operands
        ]
        + [pl.BlockSpec(bias.shape, lambda head: (0,) * bias.ndim)],
        out_specs=tuple(head_spec(out.shape, 0) for out in outs),
        compiler_params=pltpu.CompilerParams(vmem_limit_bytes=16 * 2**20),
        cost_estimate=pl.CostEstimate(
            flops=7 * frames * count * 2 * products * tokens * 9 * tokens * dim,
            bytes_accessed=count * (frames + 2) * 3 * 2 * tokens * dim * 2,
            transcendentals=frames * count * tokens * 9 * tokens,
        ),
    )(*operands, bias)


def step_along(tensor, axis, sign):
    size = lax.axis_size(axis)
    return lax.ppermute(tensor, axis, [(i, i + sign) for i in range(size) if 0 <= i + sign < size])


def turn(tensor, shift):
    size = lax.axis_size("head")
    return lax.ppermute(tensor, "head", [(i, (i + shift) % size) for i in range(size)])


def frame_edges(rows):
    low = step_along(jnp.stack([row[-1] for row in rows]), "frame", 1)
    return low, step_along(jnp.stack([row[0] for row in rows]), "frame", -1)


def row_sides(own):
    return step_along(own, "row", 1), step_along(own, "row", -1)


def tile_biases(active, frames, columns_here, cells):
    size = lax.axis_size("head")
    me = lax.axis_index("head")
    frame_at = lax.axis_index("frame") * frames
    row_at = lax.axis_index("row")
    all_frames, all_rows, count, slots = active.shape
    padded = jnp.pad(active.astype(jnp.float32), ((1, 1), (1, 1), (0, 0), (0, 0)))
    near = lax.dynamic_slice(padded, (frame_at, row_at, 0, 0), (frames + 2, 3, count, slots))
    near = near.reshape(frames + 2, 3, count, 9, 3)
    steps = jnp.arange(3, dtype=jnp.int32) - 1
    frame_ids = frame_at + jnp.arange(frames, dtype=jnp.int32)[:, None] + steps
    frame_in = (frame_ids >= 0) & (frame_ids < all_frames)
    row_in = (row_at + steps >= 0) & (row_at + steps < all_rows)
    inside = (frame_in[:, :, None] & row_in).reshape(frames, 9).astype(jnp.float32)
    ahead = near[1 : 1 + frames, 1] * inside[:, None, :, None]
    pick = np.zeros((frames + 2, 3, 9, frames, 9), np.float32)
    for at in range(frames):
        for offset in range(9):
            pick[at + offset // 3, offset % 3, 8 - offset, at, offset] = 1.0
    behind = jnp.einsum("xyioc,xyofq->fiqc", near, pick)
    part = jnp.arange(size, dtype=jnp.int32)
    tile = ((me + part) % size * columns_here) // TC
    repeat = np.kron(np.eye(9 * size), np.ones((1, cells)))
    spread_out = jnp.asarray(repeat, jnp.bfloat16)
    smalls = []
    for table, sign in ((ahead, 1), (behind, -1)):
        owner = tile[None] == jnp.arange(count, dtype=jnp.int32)[:, None]
        shift = (sign * (tile[None, :] - tile[:, None]))[None] == steps[:, None, None]
        chosen = (owner[:, None, :, None] & shift[None]).astype(jnp.float32)
        smalls.append(jnp.einsum("fioc,icpk->fpok", table, chosen))
    small = jnp.stack(smalls).reshape(2 * frames * size, -1).astype(jnp.bfloat16)
    allowed = jnp.dot(small, spread_out, preferred_element_type=jnp.float32)
    bias = jnp.where(allowed > 0.5, 0.0, MASKED).reshape(2, frames, size, -1)
    return bias[0], bias[1]


def on_device(queries, keys, values, out_grad, active):
    frames, rows, columns_here, heads, dim = queries.shape
    size = lax.axis_size("head")
    me = lax.axis_index("head")
    groups = heads // size
    cells = rows * columns_here
    tokens = cells * size
    scaling = dim ** (-0.5)
    assert rows == TR and TC % columns_here == 0

    def pair_of(first, second, shift):
        start = (me + shift) % size * groups
        picked = [
            lax.dynamic_slice_in_dim(jnp.transpose(t, (0, 3, 1, 2, 4)), start, groups, 1) for t in (first, second)
        ]
        return jnp.stack(picked, 1).reshape(frames, 2, groups, cells, dim)

    def move(blocks):
        return [
            (first, [piece if b == 0 else turn(piece, b) for b, piece in enumerate(grads)]) for first, grads in blocks
        ]

    def assemble(blocks):
        whole = jnp.zeros((2, frames, rows, heads, columns_here, dim), jnp.bfloat16)
        for first, pieces in blocks:
            for b, piece in enumerate(pieces):
                piece = piece.reshape((2, frames, -1, rows, columns_here, dim)).transpose(0, 1, 3, 2, 4, 5)
                start = (me + size - b) % size * groups + first
                whole = lax.dynamic_update_slice_in_dim(whole, piece, start, 3)
        whole = jnp.transpose(whole, (0, 1, 2, 4, 3, 5))
        return whole[0], whole[1]

    front_bias, back_bias = tile_biases(active, frames, columns_here, cells)
    key_here, front_bias = lax.optimization_barrier((pair_of(keys, values, 0), front_bias))
    key_near = row_sides(key_here)
    key_sent = [pair_of(keys, values, shift) for shift in range(1, size)]
    key_moved = [turn(key_sent[size - b - 1], size - b) for b in range(1, size)]
    query_held = [pair_of(queries, out_grad, shift) for shift in range(size)]
    query_held, key_sent = lax.optimization_barrier((query_held, key_sent))
    key_far = [row_sides(part) for part in key_moved]
    query_moved = [turn(query_held[size - b], size - b) for b in range(1, size)]
    query_all = jnp.stack(query_held[:1] + query_moved, 1)
    (far_up, far_down), *rest = key_far
    query_all, far_up = lax.optimization_barrier((query_all, far_up))
    key_far = [(far_up, far_down)] + rest
    query_before, query_after = row_sides(query_all)
    key_parts, sides = [key_here] + key_moved, [key_near] + key_far
    key_halo = key_parts + [before for before, _ in sides] + [after for _, after in sides]
    key_halo += frame_edges([row for part, (up, down) in zip(key_parts, sides) for row in (up, part, down)])
    query_halo = [query_all, query_before, query_after]
    query_rows = (query_before, query_all, query_after)
    query_halo += frame_edges([row[:, b] for b in range(size) for row in query_rows])

    def grads_shape(count):
        return [jax.ShapeDtypeStruct((2, frames, count, cells, dim), jnp.bfloat16)] * size

    attended_shape = jax.ShapeDtypeStruct((frames, groups, tokens, dim), jnp.bfloat16)
    stat_shape = jax.ShapeDtypeStruct((frames, groups, 2, tokens), jnp.float32)
    attended, stats = run(
        attend_kernel, scaling, size, [query_all] + key_halo, front_bias, [attended_shape, stat_shape], 0, groups, 2
    )
    halves = ((0, groups - groups // 2), (groups - groups // 2, groups // 2))
    stat_sides = row_sides(stats)
    front_blocks, shown = [], stats
    for first, count in halves:
        front_grads = run(
            query_kernel, scaling, size, [query_all] + key_halo + [attended, shown], front_bias,
            grads_shape(count), first, count, 3
        )
        front_blocks.append((first, front_grads))
        shown, stat_sides = lax.optimization_barrier((shown, stat_sides))
    stat_halo = [stats] + list(stat_sides) + list(frame_edges((stat_sides[0], stats, stat_sides[1])))
    front_blocks = move(front_blocks)
    back_blocks = []
    for first, count in halves:
        back_grads = run(
            back_kernel, scaling, size, key_parts + query_halo + stat_halo, back_bias, grads_shape(count),
            first, count, 4
        )
        back_bias, back_grads = lax.optimization_barrier((back_bias, back_grads))
        back_blocks.append((first, back_grads))
    back_blocks = move(back_blocks)
    first, pieces = back_blocks[0]
    front_blocks, pieces[-1] = lax.optimization_barrier((front_blocks, pieces[-1]))
    return assemble(front_blocks) + assemble(back_blocks)


def solution(mesh):
    spec = P("frame", "row", "head", None, None)
    return jax.shard_map(
        on_device, mesh=mesh, in_specs=(spec,) * 4 + (P(),), out_specs=(spec,) * 4, check_vma=False
    )
```
